512 devices in a mesh: frames: 64 (over y, z), tok: 2 (over core), dp: 4 (over x).
Axes of the slice: x: 4, y: 4, z: 16, core: 2. Of those that a mesh axis runs over, the one named last changes fastest.
Arguments:
- frame_input: bfloat16 [32768, 1024], P(('dp', 'frames'), 'tok'), parts along dimension 0, may hold values from -6 to 6
- state_write: bfloat16 [32768, 128], P(('dp', 'frames')), parts along dimension 0, may hold values from -0.3125 to 0.3125
- state_read: bfloat16 [32768, 128], P(('dp', 'frames')), parts along dimension 0, may hold values from -0.5 to 0.5
- log_decay: float32 [2, 16, 32768], P(None, 'tok', ('dp', 'frames')), parts along dimension 2, may hold values from -2 to 0, as said below
- skip_gain: float32 [16], P('tok'), may hold values from 0.5 to 1.5
- key_weight: bfloat16 [1024, 1280], P(None, 'tok'), may hold values from -0.1875 to 0.1875
- value_weight: bfloat16 [1024, 1280], P(None, 'tok'), may hold values from -0.1875 to 0.1875
- queries: bfloat16 [65536, 1280], P(('dp', 'frames'), 'tok'), parts along dimension 0, may hold values from -160 to 160
- span_start: int32 [1024], P(('dp', 'frames')), parts along dimension 0, may hold values from 0 to 8128, as said below
- span_len: int32 [1024], P(('dp', 'frames')), parts along dimension 0, may hold values from 64 to 128, as said below
Outputs:
- encoded: bfloat16 [32768, 1024], P(('dp', 'frames'), 'tok'), parts along dimension 0
- attended: bfloat16 [65536, 1280], P(('dp', 'frames'), 'tok'), parts along dimension 0
The draws below stay inside these ranges and needn't reach their ends.
There are 4 independent parts, one for each index of `dp`. The reference program is written for one: setup_inputs(seed, part) draws one part's arguments, and reference() takes and returns one part's arrays. A program takes and returns all parts, laid end to end along the dimension named above; an argument that names none is the same for every part. Nothing has to cross between parts.
Inputs may be any that keep to these rules, and one draw needn't show every extreme that they name: `log_decay`: Nonpositive. `span_start`: A multiple of 64. The span of group g lies within frames g // 4 * 128 - 64 to (g // 4 + 1) * 128 + 63 and within the recording. The first group's span starts at frame 0; the last group's span is the last 64 frames. `span_len`: A multiple of 64.
All inputs are finite; a program needn't handle non-finite values.
Results may differ from the reference program's by a relative error of at most 0.022.
Values may be sent and summed in bfloat16 or wider, within the bound.
A program may use at most 128 MiB of HBM per device.

```python
import math
import jax
import jax.numpy as jnp
from jax import lax

SOURCE_ATTN_UNIT = 16
HEAD_DIM = 64
STATE = 128
DHEADS = 20
DHD = 64
F_DEV = 128
TOK_DEV = 256
STRETCH = 64
ALIGN = 64
ENC = 1024
DEC = 1280
HALO = 64
SPAN_MAX = 128
AUDIO_STEP_TOTAL = 8192
TOKENS = 16384
STRETCHES = 256
N_FRAMES = 64


def span_pair(key):
    concurrent_lanes = jax.random.split(jax.random.fold_in(key, 5), 3)
    stretch_ids = jnp.arange(STRETCHES, dtype=jnp.int32)
    owner_device = stretch_ids // (TOK_DEV // STRETCH)
    most_units = SPAN_MAX // ALIGN
    span_units = jax.random.randint(concurrent_lanes[0], (STRETCHES,), 1, most_units + 1)
    chosen_stretch = jax.random.randint(concurrent_lanes[1], (), 0, STRETCHES - 1)
    span_units = jnp.where(stretch_ids == chosen_stretch, most_units, span_units)
    span_units = jnp.where(stretch_ids == STRETCHES - 1, 1, span_units)
    low_unit = jnp.maximum(owner_device * F_DEV - HALO, 0) // ALIGN
    high_unit = jnp.minimum(owner_device * F_DEV + F_DEV + HALO, AUDIO_STEP_TOTAL) // ALIGN - span_units
    begin_unit = jax.random.randint(concurrent_lanes[2], (STRETCHES,), low_unit, high_unit + 1)
    begin_unit = jnp.where(stretch_ids == 0, 0, begin_unit)
    begin_unit = jnp.where(stretch_ids == STRETCHES - 1, AUDIO_STEP_TOTAL // ALIGN - 1, begin_unit)
    return ((begin_unit * ALIGN).astype(jnp.int32), (span_units * ALIGN).astype(jnp.int32))


def draw_span_start(key, part):
    return span_pair(key)[0]


def draw_span_len(key, part):
    return span_pair(key)[1]


def draw_log_decay(key, part):
    key = jax.random.fold_in(key, 3)
    concurrent_lanes = jax.random.split(key, 7)
    fast_share = 5
    is_fast = jax.random.randint(concurrent_lanes[0], (2, SOURCE_ATTN_UNIT, 1), 0, 10) < fast_share
    fast_rate = jnp.exp(jax.random.uniform(concurrent_lanes[1], (2, SOURCE_ATTN_UNIT, 1), minval=math.log(1.0 / 16.0), maxval=math.log(1.0 / 8.0)))
    slow_rate = 0.5 / AUDIO_STEP_TOTAL * jax.random.uniform(concurrent_lanes[2], (2, SOURCE_ATTN_UNIT, 1), minval=0.5, maxval=1.0)
    reference_speed = jnp.where(is_fast, fast_rate, slow_rate)
    processor_scale_factor = jnp.exp(jax.random.uniform(concurrent_lanes[3], (2, SOURCE_ATTN_UNIT, AUDIO_STEP_TOTAL // F_DEV, 1), minval=-0.35, maxval=0.35))
    processor_scale_factor = jnp.broadcast_to(processor_scale_factor, (2, SOURCE_ATTN_UNIT, AUDIO_STEP_TOTAL // F_DEV, F_DEV)).reshape(2, SOURCE_ATTN_UNIT, AUDIO_STEP_TOTAL)
    outer_noise_wobble = jnp.exp(jax.random.uniform(concurrent_lanes[4], (2, SOURCE_ATTN_UNIT, AUDIO_STEP_TOTAL), minval=-0.7, maxval=0.7))
    spike_where = jax.random.randint(concurrent_lanes[5], (2, SOURCE_ATTN_UNIT, 2, 1), 0, AUDIO_STEP_TOTAL)
    spike_extra_cost = jnp.log(jax.random.uniform(concurrent_lanes[6], (2, SOURCE_ATTN_UNIT, 2, 1), minval=0.5, maxval=0.8))
    present_offset = jnp.arange(AUDIO_STEP_TOTAL, dtype=jnp.int32)
    spike_occurrences = jnp.sum(jnp.where(present_offset == spike_where, spike_extra_cost, 0.0), axis=2)
    return (spike_occurrences - reference_speed * processor_scale_factor * outer_noise_wobble).astype(jnp.float32)


def draw_queries(key, part):
    key = jax.random.fold_in(key, 7)
    concurrent_lanes = jax.random.split(key, 1)
    standard = jax.random.truncated_normal(concurrent_lanes[0], -4.0, 4.0, (TOKENS, DEC), jnp.float32)
    return standard.astype(jnp.bfloat16)


def block_levels(rng, dims, pieces, low, largest):
    def one(axis_at, shards_of):
        heights = jax.random.uniform(jax.random.fold_in(jax.random.fold_in(rng, 6), axis_at), (shards_of,), jnp.float32, low / len(pieces), largest / len(pieces))
        return jnp.repeat(jnp.exp(heights), dims[axis_at] // shards_of).reshape((-1,) + (1,) * (len(dims) - axis_at - 1))

    loudness = one(*pieces[0])
    for cut in pieces[1:]:
        loudness = loudness * one(*cut)
    return loudness


def gaussian(key, dims, scale, most, pieces=(), kind=jnp.bfloat16):
    array = jax.random.normal(key, dims, jnp.float32) * scale
    if len(pieces) > 0:
        array = block_levels(key, dims, pieces, -0.22, 0.18) * array
    return jnp.clip(array, min=-most, max=most).astype(kind)


def setup_inputs(seed: int = 0, part: int = 0) -> dict:
    splits = jax.random.split(jax.random.key(seed), 11)
    part_keys = jax.random.split(jax.random.fold_in(splits[10], part), 11)
    frame_input = gaussian(part_keys[0], (AUDIO_STEP_TOTAL, ENC), 1.0, 6.0, ((0, 64), (1, 2)))
    state_write = gaussian(part_keys[1], (AUDIO_STEP_TOTAL, STATE), (2.0 * AUDIO_STEP_TOTAL ** -0.5), 0.3125, ((0, 64),))
    state_read = gaussian(part_keys[2], (AUDIO_STEP_TOTAL, STATE), STATE ** -0.5, 0.5, ((0, 64),))
    log_decay = draw_log_decay(jax.random.fold_in(jax.random.fold_in(splits[10], part), 71), part)
    skip_gain = jnp.clip(0.5 + 1.0 * jax.random.uniform(splits[4], (SOURCE_ATTN_UNIT,), jnp.float32) ** block_levels(splits[4], (SOURCE_ATTN_UNIT,), ((0, 2),), -0.2, 0.2), 0.5, 1.5)
    key_weight = gaussian(splits[5], (ENC, DEC), ENC ** -0.5, 0.1875, ((1, 2),))
    value_weight = gaussian(splits[6], (ENC, DEC), ENC ** -0.5, 0.1875, ((1, 2),))
    queries = draw_queries(jax.random.fold_in(jax.random.fold_in(splits[10], part), 71), part)
    span_start = draw_span_start(jax.random.fold_in(jax.random.fold_in(splits[10], part), 71), part)
    span_len = draw_span_len(jax.random.fold_in(jax.random.fold_in(splits[10], part), 71), part)
    return dict(frame_input=frame_input, state_write=state_write, state_read=state_read, log_decay=log_decay, skip_gain=skip_gain, key_weight=key_weight, value_weight=value_weight, queries=queries, span_start=span_start, span_len=span_len)


highest = lax.Precision.HIGHEST


def block_terms(x_block, b_block, c_block, rate_block):
    block_size = rate_block.shape[1]
    cumulative = jnp.cumsum(rate_block, axis=1)
    gram_matrix = jnp.dot(c_block, b_block.T, preferred_element_type=jnp.float32)
    spread = cumulative[:, :, None] - cumulative[:, None, :]
    row_ids = jnp.arange(block_size)
    causal = (row_ids[:, None] >= row_ids[None, :])[None]
    weights = jnp.where(causal, jnp.exp(jnp.where(causal, spread, 0.0)), 0.0) * gram_matrix[None]
    weights = lax.optimization_barrier(weights.astype(jnp.bfloat16)).astype(jnp.float32)
    intra_part = jnp.einsum("hts,shp->thp", weights, x_block.astype(jnp.float32))
    to_end = jnp.exp(cumulative[:, -1:] - cumulative)
    scaled = x_block.astype(jnp.float32) * to_end.T[:, :, None]
    scaled = lax.optimization_barrier(scaled.astype(jnp.bfloat16)).astype(jnp.float32)
    local_state = jnp.einsum("fhp,fn->hpn", scaled, b_block.astype(jnp.float32), precision=highest)
    return intra_part, local_state, jnp.exp(cumulative[:, -1]), cumulative


def carried_output(c_block, state, cumulative):
    rounded = lax.optimization_barrier(state.astype(jnp.bfloat16)).astype(jnp.float32)
    reading = jnp.einsum("fn,hpn->fhp", c_block.astype(jnp.float32), rounded, precision=highest)
    return jnp.exp(cumulative).T[:, :, None] * reading


def one_direction(x_heads, state_write, state_read, log_rates):
    block_count = AUDIO_STEP_TOTAL // F_DEV
    x_blocks = x_heads.reshape(block_count, F_DEV, SOURCE_ATTN_UNIT, HEAD_DIM)
    b_blocks = state_write.reshape(block_count, F_DEV, STATE)
    c_blocks = state_read.reshape(block_count, F_DEV, STATE)
    rate_blocks = log_rates.reshape(SOURCE_ATTN_UNIT, block_count, F_DEV).transpose(1, 0, 2)

    def advance(state, item):
        x_block, b_block, c_block, rate_block = item
        intra_part, local_state, decay_total, cumulative = block_terms(x_block, b_block, c_block, rate_block)
        output = intra_part + carried_output(c_block, state, cumulative)
        return decay_total[:, None, None] * state + local_state, output

    initial = jnp.zeros((SOURCE_ATTN_UNIT, HEAD_DIM, STATE), jnp.float32)
    _, outputs = lax.scan(advance, initial, (x_blocks, b_blocks, c_blocks, rate_blocks))
    return outputs.reshape(AUDIO_STEP_TOTAL, SOURCE_ATTN_UNIT, HEAD_DIM)


def reference(frame_input, state_write, state_read, log_decay, skip_gain, key_weight, value_weight, queries, span_start, span_len):
    x_heads = frame_input.reshape(AUDIO_STEP_TOTAL, SOURCE_ATTN_UNIT, HEAD_DIM)
    forward = one_direction(x_heads, state_write, state_read, log_decay[0])
    backward = one_direction(x_heads[::-1], state_write[::-1], state_read[::-1], log_decay[1][:, ::-1])[::-1]
    encoded = forward + backward + skip_gain[None, :, None] * x_heads.astype(jnp.float32)
    encoded = encoded.reshape(AUDIO_STEP_TOTAL, ENC).astype(jnp.bfloat16)
    keys = jnp.dot(encoded, key_weight, preferred_element_type=jnp.float32).astype(jnp.bfloat16)
    values = jnp.dot(encoded, value_weight, preferred_element_type=jnp.float32).astype(jnp.bfloat16)
    padded_keys = jnp.pad(keys, ((HALO, HALO), (0, 0)))
    padded_values = jnp.pad(values, ((HALO, HALO), (0, 0)))
    per_device = TOK_DEV // STRETCH

    def attend_block(block_index):
        offset = (block_index * F_DEV).astype(jnp.int32)
        window_keys = lax.dynamic_slice(padded_keys, (offset, jnp.int32(0)), (2 * F_DEV, DEC))
        window_values = lax.dynamic_slice(padded_values, (offset, jnp.int32(0)), (2 * F_DEV, DEC))
        token_offset = (block_index * TOK_DEV).astype(jnp.int32)
        block_queries = lax.dynamic_slice(queries, (token_offset, jnp.int32(0)), (TOK_DEV, DEC))
        group_offset = (block_index * per_device).astype(jnp.int32)
        starts = lax.dynamic_slice(span_start, (group_offset,), (per_device,))
        lengths = lax.dynamic_slice(span_len, (group_offset,), (per_device,))
        token_starts = jnp.repeat(starts, STRETCH)
        token_ends = token_starts + jnp.repeat(lengths, STRETCH)
        positions = (block_index * F_DEV - HALO).astype(jnp.int32) + jnp.arange(2 * F_DEV, dtype=jnp.int32)
        allowed = (positions[None, :] >= token_starts[:, None]) & (positions[None, :] < token_ends[:, None])
        query_heads = block_queries.astype(jnp.float32).reshape(TOK_DEV, DHEADS, DHD)
        key_heads = window_keys.astype(jnp.float32).reshape(2 * F_DEV, DHEADS, DHD)
        value_heads = window_values.astype(jnp.float32).reshape(2 * F_DEV, DHEADS, DHD)
        scores = jnp.einsum("thd,khd->htk", query_heads, key_heads) * (DHD ** -0.5)
        scores = jnp.where(allowed[None], scores, -jnp.inf)
        row_max = jnp.max(scores, axis=-1, keepdims=True)
        exponent = jnp.exp(scores - row_max)
        probs = exponent / jnp.sum(exponent, axis=-1, keepdims=True)
        probs = lax.optimization_barrier(probs.astype(jnp.bfloat16)).astype(jnp.float32)
        mixed = jnp.einsum("htk,khd->thd", probs, value_heads)
        return mixed.astype(jnp.bfloat16).reshape(TOK_DEV, DEC)

    attended = lax.map(attend_block, jnp.arange(N_FRAMES, dtype=jnp.int32)).reshape(TOKENS, DEC)
    return encoded, attended
```

```python
import functools

import jax
import jax.numpy as jnp
from jax import lax
from jax.experimental import pallas as pl
from jax.experimental.pallas import tpu as pltpu
from jax.sharding import PartitionSpec as P

DHD = 64
F = 128
N = 128
HD = 64
NI = 4
MESH = pl.DeviceIdType.MESH
HIGH = lax.Precision.HIGHEST
NT = (((1,), (1,)), ((), ()))


def dot(a, b):
    return jnp.dot(a, b, preferred_element_type=jnp.float32)


def rows_of(tile, first, heads, depth):
    return jnp.concatenate(
        [jnp.broadcast_to(tile[first + k : first + k + 1], (depth, N)) for k in range(heads)], axis=0
    )


def mixer(
    dims,
    x_ref,
    b_ref,
    c_ref,
    ld_ref,
    gain_ref,
    out_ref,
    lsend,
    lrecv,
    tsend,
    trecv,
    gsend,
    grecv,
    gtsend,
    gtrecv,
    ysend,
    yrecv,
    ytsend,
    ytrecv,
    csend,
    crecv,
    rsend,
    rrecv,
    pre,
    ef,
    eb,
    pf,
    qb,
    ssem,
    rsem,
):
    ny, ng, tok_count = dims
    width = x_ref.shape[1]
    heads = width // HD
    piece = width // NI
    hp = heads // NI
    sub = piece // ng
    frames = ny * ng * NI
    me = lax.axis_index("frames")
    tok = lax.axis_index("tok")
    y = me // (ng * NI)
    g = lax.rem(me // NI, ng)
    i = lax.rem(me, NI)

    def at_i(p):
        return me - i + p

    def at_g(p):
        return me + (p - g) * NI

    def at_y(p):
        return me + (p - y) * (ng * NI)

    prev = lax.rem(me + frames - 1, frames)
    succ = lax.rem(me + 1, frames)

    barrier = pltpu.get_barrier_semaphore()
    greeted = 0
    for own, count, place in ((i, NI, at_i), (g, ng, at_g), (y, ny, at_y)):
        for k in range(1, count):
            pl.semaphore_signal(
                barrier,
                inc=1,
                device_id={"frames": place(lax.rem(own + k, count))},
                device_id_type=MESH,
            )
            greeted += 1
    for side in (prev, succ):
        for k in range(tok_count):
            pl.semaphore_signal(
                barrier,
                inc=1,
                device_id={"frames": side, "tok": lax.rem(tok + k, tok_count)},
                device_id_type=MESH,
            )
            greeted += 1
    if tok_count > 1:
        pl.semaphore_signal(barrier, inc=1, device_id={"tok": 1 - tok}, device_id_type=MESH)
        greeted += 1

    sent = []

    def remote(src, dst, index, device):
        return pltpu.make_async_remote_copy(
            src_ref=src,
            dst_ref=dst,
            send_sem=ssem.at[index],
            recv_sem=rsem.at[index],
            device_id=device,
            device_id_type=MESH,
        )

    def scatter(own, count, place, src, dst, first):
        for k in range(1, count):
            p = lax.rem(own + k, count)
            copy = remote(src.at[p], dst.at[own], first + k - 1, {"frames": place(p)})
            copy.start()
            sent.append(copy)

    def share(own, count, place, src, dst, first):
        for k in range(1, count):
            p = lax.rem(own + k, count)
            copy = remote(src, dst.at[own], first + k - 1, {"frames": place(p)})
            copy.start()
            sent.append(copy)

    def arrive(own, count, place, src, dst, first):
        for k in range(1, count):
            q = lax.rem(own + count - k, count)
            remote(src, dst.at[q], first + k - 1, {"frames": place(q)}).wait_recv()

    r_id = lax.broadcasted_iota(jnp.int32, (F, F), 0)
    s_id = lax.broadcasted_iota(jnp.int32, (F, F), 1)
    after = (r_id > s_id).astype(jnp.float32)
    before = (r_id < s_id).astype(jnp.float32)
    upto = (r_id <= s_id).astype(jnp.float32)
    ld_f = ld_ref[0]
    ld_b = ld_ref[1]
    tail_f = jnp.dot(ld_f, after, precision=HIGH, preferred_element_type=jnp.float32)
    row_b = jnp.dot(ld_b, before, precision=HIGH, preferred_element_type=jnp.float32)
    tot_f = jnp.broadcast_to(jnp.sum(ld_f, axis=1, keepdims=True), (heads, N))
    tot_b = jnp.broadcast_to(jnp.sum(ld_b, axis=1, keepdims=True), (heads, N))
    tsend[...] = jnp.zeros_like(tsend)
    for p in range(NI):
        tsend[p, 0:hp, :] = tot_f[p * hp : (p + 1) * hp]
        tsend[p, hp : 2 * hp, :] = tot_b[p * hp : (p + 1) * hp]
    wf = jnp.exp(tail_f)
    wb = jnp.exp(row_b)
    b_all = b_ref[...]
    for p in range(NI):
        xt = x_ref[:, p * piece : (p + 1) * piece].astype(jnp.float32).T
        for k, w in enumerate((wf, wb)):
            scaled = (xt * rows_of(w, p * hp, hp, HD)).astype(jnp.bfloat16)
            lsend[p, k * piece : (k + 1) * piece, :] = dot(scaled, b_all).astype(jnp.bfloat16)

    pl.semaphore_wait(barrier, greeted)
    base = 0
    i_data, i_tot = base, base + NI - 1
    base += 2 * (NI - 1)
    g_data, g_tot = base, base + ng - 1
    base += 2 * (ng - 1)
    y_data, y_tot = base, base + ny - 1
    base += 2 * (ny - 1)
    c_data = base
    base += ng - 1
    r_data = base
    base += NI - 1
    e_data = base

    scatter(i, NI, at_i, tsend, trecv, i_tot)
    scatter(i, NI, at_i, lsend, lrecv, i_data)
    lrecv[pl.ds(i, 1)] = lsend[pl.ds(i, 1)]
    trecv[pl.ds(i, 1)] = tsend[pl.ds(i, 1)]

    gram = lax.dot_general(c_ref[...], b_all, NT, preferred_element_type=jnp.float32)
    gram = jnp.where(r_id == s_id, 2.0 * gram, gram)
    row_f = jnp.dot(ld_f, upto, precision=HIGH, preferred_element_type=jnp.float32)
    col_f = lax.dot_general(
        (s_id <= r_id).astype(jnp.float32), ld_f, NT, precision=HIGH, preferred_element_type=jnp.float32
    )
    col_b = lax.dot_general(
        (s_id < r_id).astype(jnp.float32), ld_b, NT, precision=HIGH, preferred_element_type=jnp.float32
    )
    lower = s_id <= r_id
    left = s_id < HD
    for p in range(heads // 2):
        cols = slice(p * 2 * HD, (p + 1) * 2 * HD)
        x_pair = x_ref[:, cols].astype(jnp.float32)
        weights = []
        spread_f = []
        spread_b = []
        for h in (2 * p, 2 * p + 1):
            at_f = jnp.broadcast_to(col_f[:, h : h + 1], (F, F))
            at_b = jnp.broadcast_to(col_b[:, h : h + 1], (F, F))
            exponent = jnp.where(lower, at_f - row_f[h : h + 1], row_b[h : h + 1] - at_b)
            weights.append((jnp.exp(exponent) * gram).astype(jnp.bfloat16))
            spread_f.append(at_f)
            spread_b.append(tot_b[h : h + 1] - at_b)
        apart = jnp.concatenate(
            [jnp.where(left, x_pair, 0.0), jnp.where(left, 0.0, x_pair)], axis=0
        ).astype(jnp.bfloat16)
        intra = dot(jnp.concatenate(weights, axis=1), apart)
        gain = jnp.where(left[0:1], gain_ref[2 * p], gain_ref[2 * p + 1])
        pre[:, cols] = intra + gain * x_pair
        ef[:, cols] = jnp.exp(jnp.where(left, spread_f[0], spread_f[1]))
        eb[:, cols] = jnp.exp(jnp.where(left, spread_b[0], spread_b[1]))

    arrive(i, NI, at_i, tsend.at[0], trecv, i_tot)
    arrive(i, NI, at_i, lsend.at[0], lrecv, i_data)
    tots = [trecv[j] for j in range(NI)]
    state = jnp.zeros((piece, N), jnp.float32)
    for j in range(NI):
        pf[j] = state
        state = jnp.exp(rows_of(tots[j], 0, hp, HD)) * state + lrecv[j, 0:piece, :].astype(jnp.float32)
    for k in range(ng):
        gsend[k, 0:sub, :] = state[k * sub : (k + 1) * sub].astype(jnp.bfloat16)
    state = jnp.zeros((piece, N), jnp.float32)
    for j in reversed(range(NI)):
        qb[j] = state
        state = jnp.exp(rows_of(tots[j], hp, hp, HD)) * state + lrecv[j, piece : 2 * piece, :].astype(
            jnp.float32
        )
    for k in range(ng):
        gsend[k, sub : 2 * sub, :] = state[k * sub : (k + 1) * sub].astype(jnp.bfloat16)
    gtsend[...] = functools.reduce(jnp.add, tots)
    share(g, ng, at_g, gtsend, gtrecv, g_tot)
    scatter(g, ng, at_g, gsend, grecv, g_data)
    grecv[pl.ds(g, 1)] = gsend[pl.ds(g, 1)]
    gtrecv[g] = gtsend[...]

    arrive(g, ng, at_g, gtsend, gtrecv, g_tot)
    arrive(g, ng, at_g, gsend.at[0], grecv, g_data)
    head = (g * sub) // HD
    gt_f = []
    gt_b = []
    for k in range(ng):
        tile = gtrecv[k]
        one_f, one_b = tile[0:1], tile[hp : hp + 1]
        for h in range(1, hp):
            one_f = jnp.where(head == h, tile[h : h + 1], one_f)
            one_b = jnp.where(head == h, tile[hp + h : hp + h + 1], one_b)
        gt_f.append(one_f)
        gt_b.append(one_b)
    in_f, in_b = [None] * ng, [None] * ng
    before_f, before_b = [None] * ng, [None] * ng
    state, total = jnp.zeros((sub, N), jnp.float32), jnp.zeros((1, N), jnp.float32)
    for k in range(ng):
        in_f[k], before_f[k] = state, total
        state = jnp.exp(gt_f[k]) * state + grecv[k, 0:sub, :].astype(jnp.float32)
        total = total + gt_f[k]
    row_state_f, row_tot_f = state, total
    state, total = jnp.zeros((sub, N), jnp.float32), jnp.zeros((1, N), jnp.float32)
    for k in reversed(range(ng)):
        in_b[k], before_b[k] = state, total
        state = jnp.exp(gt_b[k]) * state + grecv[k, sub : 2 * sub, :].astype(jnp.float32)
        total = total + gt_b[k]
    row_state_b, row_tot_b = state, total

    if ny > 1:
        ysend[0:sub, :] = row_state_f.astype(jnp.bfloat16)
        ysend[sub : 2 * sub, :] = row_state_b.astype(jnp.bfloat16)
        ytsend[...] = jnp.concatenate(
            [row_tot_f, row_tot_b, jnp.zeros((6, N), jnp.float32)], axis=0
        )
        share(y, ny, at_y, ytsend, ytrecv, y_tot)
        share(y, ny, at_y, ysend, yrecv, y_data)
        yrecv[y] = ysend[...]
        ytrecv[y] = ytsend[...]
        arrive(y, ny, at_y, ytsend, ytrecv, y_tot)
        arrive(y, ny, at_y, ysend, yrecv, y_data)
    enter_f = jnp.zeros((sub, N), jnp.float32)
    enter_b = jnp.zeros((sub, N), jnp.float32)
    if ny > 1:
        state = jnp.zeros((sub, N), jnp.float32)
        for k in range(ny):
            enter_f = jnp.where(y == k, state, enter_f)
            state = jnp.exp(ytrecv[k, 0:1, :]) * state + yrecv[k, 0:sub, :].astype(jnp.float32)
        state = jnp.zeros((sub, N), jnp.float32)
        for k in reversed(range(ny)):
            enter_b = jnp.where(y == k, state, enter_b)
            state = jnp.exp(ytrecv[k, 1:2, :]) * state + yrecv[k, sub : 2 * sub, :].astype(jnp.float32)
    for k in range(ng):
        csend[k, 0:sub, :] = (in_f[k] + jnp.exp(before_f[k]) * enter_f).astype(jnp.bfloat16)
        csend[k, sub : 2 * sub, :] = (in_b[k] + jnp.exp(before_b[k]) * enter_b).astype(jnp.bfloat16)
    scatter(g, ng, at_g, csend, crecv, c_data)
    crecv[pl.ds(g, 1)] = csend[pl.ds(g, 1)]
    arrive(g, ng, at_g, csend.at[0], crecv, c_data)

    enter_f = jnp.concatenate([crecv[k, 0:sub, :] for k in range(ng)], axis=0).astype(jnp.float32)
    enter_b = jnp.concatenate([crecv[k, sub : 2 * sub, :] for k in range(ng)], axis=0).astype(jnp.float32)
    total = jnp.zeros((8, N), jnp.float32)
    for j in range(NI):
        rsend[j, 0:piece, :] = (pf[j] + jnp.exp(rows_of(total, 0, hp, HD)) * enter_f).astype(jnp.bfloat16)
        total = total + tots[j]
    total = jnp.zeros((8, N), jnp.float32)
    for j in reversed(range(NI)):
        rsend[j, piece : 2 * piece, :] = (qb[j] + jnp.exp(rows_of(total, hp, hp, HD)) * enter_b).astype(
            jnp.bfloat16
        )
        total = total + tots[j]
    scatter(i, NI, at_i, rsend, rrecv, r_data)
    rrecv[pl.ds(i, 1)] = rsend[pl.ds(i, 1)]
    arrive(i, NI, at_i, rsend.at[0], rrecv, r_data)

    c_all = c_ref[...]
    for p in range(NI):
        cols = slice(p * piece, (p + 1) * piece)
        read_f = lax.dot_general(c_all, rrecv[p, 0:piece, :], NT, preferred_element_type=jnp.float32)
        read_b = lax.dot_general(
            c_all, rrecv[p, piece : 2 * piece, :], NT, preferred_element_type=jnp.float32
        )
        done = pre[:, cols] + ef[:, cols] * read_f + eb[:, cols] * read_b
        out_ref[tok, F // 2 : F // 2 + F, cols] = done.astype(jnp.bfloat16)
    rim = F // 2
    mine = out_ref.at[tok, rim : rim + F]
    low = out_ref.at[tok, rim : 2 * rim]
    high = out_ref.at[tok, 2 * rim : 3 * rim]
    final = []
    for k in range(tok_count):
        there = lax.rem(tok + k, tok_count)
        index = e_data + 3 * k
        final.append(
            remote(low, out_ref.at[tok, 3 * rim : 4 * rim], index, {"frames": prev, "tok": there})
        )
        final.append(
            remote(high, out_ref.at[tok, 0:rim], index + 1, {"frames": succ, "tok": there})
        )
        if k > 0:
            final.append(remote(mine, mine, index + 2, {"tok": there}))
    for copy in final:
        copy.start()
    sent.extend(final)
    for k in range(tok_count):
        source = lax.rem(tok + tok_count - k, tok_count)
        index = e_data + 3 * k
        remote(low, out_ref.at[source, 3 * rim : 4 * rim], index, {"frames": prev}).wait_recv()
        remote(high, out_ref.at[source, 0:rim], index + 1, {"frames": succ}).wait_recv()
        if k > 0:
            remote(mine, out_ref.at[source, rim : rim + F], index + 2, {"tok": source}).wait_recv()
    for copy in sent:
        copy.wait_send()


def reader(start_ref, len_ref, wide_ref, wk_ref, wv_ref, q_ref, enc_ref, out_ref, bias):
    tok = lax.axis_index("tok")
    parts, window, half = wide_ref.shape
    tokens, width = q_ref.shape
    rim = window // 4
    groups = start_ref.shape[0]
    per_group = tokens // groups
    enc_ref[...] = wide_ref[tok, rim : 3 * rim, :]
    first = lax.axis_index("frames") * (window // 2) - rim
    place = lax.broadcasted_iota(jnp.int32, (per_group, window), 1) + first
    for k in range(groups):
        start = start_ref[k]
        allowed = (place >= start) & (place < start + len_ref[k])
        bias[k * per_group : (k + 1) * per_group, :] = jnp.where(allowed, 0.0, -jnp.inf)

    def project(weight_ref):
        total = dot(wide_ref[0], weight_ref[0:half, :])
        for k in range(1, parts):
            total = total + dot(wide_ref[k], weight_ref[k * half : (k + 1) * half, :])
        return total

    keys = project(wk_ref)
    values = project(wv_ref).astype(jnp.bfloat16)
    left = lax.broadcasted_iota(jnp.int32, (1, 2 * DHD), 1) < DHD
    for p in range(width // (2 * DHD)):
        cols = slice(p * 2 * DHD, (p + 1) * 2 * DHD)
        q_pair = q_ref[:, cols]
        k_pair = keys[:, cols]
        v_pair = values[:, cols]
        both = []
        for only in (jnp.where(left, k_pair, 0.0), jnp.where(left, 0.0, k_pair)):
            scores = lax.dot_general(
                q_pair, only.astype(jnp.bfloat16), NT, preferred_element_type=jnp.float32
            )
            scores = scores + bias[...]
            top = jnp.max(scores, axis=1, keepdims=True)
            raised = jnp.exp((scores - top) * DHD ** (-0.5))
            share = 1.0 / jnp.sum(raised, axis=1, keepdims=True)
            both.append(dot((raised * share).astype(jnp.bfloat16), v_pair))
        out_ref[:, cols] = jnp.where(left, both[0], both[1]).astype(jnp.bfloat16)


def solution(mesh):
    frames = mesh.shape["frames"]
    tok_count = mesh.shape["tok"]
    ng = min(4, frames // NI)
    ny = frames // (NI * ng)
    vmem = pl.BlockSpec(memory_space=pltpu.VMEM)
    smem = pl.BlockSpec(memory_space=pltpu.SMEM)

    def local(x, b, c, log_decay, gain, key_weight, value_weight, queries, span_start, span_len):
        count, width = x.shape
        piece = width // NI
        sub = piece // ng
        bf, f32 = jnp.bfloat16, jnp.float32
        copies = 3 * (NI - 1) + 3 * (ng - 1) + 2 * (ny - 1) + 3 * tok_count
        wide = pl.pallas_call(
            functools.partial(mixer, (ny, ng, tok_count)),
            out_shape=jax.ShapeDtypeStruct((tok_count, 2 * count, width), bf),
            in_specs=[vmem, vmem, vmem, vmem, smem],
            out_specs=vmem,
            scratch_shapes=[
                pltpu.VMEM((NI, 2 * piece, N), bf),
                pltpu.VMEM((NI, 2 * piece, N), bf),
                pltpu.VMEM((NI, 8, N), f32),
                pltpu.VMEM((NI, 8, N), f32),
                pltpu.VMEM((ng, 2 * sub, N), bf),
                pltpu.VMEM((ng, 2 * sub, N), bf),
                pltpu.VMEM((8, N), f32),
                pltpu.VMEM((ng, 8, N), f32),
                pltpu.VMEM((2 * sub, N), bf),
                pltpu.VMEM((ny, 2 * sub, N), bf),
                pltpu.VMEM((8, N), f32),
                pltpu.VMEM((ny, 8, N), f32),
                pltpu.VMEM((ng, 2 * sub, N), bf),
                pltpu.VMEM((ng, 2 * sub, N), bf),
                pltpu.VMEM((NI, 2 * piece, N), bf),
                pltpu.VMEM((NI, 2 * piece, N), bf),
                pltpu.VMEM((count, width), f32),
                pltpu.VMEM((count, width), f32),
                pltpu.VMEM((count, width), f32),
                pltpu.VMEM((NI, piece, N), f32),
                pltpu.VMEM((NI, piece, N), f32),
                pltpu.SemaphoreType.DMA((copies,)),
                pltpu.SemaphoreType.DMA((copies,)),
            ],
            compiler_params=pltpu.CompilerParams(
                collective_id=0, has_side_effects=True, vmem_limit_bytes=16 * 2**20
            ),
        )(x, b, c, log_decay, gain)
        return pl.pallas_call(
            reader,
            out_shape=(
                jax.ShapeDtypeStruct((count, width), bf),
                jax.ShapeDtypeStruct(queries.shape, bf),
            ),
            in_specs=[smem, smem, vmem, vmem, vmem, vmem],
            out_specs=(vmem, vmem),
            scratch_shapes=[pltpu.VMEM((queries.shape[0], 2 * count), f32)],
            compiler_params=pltpu.CompilerParams(vmem_limit_bytes=24 * 2**20),
        )(span_start, span_len, wide, key_weight, value_weight, queries)

    placed = (
        P(("dp", "frames"), "tok"),
        P(("dp", "frames"), None),
        P(("dp", "frames"), None),
        P(None, "tok", ("dp", "frames")),
        P("tok"),
        P(None, "tok"),
        P(None, "tok"),
        P(("dp", "frames"), "tok"),
        P(("dp", "frames")),
        P(("dp", "frames")),
    )
    return jax.shard_map(
        local,
        mesh=mesh,
        in_specs=placed,
        out_specs=(P(("dp", "frames"), "tok"), P(("dp", "frames"), "tok")),
        check_vma=False,
    )
```

```python
import functools

import jax
import jax.numpy as jnp
from jax import lax
from jax.experimental import pallas as pl
from jax.experimental.pallas import tpu as pltpu
from jax.sharding import PartitionSpec as P

DHD = 64
F = 128
RIM = 64
N = 128
HD = 64
NI = 4
HP = 2
PIECE = HP * HD
MESH = pl.DeviceIdType.MESH
HIGH = lax.Precision.HIGHEST
NT = (((1,), (1,)), ((), ()))
BF = jnp.bfloat16
F32 = jnp.float32


def dot(a, b):
    return jnp.dot(a, b, preferred_element_type=F32)


def dot_nt(a, b, precision=None):
    return lax.dot_general(a, b, NT, precision=precision, preferred_element_type=F32)


def tall(tile, first):
    return jnp.concatenate(
        [jnp.broadcast_to(tile[first + k : first + k + 1], (HD, N)) for k in range(HP)], axis=0
    )


def mixer(
    dims,
    x_hbm,
    b_hbm,
    c_hbm,
    ld_hbm,
    gain_hbm,
    wk_hbm,
    wv_hbm,
    q_hbm,
    start_hbm,
    len_hbm,
    wide,
    keys,
    values,
    q_out,
    bias,
    xv,
    bv,
    cv,
    ldv,
    gain,
    starts,
    lens,
    wk,
    wv,
    lsend,
    lrecv,
    crx,
    ldrx,
    gsend,
    grecv,
    gtsend,
    gtrecv,
    ysend,
    yrecv,
    ytsend,
    ytrecv,
    csend,
    crecv,
    pre,
    prebf,
    rim_l,
    rim_r,
    within,
    grown,
    local_part,
    rwin,
    rin,
    rx,
    kacc,
    vacc,
    hsem,
    ssem,
    rsem,
):
    ny, ng, tok_count = dims
    heads = ldv.shape[1]
    half = xv.shape[1]
    sub = PIECE // ng
    frames = ny * ng * NI
    row = ng * NI
    me = lax.axis_index("frames")
    tok = lax.axis_index("tok")
    y = me // row
    g = lax.rem(me // NI, ng)
    i = lax.rem(me, NI)
    base = me - i

    def at_i(p):
        return base + p

    def at_g(p):
        return me + (p - g) * NI

    def at_y(p):
        return me + (p - y) * row

    prev = lax.rem(me + frames - 1, frames)
    succ = lax.rem(me + 1, frames)
    base_prev = lax.rem(base + frames - NI, frames)
    base_succ = lax.rem(base + NI, frames)

    fetched = {}

    def fetch(name, src, dst):
        copy = pltpu.make_async_copy(src, dst, hsem.at[len(fetched)])
        copy.start()
        fetched[name] = copy

    fetch("ld", ld_hbm, ldv)
    fetch("x", x_hbm, xv)
    fetch("b", b_hbm, bv)
    fetch("c", c_hbm, cv)
    fetch("gain", gain_hbm, gain)
    fetch("start", start_hbm, starts)
    fetch("len", len_hbm, lens)
    fetch("wk", wk_hbm, wk)
    fetch("wv", wv_hbm, wv)
    fetch("q", q_hbm, q_out)

    barrier = pltpu.get_barrier_semaphore()

    def greet(**device):
        pl.semaphore_signal(barrier, inc=1, device_id=device, device_id_type=MESH)

    greeted = 0
    for own, count, place in ((i, NI, at_i), (g, ng, at_g), (y, ny, at_y)):
        for k in range(1, count):
            greet(frames=place(lax.rem(own + k, count)))
            greeted += 1
    greet(frames=prev)
    greet(frames=succ)
    greeted += 2
    if tok_count > 1:
        greet(tok=1 - tok)
        greeted += 1

    @pl.when(i == 0)
    def _():
        for k in range(NI):
            greet(frames=base_prev + k)

    @pl.when(i == NI - 1)
    def _():
        for k in range(NI):
            greet(frames=base_succ + k)

    greeted += 2

    sent = []
    taken = [0]

    def take(n):
        first = taken[0]
        taken[0] += n
        return first

    def remote(src, dst, index, device, landing=None):
        return pltpu.make_async_remote_copy(
            src_ref=src,
            dst_ref=dst,
            send_sem=ssem.at[index],
            recv_sem=rsem.at[index if landing is None else landing],
            device_id=device,
            device_id_type=MESH,
        )

    def start(copy):
        copy.start()
        sent.append(copy)

    def scatter(own, count, place, src, dst, first):
        for k in range(1, count):
            p = lax.rem(own + k, count)
            start(remote(src.at[p], dst.at[own], first + k - 1, {"frames": place(p)}))

    def share(own, count, place, src, dst, first):
        for k in range(1, count):
            p = lax.rem(own + k, count)
            start(remote(src, dst.at[own], first + k - 1, {"frames": place(p)}))

    def arrive(own, count, place, src, dst, first):
        for k in range(1, count):
            q = lax.rem(own + count - k, count)
            remote(src, dst.at[q], first + k - 1, {"frames": place(q)}).wait_recv()

    sem_ld, sem_c = take(NI - 1), take(NI - 1)
    sem_l = (take(NI - 1), take(NI - 1))
    sem_gt = take(ng - 1)
    sem_g = (take(ng - 1), take(ng - 1))
    sem_yt = take(ny - 1)
    sem_y = (take(ny - 1), take(ny - 1))
    sem_b = (take(ng - 1), take(ng - 1))
    sem_rim = take(2)
    sem_r = take(NI - 1)
    sem_rx = take(NI)
    sem_w = take(NI)

    pl.semaphore_wait(barrier, greeted)
    share(i, NI, at_i, ld_hbm, ldrx, sem_ld)
    share(i, NI, at_i, c_hbm, crx, sem_c)

    r_id = lax.broadcasted_iota(jnp.int32, (F, F), 0)
    s_id = lax.broadcasted_iota(jnp.int32, (F, F), 1)
    fetched["ld"].wait()
    ld_f = ldv[0]
    ld_b = ldv[1]
    tail_f = jnp.dot(ld_f, (r_id > s_id).astype(F32), precision=HIGH, preferred_element_type=F32)
    row_b = jnp.dot(ld_b, (r_id < s_id).astype(F32), precision=HIGH, preferred_element_type=F32)
    to_end = (jnp.exp(tail_f), jnp.exp(row_b))
    fetched["x"].wait()
    fetched["b"].wait()
    turned = []
    for d in range(2):
        for p in range(NI):
            if d == 0:
                turned.append(xv[:, p * PIECE : (p + 1) * PIECE].astype(F32).T)
            scaled = (turned[p] * tall(to_end[d], p * HP)).astype(BF)
            lsend[d, p] = dot(scaled, bv[...]).astype(BF)
        scatter(i, NI, at_i, lsend.at[d], lrecv.at[d], sem_l[d])
        lrecv[d, pl.ds(i, 1)] = lsend[d, pl.ds(i, 1)]

    fetched["c"].wait()
    fetched["gain"].wait()
    crx[pl.ds(i, 1)] = cv[...][None]
    ldrx[pl.ds(i, 1)] = ldv[...][None]
    gram = dot_nt(cv[...], bv[...])
    gram = jnp.where(r_id == s_id, 2.0 * gram, gram)
    row_f = jnp.dot(ld_f, (r_id <= s_id).astype(F32), precision=HIGH, preferred_element_type=F32)
    lower = s_id <= r_id
    col_f = dot_nt(lower.astype(F32), ld_f, HIGH)
    col_b = dot_nt((s_id < r_id).astype(F32), ld_b, HIGH)
    left = s_id < HD
    for p in range(NI):
        x_pair = xv[:, p * PIECE : (p + 1) * PIECE].astype(F32)
        weights = []
        for h in range(HP * p, HP * p + HP):
            at_f = jnp.broadcast_to(col_f[:, h : h + 1], (F, F))
            at_b = jnp.broadcast_to(col_b[:, h : h + 1], (F, F))
            exponent = jnp.where(lower, at_f - row_f[h : h + 1], row_b[h : h + 1] - at_b)
            weights.append((jnp.exp(exponent) * gram).astype(BF))
        apart = jnp.concatenate(
            [jnp.where(left, x_pair, 0.0), jnp.where(left, 0.0, x_pair)], axis=0
        ).astype(BF)
        intra = dot(jnp.concatenate(weights, axis=1), apart)
        inside = intra + jnp.where(left[0:1], gain[HP * p], gain[HP * p + 1]) * x_pair
        pre[p] = inside
        prebf[p] = inside.astype(BF)
    rims = (
        remote(prebf.at[:, 0:RIM], rim_r, sem_rim, {"frames": prev}),
        remote(prebf.at[:, RIM:F], rim_l, sem_rim + 1, {"frames": succ}),
    )
    for copy in rims:
        start(copy)

    rows, tots, decays = [], [], []
    state_of = [None, None]

    def group_states(d):
        if d == 0:
            arrive(i, NI, at_i, ld_hbm, ldrx, sem_ld)
            for j in range(NI):
                picked = jnp.concatenate(
                    [
                        functools.reduce(
                            lambda a, p: jnp.where(i == p, ldrx[j, e, HP * p : HP * p + HP, :], a),
                            range(1, NI),
                            ldrx[j, e, 0:HP, :],
                        )
                        for e in range(2)
                    ],
                    axis=0,
                )
                rows.append(picked)
                tots.append(
                    jnp.broadcast_to(jnp.sum(picked, axis=1, keepdims=True), (2 * HP, N))
                )
                decays.append(jnp.exp(tots[j]))
            gtsend[...] = jnp.concatenate(
                [functools.reduce(jnp.add, tots), jnp.zeros((8 - 2 * HP, N), F32)], axis=0
            )
            share(g, ng, at_g, gtsend, gtrecv, sem_gt)
            gtrecv[g] = gtsend[...]
        arrive(i, NI, at_i, lsend.at[d, 0], lrecv.at[d], sem_l[d])
        state = jnp.zeros((PIECE, N), F32)
        for j in range(NI) if d == 0 else reversed(range(NI)):
            within[d, j] = state.astype(BF)
            state = tall(decays[j], d * HP) * state + lrecv[d, j].astype(F32)
        for k in range(ng):
            gsend[d, k] = state[k * sub : (k + 1) * sub].astype(BF)
        scatter(g, ng, at_g, gsend.at[d], grecv.at[d], sem_g[d])
        grecv[d, pl.ds(g, 1)] = gsend[d, pl.ds(g, 1)]

    group_tots = [[], []]
    into = [[None] * ng, [None] * ng]
    ahead = [[None] * ng, [None] * ng]

    def row_states(d):
        if d == 0:
            arrive(g, ng, at_g, gtsend, gtrecv, sem_gt)
            head = (g * sub) // HD
            for k in range(ng):
                for e in range(2):
                    one = gtrecv[k, e * HP : e * HP + 1, :]
                    for h in range(1, HP):
                        one = jnp.where(head == h, gtrecv[k, e * HP + h : e * HP + h + 1, :], one)
                    group_tots[e].append(one)
            if ny > 1:
                ytsend[...] = jnp.concatenate(
                    [functools.reduce(jnp.add, group_tots[e]) for e in range(2)]
                    + [jnp.zeros((6, N), F32)],
                    axis=0,
                )
                share(y, ny, at_y, ytsend, ytrecv, sem_yt)
                ytrecv[y] = ytsend[...]
        arrive(g, ng, at_g, gsend.at[d, 0], grecv.at[d], sem_g[d])
        state, total = jnp.zeros((sub, N), F32), jnp.zeros((1, N), F32)
        for k in range(ng) if d == 0 else reversed(range(ng)):
            into[d][k], ahead[d][k] = state, jnp.exp(total)
            state = jnp.exp(group_tots[d][k]) * state + grecv[d, k].astype(F32)
            total = total + group_tots[d][k]
        if ny > 1:
            ysend[d] = state.astype(BF)
            share(y, ny, at_y, ysend.at[d], yrecv.at[d], sem_y[d])
            yrecv[d, pl.ds(y, 1)] = ysend[d][None]

    def entering(d):
        enter = jnp.zeros((sub, N), F32)
        if ny > 1:
            if d == 0:
                arrive(y, ny, at_y, ytsend, ytrecv, sem_yt)
            arrive(y, ny, at_y, ysend.at[d], yrecv.at[d], sem_y[d])
            state = jnp.zeros((sub, N), F32)
            for k in range(ny) if d == 0 else reversed(range(ny)):
                enter = jnp.where(y == k, state, enter)
                state = jnp.exp(ytrecv[k, d : d + 1, :]) * state + yrecv[d, k].astype(F32)
        for k in range(ng):
            csend[d, k] = (into[d][k] + ahead[d][k] * enter).astype(BF)
        scatter(g, ng, at_g, csend.at[d], crecv.at[d], sem_b[d])
        crecv[d, pl.ds(g, 1)] = csend[d, pl.ds(g, 1)]

    group_states(0)
    group_states(1)

    arrive(i, NI, at_i, c_hbm, crx, sem_c)
    picked_f = jnp.concatenate([r[0:HP] for r in rows], axis=0)
    picked_b = jnp.concatenate([r[HP : 2 * HP] for r in rows], axis=0)
    cols = (
        dot_nt(lower.astype(F32), picked_f, HIGH),
        dot_nt((s_id >= r_id).astype(F32), picked_b, HIGH),
    )

    def group_terms(d):
        total = jnp.zeros((2 * HP, N), F32)
        for j in range(NI) if d == 0 else reversed(range(NI)):
            at = [jnp.broadcast_to(cols[d][:, HP * j + h : HP * j + h + 1], (F, F)) for h in range(HP)]
            spread = jnp.exp(jnp.where(left, at[0], at[1]))
            lead = jnp.exp(
                jnp.where(left[0:1], total[d * HP : d * HP + 1], total[d * HP + 1 : d * HP + 2])
            )
            grown[d, j] = spread * lead
            part = spread * dot_nt(crx[j], within[d, j])
            local_part[j] = part if d == 0 else local_part[j] + part
            total = total + tots[j]

    group_terms(0)
    row_states(0)
    row_states(1)
    group_terms(1)
    entering(0)
    entering(1)

    fetched["start"].wait()
    fetched["len"].wait()
    groups = starts.shape[0]
    tokens, window = bias.shape
    per_group = tokens // groups
    place = lax.broadcasted_iota(jnp.int32, (per_group, window), 1) + (me * F - RIM)
    for k in range(groups):
        allowed = (place >= starts[k]) & (place < starts[k] + lens[k])
        bias[k * per_group : (k + 1) * per_group, :] = jnp.where(allowed, 0.0, -jnp.inf)
    rwin[0:RIM] = jnp.zeros((RIM, N), BF)
    rwin[RIM + NI * F :] = jnp.zeros((RIM, N), BF)

    for d in range(2):
        arrive(g, ng, at_g, csend.at[d, 0], crecv.at[d], sem_b[d])
        carried = crecv[d].reshape(PIECE, N)
        for j in range(NI):
            part = local_part[j] + grown[d, j] * dot_nt(crx[j], carried)
            if d == 0:
                local_part[j] = part
            else:
                rwin[RIM + j * F : RIM + (j + 1) * F] = part.astype(BF)
    for k in range(1, NI):
        p = lax.rem(i + k, NI)
        src = rwin.at[pl.ds(pl.multiple_of(p * F, F), 2 * F)]
        start(remote(src, rin.at[i], sem_r + k - 1, {"frames": at_i(p)}))
    start(
        remote(rwin.at[RIM : 2 * RIM], rx.at[i], sem_rx, {"frames": base_prev + NI - 1}, sem_rx + i)
    )
    start(
        remote(rwin.at[NI * F : NI * F + RIM], rx.at[i], sem_rx + 1, {"frames": base_succ}, sem_rx + i)
    )
    rin[pl.ds(i, 1)] = rwin[pl.ds(pl.multiple_of(i * F, F), 2 * F)][None]
    remote(prebf.at[:, 0:RIM], rim_r, sem_rim, {"frames": prev}).wait_recv()
    remote(prebf.at[:, RIM:F], rim_l, sem_rim + 1, {"frames": succ}).wait_recv()

    def rows_in(q):
        remote(rwin.at[0:RIM], rx.at[q], sem_rx, {"frames": prev}, sem_rx + q).wait_recv()

    for k in range(NI):
        q = lax.rem(i + NI - k, NI)
        if k > 0:
            remote(
                rwin.at[0 : 2 * F], rin.at[q], sem_r + k - 1, {"frames": at_i(q)}
            ).wait_recv()

        @pl.when((i == 0) | (i == NI - 1))
        def _():
            rows_in(q)

        @pl.when(i == 0)
        def _():
            rin[q, 0:RIM] = rx[q]

        @pl.when(i == NI - 1)
        def _():
            rin[q, RIM + F :] = rx[q]

        wide[tok, q, 0:RIM] = (rim_l[q].astype(F32) + rin[q, 0:RIM].astype(F32)).astype(BF)
        wide[tok, q, RIM : RIM + F] = (pre[q] + rin[q, RIM : RIM + F].astype(F32)).astype(BF)
        wide[tok, q, RIM + F :] = (rim_r[q].astype(F32) + rin[q, RIM + F :].astype(F32)).astype(BF)
        if tok_count > 1:
            start(remote(wide.at[tok, q], wide.at[tok, q], sem_w + k, {"tok": 1 - tok}))

    fetched["wk"].wait()
    fetched["wv"].wait()

    def half_rows(t):
        return jnp.concatenate([wide[t, p] for p in range(NI)], axis=1)

    mine = half_rows(tok)
    at = pl.ds(pl.multiple_of(tok * half, half), half)
    kacc[...] = dot(mine, wk[at, :])
    vacc[...] = dot(mine, wv[at, :])
    if tok_count > 1:
        other = 1 - tok
        for k in range(NI):
            q = lax.rem(i + NI - k, NI)
            remote(wide.at[tok, q], wide.at[other, q], sem_w + k, {"tok": other}).wait_recv()
        theirs = half_rows(other)
        at = pl.ds(pl.multiple_of(other * half, half), half)
        keys[...] = (kacc[...] + dot(theirs, wk[at, :])).astype(BF)
        values[...] = (vacc[...] + dot(theirs, wv[at, :])).astype(BF)
    else:
        keys[...] = kacc[...].astype(BF)
        values[...] = vacc[...].astype(BF)
    fetched["q"].wait()
    for copy in sent:
        copy.wait_send()


def reader(wide, keys, values, queries, bias, enc_ref, out_ref):
    tok = lax.axis_index("tok")
    for p in range(NI):
        enc_ref[:, p * PIECE : (p + 1) * PIECE] = wide[tok, p, RIM : RIM + F]
    left = lax.broadcasted_iota(jnp.int32, (1, 2 * DHD), 1) < DHD
    for p in range(queries.shape[1] // (2 * DHD)):
        cols = slice(p * 2 * DHD, (p + 1) * 2 * DHD)
        q_pair = queries[:, cols]
        k_pair = keys[:, cols].astype(F32)
        v_pair = values[:, cols]
        both = []
        for only in (jnp.where(left, k_pair, 0.0), jnp.where(left, 0.0, k_pair)):
            scores = dot_nt(q_pair, only.astype(BF)) + bias[...]
            top = jnp.max(scores, axis=1, keepdims=True)
            raised = jnp.exp((scores - top) * DHD ** (-0.5))
            whole = 1.0 / jnp.sum(raised, axis=1, keepdims=True)
            both.append(dot((raised * whole).astype(BF), v_pair))
        out_ref[:, cols] = jnp.where(left, both[0], both[1]).astype(BF)


def solution(mesh):
    frames = mesh.shape["frames"]
    tok_count = mesh.shape["tok"]
    ng = min(4, frames // NI)
    ny = frames // (NI * ng)
    sub = PIECE // ng
    vmem = pl.BlockSpec(memory_space=pltpu.VMEM)
    hbm = pl.BlockSpec(memory_space=pltpu.HBM)

    def local(x, b, c, log_decay, gain, key_weight, value_weight, queries, span_start, span_len):
        count, width = x.shape
        window = 2 * count
        tokens, out_width = queries.shape
        copies = 5 * (NI - 1) + 5 * (ng - 1) + 3 * (ny - 1) + 2 + 2 * NI
        wide, keys, values, held, bias = pl.pallas_call(
            functools.partial(mixer, (ny, ng, tok_count)),
            out_shape=(
                jax.ShapeDtypeStruct((tok_count, NI, window, PIECE), BF),
                jax.ShapeDtypeStruct((window, out_width), BF),
                jax.ShapeDtypeStruct((window, out_width), BF),
                jax.ShapeDtypeStruct(queries.shape, BF),
                jax.ShapeDtypeStruct((tokens, window), F32),
            ),
            in_specs=[hbm] * 10,
            out_specs=(vmem,) * 5,
            scratch_shapes=[
                pltpu.VMEM(x.shape, BF),
                pltpu.VMEM(b.shape, BF),
                pltpu.VMEM(c.shape, BF),
                pltpu.VMEM(log_decay.shape, F32),
                pltpu.SMEM(gain.shape, F32),
                pltpu.SMEM(span_start.shape, jnp.int32),
                pltpu.SMEM(span_len.shape, jnp.int32),
                pltpu.VMEM(key_weight.shape, BF),
                pltpu.VMEM(value_weight.shape, BF),
                pltpu.VMEM((2, NI, PIECE, N), BF),
                pltpu.VMEM((2, NI, PIECE, N), BF),
                pltpu.VMEM((NI,) + c.shape, BF),
                pltpu.VMEM((NI,) + log_decay.shape, F32),
                pltpu.VMEM((2, ng, sub, N), BF),
                pltpu.VMEM((2, ng, sub, N), BF),
                pltpu.VMEM((8, N), F32),
                pltpu.VMEM((ng, 8, N), F32),
                pltpu.VMEM((2, sub, N), BF),
                pltpu.VMEM((2, ny, sub, N), BF),
                pltpu.VMEM((8, N), F32),
                pltpu.VMEM((ny, 8, N), F32),
                pltpu.VMEM((2, ng, sub, N), BF),
                pltpu.VMEM((2, ng, sub, N), BF),
                pltpu.VMEM((NI, count, PIECE), F32),
                pltpu.VMEM((NI, count, PIECE), BF),
                pltpu.VMEM((NI, RIM, PIECE), BF),
                pltpu.VMEM((NI, RIM, PIECE), BF),
                pltpu.VMEM((2, NI, PIECE, N), BF),
                pltpu.VMEM((2, NI, count, PIECE), F32),
                pltpu.VMEM((NI, count, PIECE), F32),
                pltpu.VMEM((2 * RIM + NI * count, PIECE), BF),
                pltpu.VMEM((NI, window, PIECE), BF),
                pltpu.VMEM((NI, RIM, PIECE), BF),
                pltpu.VMEM((window, out_width), F32),
                pltpu.VMEM((window, out_width), F32),
                pltpu.SemaphoreType.DMA((10,)),
                pltpu.SemaphoreType.DMA((copies,)),
                pltpu.SemaphoreType.DMA((copies,)),
            ],
            compiler_params=pltpu.CompilerParams(
                collective_id=0, has_side_effects=True, vmem_limit_bytes=24 * 2**20
            ),
        )(
            *(
                pltpu.with_memory_space_constraint(a, pltpu.HBM)
                for a in (
                    x,
                    b,
                    c,
                    log_decay,
                    gain,
                    key_weight,
                    value_weight,
                    queries,
                    span_start,
                    span_len,
                )
            )
        )
        return pl.pallas_call(
            reader,
            out_shape=(
                jax.ShapeDtypeStruct((count, width), BF),
                jax.ShapeDtypeStruct(queries.shape, BF),
            ),
            in_specs=[vmem] * 5,
            out_specs=(vmem, vmem),
            compiler_params=pltpu.CompilerParams(vmem_limit_bytes=24 * 2**20),
        )(wide, keys, values, held, bias)

    placed = (
        P(("dp", "frames"), "tok"),
        P(("dp", "frames"), None),
        P(("dp", "frames"), None),
        P(None, "tok", ("dp", "frames")),
        P("tok"),
        P(None, "tok"),
        P(None, "tok"),
        P(("dp", "frames"), "tok"),
        P(("dp", "frames")),
        P(("dp", "frames")),
    )
    return jax.shard_map(
        local,
        mesh=mesh,
        in_specs=placed,
        out_specs=(P(("dp", "frames"), "tok"), P(("dp", "frames"), "tok")),
        check_vma=False,
    )
```

```python
import functools

import jax
import jax.numpy as jnp
from jax import lax
from jax.experimental import pallas as pl
from jax.experimental.pallas import tpu as pltpu
from jax.sharding import PartitionSpec as P

DHD = 64
F = 128
RIM = 64
N = 128
HD = 64
NI = 2
PAIRS = 4
HP = 2 * PAIRS // NI
LP = PAIRS // NI
PIECE = HP * HD
MESH = pl.DeviceIdType.MESH
HIGH = lax.Precision.HIGHEST
NT = (((1,), (1,)), ((), ()))
BF = jnp.bfloat16
F32 = jnp.float32


def dot(a, b):
    return jnp.dot(a, b, preferred_element_type=F32)


def dot_nt(a, b, precision=None):
    return lax.dot_general(a, b, NT, precision=precision, preferred_element_type=F32)


def thirds(a):
    high = a.astype(BF)
    rest = a - high.astype(F32)
    mid = rest.astype(BF)
    return high, mid, (rest - mid.astype(F32)).astype(BF)


def sum_rows(parts, mask):
    both = dot(jnp.concatenate(parts, axis=0), mask.astype(BF))
    n = parts[0].shape[0]
    return both[0:n] + both[n : 2 * n] + both[2 * n : 3 * n]


def sum_cols(mask, parts):
    return functools.reduce(jnp.add, [dot_nt(mask.astype(BF), p) for p in reversed(parts)])


def tall(tile, first):
    return jnp.concatenate(
        [jnp.broadcast_to(tile[first + k : first + k + 1], (HD, N)) for k in range(HP)], axis=0
    )


def mixer(
    dims,
    x_hbm,
    b_hbm,
    c_hbm,
    ld_hbm,
    gain_hbm,
    wk_hbm,
    wv_hbm,
    q_hbm,
    start_hbm,
    len_hbm,
    wide,
    keys,
    values,
    q_out,
    bias,
    xv,
    bv,
    cv,
    ldv,
    gain,
    starts,
    lens,
    wk,
    wv,
    lsend,
    lrecv,
    crx,
    ldrx,
    gsend,
    grecv,
    gtsend,
    gtrecv,
    ysend,
    yrecv,
    ytsend,
    ytrecv,
    csend,
    crecv,
    pre,
    prebf,
    rim_l,
    rim_r,
    within,
    grown,
    local_part,
    rwin,
    rin,
    rx,
    kacc,
    vacc,
    hsem,
    ssem,
    rsem,
):
    ny, ng, tok_count = dims
    heads = ldv.shape[1]
    half = xv.shape[1]
    sub = PIECE // ng
    frames = ny * ng * NI
    row = ng * NI
    me = lax.axis_index("frames")
    tok = lax.axis_index("tok")
    y = me // row
    g = lax.rem(me // NI, ng)
    i = lax.rem(me, NI)
    base = me - i

    def at_i(p):
        return base + p

    def at_g(p):
        return me + (p - g) * NI

    def at_y(p):
        return me + (p - y) * row

    prev = lax.rem(me + frames - 1, frames)
    succ = lax.rem(me + 1, frames)
    base_prev = lax.rem(base + frames - NI, frames)
    base_succ = lax.rem(base + NI, frames)

    fetched = {}

    def fetch(name, src, dst):
        copy = pltpu.make_async_copy(src, dst, hsem.at[len(fetched)])
        copy.start()
        fetched[name] = copy

    fetch("ld", ld_hbm, ldv)
    fetch("x", x_hbm, xv)
    fetch("b", b_hbm, bv)
    fetch("c", c_hbm, cv)
    fetch("gain", gain_hbm, gain)
    fetch("start", start_hbm, starts)
    fetch("len", len_hbm, lens)
    fetch("wk", wk_hbm, wk)
    fetch("wv", wv_hbm, wv)
    fetch("q", q_hbm, q_out)

    barrier = pltpu.get_barrier_semaphore()

    def greet(**device):
        pl.semaphore_signal(barrier, inc=1, device_id=device, device_id_type=MESH)

    greeted = 0
    for own, count, place in ((i, NI, at_i), (g, ng, at_g), (y, ny, at_y)):
        for k in range(1, count):
            greet(frames=place(lax.rem(own + k, count)))
            greeted += 1
    greet(frames=prev)
    greet(frames=succ)
    greeted += 2
    if tok_count > 1:
        greet(tok=1 - tok)
        greeted += 1

    @pl.when(i == 0)
    def _():
        for k in range(NI):
            greet(frames=base_prev + k)

    @pl.when(i == NI - 1)
    def _():
        for k in range(NI):
            greet(frames=base_succ + k)

    greeted += 2

    sent = []
    taken = [0]

    def take(n):
        first = taken[0]
        taken[0] += n
        return first

    def remote(src, dst, index, device, landing=None):
        return pltpu.make_async_remote_copy(
            src_ref=src,
            dst_ref=dst,
            send_sem=ssem.at[index],
            recv_sem=rsem.at[index if landing is None else landing],
            device_id=device,
            device_id_type=MESH,
        )

    def start(copy):
        copy.start()
        sent.append(copy)

    def scatter(own, count, place, src, dst, first):
        for k in range(1, count):
            p = lax.rem(own + k, count)
            start(remote(src.at[p], dst.at[own], first + k - 1, {"frames": place(p)}))

    def share(own, count, place, src, dst, first):
        for k in range(1, count):
            p = lax.rem(own + k, count)
            start(remote(src, dst.at[own], first + k - 1, {"frames": place(p)}))

    def arrive(own, count, place, src, dst, first):
        for k in range(1, count):
            q = lax.rem(own + count - k, count)
            remote(src, dst.at[q], first + k - 1, {"frames": place(q)}).wait_recv()

    sem_ld, sem_c = take(NI - 1), take(NI - 1)
    sem_l = (take(NI - 1), take(NI - 1))
    sem_gt = take(ng - 1)
    sem_g = (take(ng - 1), take(ng - 1))
    sem_yt = take(ny - 1)
    sem_y = (take(ny - 1), take(ny - 1))
    sem_b = (take(ng - 1), take(ng - 1))
    sem_rim = take(2)
    sem_r = take(NI - 1)
    sem_rx = take(NI)
    sem_w = take(NI)

    pl.semaphore_wait(barrier, greeted)
    share(i, NI, at_i, ld_hbm, ldrx, sem_ld)
    share(i, NI, at_i, c_hbm, crx, sem_c)

    r_id = lax.broadcasted_iota(jnp.int32, (F, F), 0)
    s_id = lax.broadcasted_iota(jnp.int32, (F, F), 1)
    fetched["ld"].wait()
    parts_f = thirds(ldv[0])
    to_end = [jnp.exp(sum_rows(parts_f, (r_id > s_id).astype(F32))), None]
    fetched["x"].wait()
    fetched["b"].wait()
    turned = []
    row_b = None
    for d in range(2):
        if d == 1:
            parts_b = thirds(ldv[1])
            row_b = sum_rows(parts_b, (r_id < s_id).astype(F32))
            to_end[1] = jnp.exp(row_b)
        for p in range(NI):
            if d == 0:
                turned.append(xv[:, p * PIECE : (p + 1) * PIECE].astype(F32).T)
            scaled = (turned[p] * tall(to_end[d], p * HP)).astype(BF)
            lsend[d, p] = dot(scaled, bv[...]).astype(BF)

            @pl.when(i != p)
            def _():
                slot = sem_l[d] + lax.rem(p - i + NI, NI) - 1
                remote(lsend.at[d, p], lrecv.at[d, i], slot, {"frames": at_i(p)}).start()

        for k in range(1, NI):
            p = lax.rem(i + k, NI)
            sent.append(remote(lsend.at[d, p], lrecv.at[d, i], sem_l[d] + k - 1, {"frames": at_i(p)}))
        lrecv[d, pl.ds(i, 1)] = lsend[d, pl.ds(i, 1)]

    fetched["c"].wait()
    fetched["gain"].wait()
    crx[pl.ds(i, 1)] = cv[...][None]
    ldrx[pl.ds(i, 1)] = ldv[...][None]
    gram = dot_nt(cv[...], bv[...])
    gram = jnp.where(r_id == s_id, 2.0 * gram, gram)
    lower = s_id <= r_id
    row_f = sum_rows(parts_f, (r_id <= s_id).astype(F32))
    col_f = sum_cols(lower.astype(F32), parts_f)
    col_b = sum_cols((s_id < r_id).astype(F32), parts_b)
    left = s_id < HD
    for p in range(PAIRS):
        x_pair = xv[:, p * 2 * HD : (p + 1) * 2 * HD].astype(F32)
        weights = []
        for h in (2 * p, 2 * p + 1):
            at_f = jnp.broadcast_to(col_f[:, h : h + 1], (F, F))
            at_b = jnp.broadcast_to(col_b[:, h : h + 1], (F, F))
            exponent = jnp.where(lower, at_f - row_f[h : h + 1], row_b[h : h + 1] - at_b)
            weights.append((jnp.exp(exponent) * gram).astype(BF))
        apart = jnp.concatenate(
            [jnp.where(left, x_pair, 0.0), jnp.where(left, 0.0, x_pair)], axis=0
        ).astype(BF)
        intra = dot(jnp.concatenate(weights, axis=1), apart)
        inside = intra + jnp.where(left[0:1], gain[2 * p], gain[2 * p + 1]) * x_pair
        pre[p] = inside
        prebf[p] = inside.astype(BF)
    rims = (
        remote(prebf.at[:, 0:RIM], rim_r, sem_rim, {"frames": prev}),
        remote(prebf.at[:, RIM:F], rim_l, sem_rim + 1, {"frames": succ}),
    )
    for copy in rims:
        start(copy)

    rows, tots, decays = [], [], []
    state_of = [None, None]

    def group_states(d):
        if d == 0:
            arrive(i, NI, at_i, ld_hbm, ldrx, sem_ld)
            for j in range(NI):
                picked = jnp.concatenate(
                    [
                        functools.reduce(
                            lambda a, p: jnp.where(i == p, ldrx[j, e, HP * p : HP * p + HP, :], a),
                            range(1, NI),
                            ldrx[j, e, 0:HP, :],
                        )
                        for e in range(2)
                    ],
                    axis=0,
                )
                rows.append(picked)
                tots.append(
                    jnp.broadcast_to(jnp.sum(picked, axis=1, keepdims=True), (2 * HP, N))
                )
                decays.append(jnp.exp(tots[j]))
            gtsend[0 : 2 * HP] = functools.reduce(jnp.add, tots)
            if 2 * HP < 8:
                gtsend[2 * HP :] = jnp.zeros((8 - 2 * HP, N), F32)
            share(g, ng, at_g, gtsend, gtrecv, sem_gt)
            gtrecv[g] = gtsend[...]
        arrive(i, NI, at_i, lsend.at[d, 0], lrecv.at[d], sem_l[d])
        state = jnp.zeros((PIECE, N), F32)
        for j in range(NI) if d == 0 else reversed(range(NI)):
            within[d, j] = state.astype(BF)
            state = tall(decays[j], d * HP) * state + lrecv[d, j].astype(F32)
        for k in range(ng):
            gsend[d, k] = state[k * sub : (k + 1) * sub].astype(BF)
        scatter(g, ng, at_g, gsend.at[d], grecv.at[d], sem_g[d])
        grecv[d, pl.ds(g, 1)] = gsend[d, pl.ds(g, 1)]

    group_tots = [[], []]
    into = [[None] * ng, [None] * ng]
    ahead = [[None] * ng, [None] * ng]

    def row_states(d):
        if d == 0:
            arrive(g, ng, at_g, gtsend, gtrecv, sem_gt)
            head = (g * sub) // HD
            for k in range(ng):
                for e in range(2):
                    one = gtrecv[k, e * HP : e * HP + 1, :]
                    for h in range(1, HP):
                        one = jnp.where(head == h, gtrecv[k, e * HP + h : e * HP + h + 1, :], one)
                    group_tots[e].append(one)
            if ny > 1:
                ytsend[...] = jnp.concatenate(
                    [functools.reduce(jnp.add, group_tots[e]) for e in range(2)]
                    + [jnp.zeros((6, N), F32)],
                    axis=0,
                )
                share(y, ny, at_y, ytsend, ytrecv, sem_yt)
                ytrecv[y] = ytsend[...]
        arrive(g, ng, at_g, gsend.at[d, 0], grecv.at[d], sem_g[d])
        state, total = jnp.zeros((sub, N), F32), jnp.zeros((1, N), F32)
        for k in range(ng) if d == 0 else reversed(range(ng)):
            into[d][k], ahead[d][k] = state, jnp.exp(total)
            state = jnp.exp(group_tots[d][k]) * state + grecv[d, k].astype(F32)
            total = total + group_tots[d][k]
        if ny > 1:
            ysend[d] = state.astype(BF)
            share(y, ny, at_y, ysend.at[d], yrecv.at[d], sem_y[d])
            yrecv[d, pl.ds(y, 1)] = ysend[d][None]

    def entering(d):
        enter = jnp.zeros((sub, N), F32)
        if ny > 1:
            if d == 0:
                arrive(y, ny, at_y, ytsend, ytrecv, sem_yt)
            arrive(y, ny, at_y, ysend.at[d], yrecv.at[d], sem_y[d])
            state = jnp.zeros((sub, N), F32)
            for k in range(ny) if d == 0 else reversed(range(ny)):
                enter = jnp.where(y == k, state, enter)
                state = jnp.exp(ytrecv[k, d : d + 1, :]) * state + yrecv[d, k].astype(F32)
        for k in range(ng):
            csend[d, k] = (into[d][k] + ahead[d][k] * enter).astype(BF)
        scatter(g, ng, at_g, csend.at[d], crecv.at[d], sem_b[d])
        crecv[d, pl.ds(g, 1)] = csend[d, pl.ds(g, 1)]

    group_states(0)
    group_states(1)

    arrive(i, NI, at_i, c_hbm, crx, sem_c)
    picked_f = jnp.concatenate([r[0:HP] for r in rows], axis=0)
    picked_b = jnp.concatenate([r[HP : 2 * HP] for r in rows], axis=0)
    cols = (
        sum_cols(lower.astype(F32), thirds(picked_f)),
        sum_cols((s_id >= r_id).astype(F32), thirds(picked_b)),
    )

    def group_terms(d):
        total = jnp.zeros((2 * HP, N), F32)
        for j in range(NI) if d == 0 else reversed(range(NI)):
            for e in range(LP):
                at = [
                    jnp.broadcast_to(cols[d][:, HP * j + 2 * e + h : HP * j + 2 * e + h + 1], (F, F))
                    for h in range(2)
                ]
                spread = jnp.exp(jnp.where(left, at[0], at[1]))
                h = d * HP + 2 * e
                lead = jnp.exp(jnp.where(left[0:1], total[h : h + 1], total[h + 1 : h + 2]))
                grown[d, j, e] = spread * lead
                part = spread * dot_nt(crx[j], within[d, j, e * N : (e + 1) * N])
                local_part[j, e] = part if d == 0 else local_part[j, e] + part
            total = total + tots[j]

    group_terms(0)
    row_states(0)
    row_states(1)
    group_terms(1)
    entering(0)
    entering(1)

    fetched["start"].wait()
    fetched["len"].wait()
    groups = starts.shape[0]
    tokens, window = bias.shape
    per_group = tokens // groups
    place = lax.broadcasted_iota(jnp.int32, (per_group, window), 1) + (me * F - RIM)
    for k in range(groups):
        allowed = (place >= starts[k]) & (place < starts[k] + lens[k])
        bias[k * per_group : (k + 1) * per_group, :] = jnp.where(allowed, 0.0, -jnp.inf)
    rwin[:, 0:RIM] = jnp.zeros((LP, RIM, N), BF)
    rwin[:, RIM + NI * F :] = jnp.zeros((LP, RIM, N), BF)

    for d in range(2):
        arrive(g, ng, at_g, csend.at[d, 0], crecv.at[d], sem_b[d])
        carried = crecv[d].reshape(PIECE, N)
        for j in range(NI):
            for e in range(LP):
                part = local_part[j, e] + grown[d, j, e] * dot_nt(crx[j], carried[e * N : (e + 1) * N])
                if d == 0:
                    local_part[j, e] = part
                else:
                    rwin[e, RIM + j * F : RIM + (j + 1) * F] = part.astype(BF)

    def pairs_of(q):
        return pl.ds(q * LP, LP)

    for k in range(1, NI):
        p = lax.rem(i + k, NI)
        src = rwin.at[:, pl.ds(pl.multiple_of(p * F, F), 2 * F)]
        start(remote(src, rin.at[pairs_of(i)], sem_r + k - 1, {"frames": at_i(p)}))
    rim_there = rx.at[pairs_of(i)]
    start(
        remote(rwin.at[:, RIM : 2 * RIM], rim_there, sem_rx, {"frames": base_prev + NI - 1}, sem_rx + i)
    )
    start(
        remote(
            rwin.at[:, NI * F : NI * F + RIM], rim_there, sem_rx + 1, {"frames": base_succ}, sem_rx + i
        )
    )
    rin[pairs_of(i)] = rwin[:, pl.ds(pl.multiple_of(i * F, F), 2 * F)]
    remote(prebf.at[:, 0:RIM], rim_r, sem_rim, {"frames": prev}).wait_recv()
    remote(prebf.at[:, RIM:F], rim_l, sem_rim + 1, {"frames": succ}).wait_recv()

    def rows_in(q):
        remote(
            rwin.at[:, 0:RIM], rx.at[pairs_of(q)], sem_rx, {"frames": prev}, sem_rx + q
        ).wait_recv()

    for k in range(NI):
        q = lax.rem(i + NI - k, NI)
        if k > 0:
            remote(
                rwin.at[:, 0 : 2 * F], rin.at[pairs_of(q)], sem_r + k - 1, {"frames": at_i(q)}
            ).wait_recv()

        @pl.when((i == 0) | (i == NI - 1))
        def _():
            rows_in(q)

        @pl.when(i == 0)
        def _():
            rin[pairs_of(q), 0:RIM] = rx[pairs_of(q)]

        @pl.when(i == NI - 1)
        def _():
            rin[pairs_of(q), RIM + F :] = rx[pairs_of(q)]

        for e in range(LP):
            m = q * LP + e
            wide[tok, m, 0:RIM] = (rim_l[m].astype(F32) + rin[m, 0:RIM].astype(F32)).astype(BF)
            wide[tok, m, RIM : RIM + F] = (pre[m] + rin[m, RIM : RIM + F].astype(F32)).astype(BF)
            wide[tok, m, RIM + F :] = (rim_r[m].astype(F32) + rin[m, RIM + F :].astype(F32)).astype(BF)
        if tok_count > 1:
            piece = wide.at[tok, pairs_of(q)]
            start(remote(piece, piece, sem_w + k, {"tok": 1 - tok}))

    fetched["wk"].wait()
    fetched["wv"].wait()

    def half_rows(t):
        return jnp.concatenate([wide[t, p] for p in range(PAIRS)], axis=1)

    mine = half_rows(tok)
    at = pl.ds(pl.multiple_of(tok * half, half), half)
    kacc[...] = dot(mine, wk[at, :])
    vacc[...] = dot(mine, wv[at, :])
    if tok_count > 1:
        other = 1 - tok
        for k in range(NI):
            q = lax.rem(i + NI - k, NI)
            piece = wide.at[other, pairs_of(q)]
            remote(piece, piece, sem_w + k, {"tok": other}).wait_recv()
        theirs = half_rows(other)
        at = pl.ds(pl.multiple_of(other * half, half), half)
        keys[...] = (kacc[...] + dot(theirs, wk[at, :])).astype(BF)
        values[...] = (vacc[...] + dot(theirs, wv[at, :])).astype(BF)
    else:
        keys[...] = kacc[...].astype(BF)
        values[...] = vacc[...].astype(BF)
    fetched["q"].wait()
    for copy in sent:
        copy.wait_send()


def reader(wide, keys, values, queries, bias, enc_hbm, out_hbm, enc, out, sem):
    tok = lax.axis_index("tok")
    for p in range(PAIRS):
        enc[:, p * 2 * HD : (p + 1) * 2 * HD] = wide[tok, p, RIM : RIM + F]
    copies = [pltpu.make_async_copy(enc, enc_hbm, sem.at[0])]
    copies[0].start()
    left = lax.broadcasted_iota(jnp.int32, (1, 2 * DHD), 1) < DHD
    for p in range(queries.shape[1] // (2 * DHD)):
        cols = slice(p * 2 * DHD, (p + 1) * 2 * DHD)
        q_pair = queries[:, cols]
        k_pair = keys[:, cols].astype(F32)
        v_pair = values[:, cols]
        both = []
        for only in (jnp.where(left, k_pair, 0.0), jnp.where(left, 0.0, k_pair)):
            scores = dot_nt(q_pair, only.astype(BF)) + bias[...]
            top = jnp.max(scores, axis=1, keepdims=True)
            raised = jnp.exp((scores - top) * DHD ** (-0.5))
            whole = 1.0 / jnp.sum(raised, axis=1, keepdims=True)
            both.append(dot(raised.astype(BF), v_pair) * whole)
        out[:, cols] = jnp.where(left, both[0], both[1]).astype(BF)
        copies.append(pltpu.make_async_copy(out.at[:, cols], out_hbm.at[:, cols], sem.at[p + 1]))
        copies[-1].start()
    for copy in copies:
        copy.wait()


def solution(mesh):
    frames = mesh.shape["frames"]
    tok_count = mesh.shape["tok"]
    ng = min(16 // NI, frames // NI)
    ny = frames // (NI * ng)
    sub = PIECE // ng
    vmem = pl.BlockSpec(memory_space=pltpu.VMEM)
    hbm = pl.BlockSpec(memory_space=pltpu.HBM)

    def local(x, b, c, log_decay, gain, key_weight, value_weight, queries, span_start, span_len):
        count, width = x.shape
        window = 2 * count
        tokens, out_width = queries.shape
        copies = 5 * (NI - 1) + 5 * (ng - 1) + 3 * (ny - 1) + 2 + 2 * NI
        wide, keys, values, held, bias = pl.pallas_call(
            functools.partial(mixer, (ny, ng, tok_count)),
            out_shape=(
                jax.ShapeDtypeStruct((tok_count, PAIRS, window, N), BF),
                jax.ShapeDtypeStruct((window, out_width), BF),
                jax.ShapeDtypeStruct((window, out_width), BF),
                jax.ShapeDtypeStruct(queries.shape, BF),
                jax.ShapeDtypeStruct((tokens, window), F32),
            ),
            in_specs=[hbm] * 10,
            out_specs=(vmem,) * 5,
            scratch_shapes=[
                pltpu.VMEM(x.shape, BF),
                pltpu.VMEM(b.shape, BF),
                pltpu.VMEM(c.shape, BF),
                pltpu.VMEM(log_decay.shape, F32),
                pltpu.SMEM(gain.shape, F32),
                pltpu.SMEM(span_start.shape, jnp.int32),
                pltpu.SMEM(span_len.shape, jnp.int32),
                pltpu.VMEM(key_weight.shape, BF),
                pltpu.VMEM(value_weight.shape, BF),
                pltpu.VMEM((2, NI, PIECE, N), BF),
                pltpu.VMEM((2, NI, PIECE, N), BF),
                pltpu.VMEM((NI,) + c.shape, BF),
                pltpu.VMEM((NI,) + log_decay.shape, F32),
                pltpu.VMEM((2, ng, sub, N), BF),
                pltpu.VMEM((2, ng, sub, N), BF),
                pltpu.VMEM((8, N), F32),
                pltpu.VMEM((ng, 8, N), F32),
                pltpu.VMEM((2, sub, N), BF),
                pltpu.VMEM((2, ny, sub, N), BF),
                pltpu.VMEM((8, N), F32),
                pltpu.VMEM((ny, 8, N), F32),
                pltpu.VMEM((2, ng, sub, N), BF),
                pltpu.VMEM((2, ng, sub, N), BF),
                pltpu.VMEM((PAIRS, count, N), F32),
                pltpu.VMEM((PAIRS, count, N), BF),
                pltpu.VMEM((PAIRS, RIM, N), BF),
                pltpu.VMEM((PAIRS, RIM, N), BF),
                pltpu.VMEM((2, NI, PIECE, N), BF),
                pltpu.VMEM((2, NI, LP, count, N), F32),
                pltpu.VMEM((NI, LP, count, N), F32),
                pltpu.VMEM((LP, 2 * RIM + NI * count, N), BF),
                pltpu.VMEM((PAIRS, window, N), BF),
                pltpu.VMEM((PAIRS, RIM, N), BF),
                pltpu.VMEM((window, out_width), F32),
                pltpu.VMEM((window, out_width), F32),
                pltpu.SemaphoreType.DMA((10,)),
                pltpu.SemaphoreType.DMA((copies,)),
                pltpu.SemaphoreType.DMA((copies,)),
            ],
            compiler_params=pltpu.CompilerParams(
                collective_id=0, has_side_effects=True, vmem_limit_bytes=24 * 2**20
            ),
        )(
            *(
                pltpu.with_memory_space_constraint(a, pltpu.HBM)
                for a in (
                    x,
                    b,
                    c,
                    log_decay,
                    gain,
                    key_weight,
                    value_weight,
                    queries,
                    span_start,
                    span_len,
                )
            )
        )
        return pl.pallas_call(
            reader,
            out_shape=(
                jax.ShapeDtypeStruct((count, width), BF),
                jax.ShapeDtypeStruct(queries.shape, BF),
            ),
            in_specs=[vmem] * 5,
            out_specs=(hbm, hbm),
            scratch_shapes=[
                pltpu.VMEM((count, width), BF),
                pltpu.VMEM(queries.shape, BF),
                pltpu.SemaphoreType.DMA((out_width // (2 * DHD) + 1,)),
            ],
            compiler_params=pltpu.CompilerParams(vmem_limit_bytes=24 * 2**20),
        )(wide, keys, values, held, bias)

    placed = (
        P(("dp", "frames"), "tok"),
        P(("dp", "frames"), None),
        P(("dp", "frames"), None),
        P(None, "tok", ("dp", "frames")),
        P("tok"),
        P(None, "tok"),
        P(None, "tok"),
        P(("dp", "frames"), "tok"),
        P(("dp", "frames")),
        P(("dp", "frames")),
    )
    return jax.shard_map(
        local,
        mesh=mesh,
        in_specs=placed,
        out_specs=(P(("dp", "frames"), "tok"), P(("dp", "frames"), "tok")),
        check_vma=False,
    )
```

```python
import functools

import jax
import jax.numpy as jnp
from jax import lax
from jax.experimental import pallas as pl
from jax.experimental.pallas import tpu as pltpu
from jax.sharding import PartitionSpec as P

DHD = 64
F = 128
RIM = 64
N = 128
HD = 64
NI = 4
PAIRS = 4
HP = 2 * PAIRS // NI
LP = PAIRS // NI
PIECE = HP * HD
MESH = pl.DeviceIdType.MESH
HIGH = lax.Precision.HIGHEST
NT = (((1,), (1,)), ((), ()))
BF = jnp.bfloat16
F32 = jnp.float32


def dot(a, b):
    return jnp.dot(a, b, preferred_element_type=F32)


def dot_nt(a, b, precision=None):
    return lax.dot_general(a, b, NT, precision=precision, preferred_element_type=F32)


def thirds(a):
    high = a.astype(BF)
    rest = a - high.astype(F32)
    mid = rest.astype(BF)
    return high, mid, (rest - mid.astype(F32)).astype(BF)


def sum_rows(parts, mask):
    both = dot(jnp.concatenate(parts, axis=0), mask.astype(BF))
    n = parts[0].shape[0]
    return both[0:n] + both[n : 2 * n] + both[2 * n : 3 * n]


def sum_cols(mask, parts):
    return functools.reduce(jnp.add, [dot_nt(mask.astype(BF), p) for p in reversed(parts)])


def tall(tile, first):
    return jnp.concatenate(
        [jnp.broadcast_to(tile[first + k : first + k + 1], (HD, N)) for k in range(HP)], axis=0
    )


def mixer(
    dims,
    x_hbm,
    b_hbm,
    c_hbm,
    ld_hbm,
    gain_hbm,
    wk_hbm,
    wv_hbm,
    q_hbm,
    start_hbm,
    len_hbm,
    wide,
    keys,
    values,
    q_out,
    bias,
    xv,
    bv,
    cv,
    ldv,
    gain,
    starts,
    lens,
    wk,
    wv,
    lsend,
    lrecv,
    crx,
    ldrx,
    gsend,
    grecv,
    gtsend,
    gtrecv,
    ysend,
    yrecv,
    ytsend,
    ytrecv,
    csend,
    crecv,
    pre,
    prebf,
    rim_l,
    rim_r,
    within,
    grown,
    local_part,
    rwin,
    rin,
    rx,
    kacc,
    vacc,
    hsem,
    ssem,
    rsem,
):
    ny, ng, tok_count = dims
    heads = ldv.shape[1]
    half = xv.shape[1]
    sub = PIECE // ng
    frames = ny * ng * NI
    row = ng * NI
    me = lax.axis_index("frames")
    tok = lax.axis_index("tok")
    y = me // row
    g = lax.rem(me // NI, ng)
    i = lax.rem(me, NI)
    base = me - i

    def at_i(p):
        return base + p

    def at_g(p):
        return me + (p - g) * NI

    def at_y(p):
        return me + (p - y) * row

    prev = lax.rem(me + frames - 1, frames)
    succ = lax.rem(me + 1, frames)
    base_prev = lax.rem(base + frames - NI, frames)
    base_succ = lax.rem(base + NI, frames)

    fetched = {}

    def fetch(name, src, dst):
        copy = pltpu.make_async_copy(src, dst, hsem.at[len(fetched)])
        copy.start()
        fetched[name] = copy

    fetch("ld", ld_hbm, ldv)
    fetch("x", x_hbm, xv)
    fetch("b", b_hbm, bv)
    fetch("c", c_hbm, cv)
    fetch("gain", gain_hbm, gain)
    fetch("start", start_hbm, starts)
    fetch("len", len_hbm, lens)
    fetch("wk", wk_hbm, wk)
    fetch("wv", wv_hbm, wv)
    fetch("q", q_hbm, q_out)

    barrier = pltpu.get_barrier_semaphore()

    def greet(**device):
        pl.semaphore_signal(barrier, inc=1, device_id=device, device_id_type=MESH)

    greeted = 0
    for own, count, place in ((i, NI, at_i), (g, ng, at_g), (y, ny, at_y)):
        for k in range(1, count):
            greet(frames=place(lax.rem(own + k, count)))
            greeted += 1
    greet(frames=prev)
    greet(frames=succ)
    greeted += 2
    if tok_count > 1:
        greet(tok=1 - tok)
        greeted += 1

    @pl.when(i == 0)
    def _():
        for k in range(NI):
            greet(frames=base_prev + k)

    @pl.when(i == NI - 1)
    def _():
        for k in range(NI):
            greet(frames=base_succ + k)

    greeted += 2

    sent = []
    taken = [0]

    def take(n):
        first = taken[0]
        taken[0] += n
        return first

    def remote(src, dst, index, device, landing=None):
        return pltpu.make_async_remote_copy(
            src_ref=src,
            dst_ref=dst,
            send_sem=ssem.at[index],
            recv_sem=rsem.at[index if landing is None else landing],
            device_id=device,
            device_id_type=MESH,
        )

    def start(copy):
        copy.start()
        sent.append(copy)

    def scatter(own, count, place, src, dst, first):
        for k in range(1, count):
            p = lax.rem(own + k, count)
            start(remote(src.at[p], dst.at[own], first + k - 1, {"frames": place(p)}))

    def share(own, count, place, src, dst, first):
        for k in range(1, count):
            p = lax.rem(own + k, count)
            start(remote(src, dst.at[own], first + k - 1, {"frames": place(p)}))

    def arrive(own, count, place, src, dst, first):
        for k in range(1, count):
            q = lax.rem(own + count - k, count)
            remote(src, dst.at[q], first + k - 1, {"frames": place(q)}).wait_recv()

    sem_ld, sem_c = take(NI - 1), take(NI - 1)
    sem_l = (take(NI - 1), take(NI - 1))
    sem_gt = take(ng - 1)
    sem_g = (take(ng - 1), take(ng - 1))
    sem_yt = take(ny - 1)
    sem_y = (take(ny - 1), take(ny - 1))
    sem_b = (take(ng - 1), take(ng - 1))
    sem_rim = take(2)
    sem_r = take(NI - 1)
    sem_rx = take(NI)
    sem_w = take(NI)

    pl.semaphore_wait(barrier, greeted)
    share(i, NI, at_i, ld_hbm, ldrx, sem_ld)
    share(i, NI, at_i, c_hbm, crx, sem_c)

    r_id = lax.broadcasted_iota(jnp.int32, (F, F), 0)
    s_id = lax.broadcasted_iota(jnp.int32, (F, F), 1)
    fetched["ld"].wait()
    parts_f = thirds(ldv[0])
    to_end = [jnp.exp(sum_rows(parts_f, (r_id > s_id).astype(F32))), None]
    fetched["x"].wait()
    fetched["b"].wait()
    turned = []
    row_b = None
    for d in range(2):
        if d == 1:
            parts_b = thirds(ldv[1])
            row_b = sum_rows(parts_b, (r_id < s_id).astype(F32))
            to_end[1] = jnp.exp(row_b)
        for p in range(NI):
            if d == 0:
                turned.append(xv[:, p * PIECE : (p + 1) * PIECE].astype(F32).T)
            scaled = (turned[p] * tall(to_end[d], p * HP)).astype(BF)
            lsend[d, p] = dot(scaled, bv[...]).astype(BF)

            @pl.when(i != p)
            def _():
                slot = sem_l[d] + lax.rem(p - i + NI, NI) - 1
                remote(lsend.at[d, p], lrecv.at[d, i], slot, {"frames": at_i(p)}).start()

        for k in range(1, NI):
            p = lax.rem(i + k, NI)
            sent.append(remote(lsend.at[d, p], lrecv.at[d, i], sem_l[d] + k - 1, {"frames": at_i(p)}))
        lrecv[d, pl.ds(i, 1)] = lsend[d, pl.ds(i, 1)]

    fetched["c"].wait()
    fetched["gain"].wait()
    crx[pl.ds(i, 1)] = cv[...][None]
    ldrx[pl.ds(i, 1)] = ldv[...][None]
    gram = dot_nt(cv[...], bv[...])
    gram = jnp.where(r_id == s_id, 2.0 * gram, gram)
    lower = s_id <= r_id
    row_f = sum_rows(parts_f, (r_id <= s_id).astype(F32))
    col_f = sum_cols(lower.astype(F32), parts_f)
    col_b = sum_cols((s_id < r_id).astype(F32), parts_b)
    left = s_id < HD
    for p in range(PAIRS):
        x_pair = xv[:, p * 2 * HD : (p + 1) * 2 * HD].astype(F32)
        weights = []
        for h in (2 * p, 2 * p + 1):
            at_f = jnp.broadcast_to(col_f[:, h : h + 1], (F, F))
            at_b = jnp.broadcast_to(col_b[:, h : h + 1], (F, F))
            exponent = jnp.where(lower, at_f - row_f[h : h + 1], row_b[h : h + 1] - at_b)
            weights.append((jnp.exp(exponent) * gram).astype(BF))
        apart = jnp.concatenate(
            [jnp.where(left, x_pair, 0.0), jnp.where(left, 0.0, x_pair)], axis=0
        ).astype(BF)
        intra = dot(jnp.concatenate(weights, axis=1), apart)
        inside = intra + jnp.where(left[0:1], gain[2 * p], gain[2 * p + 1]) * x_pair
        pre[p] = inside
        prebf[p] = inside.astype(BF)
    rims = (
        remote(prebf.at[:, 0:RIM], rim_r, sem_rim, {"frames": prev}),
        remote(prebf.at[:, RIM:F], rim_l, sem_rim + 1, {"frames": succ}),
    )
    for copy in rims:
        start(copy)

    rows, tots, decays = [], [], []
    state_of = [None, None]

    def group_states(d):
        if d == 0:
            arrive(i, NI, at_i, ld_hbm, ldrx, sem_ld)
            for j in range(NI):
                picked = jnp.concatenate(
                    [
                        functools.reduce(
                            lambda a, p: jnp.where(i == p, ldrx[j, e, HP * p : HP * p + HP, :], a),
                            range(1, NI),
                            ldrx[j, e, 0:HP, :],
                        )
                        for e in range(2)
                    ],
                    axis=0,
                )
                rows.append(picked)
                tots.append(
                    jnp.broadcast_to(jnp.sum(picked, axis=1, keepdims=True), (2 * HP, N))
                )
                decays.append(jnp.exp(tots[j]))
            gtsend[0 : 2 * HP] = functools.reduce(jnp.add, tots)
            if 2 * HP < 8:
                gtsend[2 * HP :] = jnp.zeros((8 - 2 * HP, N), F32)
            share(g, ng, at_g, gtsend, gtrecv, sem_gt)
            gtrecv[g] = gtsend[...]
        arrive(i, NI, at_i, lsend.at[d, 0], lrecv.at[d], sem_l[d])
        state = jnp.zeros((PIECE, N), F32)
        for j in range(NI) if d == 0 else reversed(range(NI)):
            within[d, j] = state.astype(BF)
            state = tall(decays[j], d * HP) * state + lrecv[d, j].astype(F32)
        for k in range(ng):
            gsend[d, k] = state[k * sub : (k + 1) * sub].astype(BF)
        scatter(g, ng, at_g, gsend.at[d], grecv.at[d], sem_g[d])
        grecv[d, pl.ds(g, 1)] = gsend[d, pl.ds(g, 1)]

    group_tots = [[], []]
    into = [[None] * ng, [None] * ng]
    ahead = [[None] * ng, [None] * ng]

    def row_states(d):
        if d == 0:
            arrive(g, ng, at_g, gtsend, gtrecv, sem_gt)
            head = (g * sub) // HD
            for k in range(ng):
                for e in range(2):
                    one = gtrecv[k, e * HP : e * HP + 1, :]
                    for h in range(1, HP):
                        one = jnp.where(head == h, gtrecv[k, e * HP + h : e * HP + h + 1, :], one)
                    group_tots[e].append(one)
            if ny > 1:
                ytsend[...] = jnp.concatenate(
                    [functools.reduce(jnp.add, group_tots[e]) for e in range(2)]
                    + [jnp.zeros((6, N), F32)],
                    axis=0,
                )
                share(y, ny, at_y, ytsend, ytrecv, sem_yt)
                ytrecv[y] = ytsend[...]
        arrive(g, ng, at_g, gsend.at[d, 0], grecv.at[d], sem_g[d])
        state, total = jnp.zeros((sub, N), F32), jnp.zeros((1, N), F32)
        for k in range(ng) if d == 0 else reversed(range(ng)):
            into[d][k], ahead[d][k] = state, jnp.exp(total)
            state = jnp.exp(group_tots[d][k]) * state + grecv[d, k].astype(F32)
            total = total + group_tots[d][k]
        if ny > 1:
            ysend[d] = state.astype(BF)
            share(y, ny, at_y, ysend.at[d], yrecv.at[d], sem_y[d])
            yrecv[d, pl.ds(y, 1)] = ysend[d][None]

    def entering(d):
        enter = jnp.zeros((sub, N), F32)
        if ny > 1:
            if d == 0:
                arrive(y, ny, at_y, ytsend, ytrecv, sem_yt)
            arrive(y, ny, at_y, ysend.at[d], yrecv.at[d], sem_y[d])
            state = jnp.zeros((sub, N), F32)
            for k in range(ny) if d == 0 else reversed(range(ny)):
                enter = jnp.where(y == k, state, enter)
                state = jnp.exp(ytrecv[k, d : d + 1, :]) * state + yrecv[d, k].astype(F32)
        for k in range(ng):
            csend[d, k] = (into[d][k] + ahead[d][k] * enter).astype(BF)
        scatter(g, ng, at_g, csend.at[d], crecv.at[d], sem_b[d])
        crecv[d, pl.ds(g, 1)] = csend[d, pl.ds(g, 1)]

    group_states(0)
    group_states(1)

    arrive(i, NI, at_i, c_hbm, crx, sem_c)
    picked_f = jnp.concatenate([r[0:HP] for r in rows], axis=0)
    picked_b = jnp.concatenate([r[HP : 2 * HP] for r in rows], axis=0)
    cols = (
        sum_cols(lower.astype(F32), thirds(picked_f)),
        sum_cols((s_id >= r_id).astype(F32), thirds(picked_b)),
    )

    def group_terms(d):
        total = jnp.zeros((2 * HP, N), F32)
        for j in range(NI) if d == 0 else reversed(range(NI)):
            for e in range(LP):
                at = [
                    jnp.broadcast_to(cols[d][:, HP * j + 2 * e + h : HP * j + 2 * e + h + 1], (F, F))
                    for h in range(2)
                ]
                spread = jnp.exp(jnp.where(left, at[0], at[1]))
                h = d * HP + 2 * e
                lead = jnp.exp(jnp.where(left[0:1], total[h : h + 1], total[h + 1 : h + 2]))
                grown[d, j, e] = spread * lead
                part = spread * dot_nt(crx[j], within[d, j, e * N : (e + 1) * N])
                local_part[j, e] = part if d == 0 else local_part[j, e] + part
            total = total + tots[j]

    group_terms(0)
    row_states(0)
    row_states(1)
    group_terms(1)
    entering(0)
    entering(1)

    fetched["start"].wait()
    fetched["len"].wait()
    groups = starts.shape[0]
    tokens, window = bias.shape
    per_group = tokens // groups
    place = lax.broadcasted_iota(jnp.int32, (per_group, window), 1) + (me * F - RIM)
    for k in range(groups):
        allowed = (place >= starts[k]) & (place < starts[k] + lens[k])
        bias[k * per_group : (k + 1) * per_group, :] = jnp.where(allowed, 0.0, -jnp.inf)
    rwin[:, 0:RIM] = jnp.zeros((LP, RIM, N), BF)
    rwin[:, RIM + NI * F :] = jnp.zeros((LP, RIM, N), BF)

    for d in range(2):
        arrive(g, ng, at_g, csend.at[d, 0], crecv.at[d], sem_b[d])
        carried = crecv[d].reshape(PIECE, N)
        for j in range(NI):
            for e in range(LP):
                part = local_part[j, e] + grown[d, j, e] * dot_nt(crx[j], carried[e * N : (e + 1) * N])
                if d == 0:
                    local_part[j, e] = part
                else:
                    rwin[e, RIM + j * F : RIM + (j + 1) * F] = part.astype(BF)

    def pairs_of(q):
        return pl.ds(q * LP, LP)

    for k in range(1, NI):
        p = lax.rem(i + k, NI)
        src = rwin.at[:, pl.ds(pl.multiple_of(p * F, F), 2 * F)]
        start(remote(src, rin.at[pairs_of(i)], sem_r + k - 1, {"frames": at_i(p)}))
    rim_there = rx.at[pairs_of(i)]
    start(
        remote(rwin.at[:, RIM : 2 * RIM], rim_there, sem_rx, {"frames": base_prev + NI - 1}, sem_rx + i)
    )
    start(
        remote(
            rwin.at[:, NI * F : NI * F + RIM], rim_there, sem_rx + 1, {"frames": base_succ}, sem_rx + i
        )
    )
    rin[pairs_of(i)] = rwin[:, pl.ds(pl.multiple_of(i * F, F), 2 * F)]
    remote(prebf.at[:, 0:RIM], rim_r, sem_rim, {"frames": prev}).wait_recv()
    remote(prebf.at[:, RIM:F], rim_l, sem_rim + 1, {"frames": succ}).wait_recv()

    def rows_in(q):
        remote(
            rwin.at[:, 0:RIM], rx.at[pairs_of(q)], sem_rx, {"frames": prev}, sem_rx + q
        ).wait_recv()

    for k in range(NI):
        q = lax.rem(i + NI - k, NI)
        if k > 0:
            remote(
                rwin.at[:, 0 : 2 * F], rin.at[pairs_of(q)], sem_r + k - 1, {"frames": at_i(q)}
            ).wait_recv()

        @pl.when((i == 0) | (i == NI - 1))
        def _():
            rows_in(q)

        @pl.when(i == 0)
        def _():
            rin[pairs_of(q), 0:RIM] = rx[pairs_of(q)]

        @pl.when(i == NI - 1)
        def _():
            rin[pairs_of(q), RIM + F :] = rx[pairs_of(q)]

        for e in range(LP):
            m = q * LP + e
            wide[tok, m, 0:RIM] = (rim_l[m].astype(F32) + rin[m, 0:RIM].astype(F32)).astype(BF)
            wide[tok, m, RIM : RIM + F] = (pre[m] + rin[m, RIM : RIM + F].astype(F32)).astype(BF)
            wide[tok, m, RIM + F :] = (rim_r[m].astype(F32) + rin[m, RIM + F :].astype(F32)).astype(BF)
        if tok_count > 1:
            piece = wide.at[tok, pairs_of(q)]
            start(remote(piece, piece, sem_w + k, {"tok": 1 - tok}))

    fetched["wk"].wait()
    fetched["wv"].wait()

    def half_rows(t):
        return jnp.concatenate([wide[t, p] for p in range(PAIRS)], axis=1)

    mine = half_rows(tok)
    at = pl.ds(pl.multiple_of(tok * half, half), half)
    kacc[...] = dot(mine, wk[at, :])
    vacc[...] = dot(mine, wv[at, :])
    if tok_count > 1:
        other = 1 - tok
        for k in range(NI):
            q = lax.rem(i + NI - k, NI)
            piece = wide.at[other, pairs_of(q)]
            remote(piece, piece, sem_w + k, {"tok": other}).wait_recv()
        theirs = half_rows(other)
        at = pl.ds(pl.multiple_of(other * half, half), half)
        keys[...] = (kacc[...] + dot(theirs, wk[at, :])).astype(BF)
        values[...] = (vacc[...] + dot(theirs, wv[at, :])).astype(BF)
    else:
        keys[...] = kacc[...].astype(BF)
        values[...] = vacc[...].astype(BF)
    fetched["q"].wait()
    for copy in sent:
        copy.wait_send()


def reader(wide, keys, values, queries, bias, enc_hbm, out_hbm, enc, out, sem):
    tok = lax.axis_index("tok")
    for p in range(PAIRS):
        enc[:, p * 2 * HD : (p + 1) * 2 * HD] = wide[tok, p, RIM : RIM + F]
    copies = [pltpu.make_async_copy(enc, enc_hbm, sem.at[0])]
    copies[0].start()
    left = lax.broadcasted_iota(jnp.int32, (1, 2 * DHD), 1) < DHD
    for p in range(queries.shape[1] // (2 * DHD)):
        cols = slice(p * 2 * DHD, (p + 1) * 2 * DHD)
        q_pair = queries[:, cols]
        k_pair = keys[:, cols].astype(F32)
        v_pair = values[:, cols]
        both = []
        for only in (jnp.where(left, k_pair, 0.0), jnp.where(left, 0.0, k_pair)):
            scores = dot_nt(q_pair, only.astype(BF)) + bias[...]
            top = jnp.max(scores, axis=1, keepdims=True)
            raised = jnp.exp((scores - top) * DHD ** (-0.5))
            whole = 1.0 / jnp.sum(raised, axis=1, keepdims=True)
            both.append(dot(raised.astype(BF), v_pair) * whole)
        out[:, cols] = jnp.where(left, both[0], both[1]).astype(BF)
        copies.append(pltpu.make_async_copy(out.at[:, cols], out_hbm.at[:, cols], sem.at[p + 1]))
        copies[-1].start()
    for copy in copies:
        copy.wait()


def solution(mesh):
    frames = mesh.shape["frames"]
    tok_count = mesh.shape["tok"]
    ng = min(16 // NI, frames // NI)
    ny = frames // (NI * ng)
    sub = PIECE // ng
    vmem = pl.BlockSpec(memory_space=pltpu.VMEM)
    hbm = pl.BlockSpec(memory_space=pltpu.HBM)

    def local(x, b, c, log_decay, gain, key_weight, value_weight, queries, span_start, span_len):
        count, width = x.shape
        window = 2 * count
        tokens, out_width = queries.shape
        copies = 5 * (NI - 1) + 5 * (ng - 1) + 3 * (ny - 1) + 2 + 2 * NI
        wide, keys, values, held, bias = pl.pallas_call(
            functools.partial(mixer, (ny, ng, tok_count)),
            out_shape=(
                jax.ShapeDtypeStruct((tok_count, PAIRS, window, N), BF),
                jax.ShapeDtypeStruct((window, out_width), BF),
                jax.ShapeDtypeStruct((window, out_width), BF),
                jax.ShapeDtypeStruct(queries.shape, BF),
                jax.ShapeDtypeStruct((tokens, window), F32),
            ),
            in_specs=[hbm] * 10,
            out_specs=(vmem,) * 5,
            scratch_shapes=[
                pltpu.VMEM(x.shape, BF),
                pltpu.VMEM(b.shape, BF),
                pltpu.VMEM(c.shape, BF),
                pltpu.VMEM(log_decay.shape, F32),
                pltpu.SMEM(gain.shape, F32),
                pltpu.SMEM(span_start.shape, jnp.int32),
                pltpu.SMEM(span_len.shape, jnp.int32),
                pltpu.VMEM(key_weight.shape, BF),
                pltpu.VMEM(value_weight.shape, BF),
                pltpu.VMEM((2, NI, PIECE, N), BF),
                pltpu.VMEM((2, NI, PIECE, N), BF),
                pltpu.VMEM((NI,) + c.shape, BF),
                pltpu.VMEM((NI,) + log_decay.shape, F32),
                pltpu.VMEM((2, ng, sub, N), BF),
                pltpu.VMEM((2, ng, sub, N), BF),
                pltpu.VMEM((8, N), F32),
                pltpu.VMEM((ng, 8, N), F32),
                pltpu.VMEM((2, sub, N), BF),
                pltpu.VMEM((2, ny, sub, N), BF),
                pltpu.VMEM((8, N), F32),
                pltpu.VMEM((ny, 8, N), F32),
                pltpu.VMEM((2, ng, sub, N), BF),
                pltpu.VMEM((2, ng, sub, N), BF),
                pltpu.VMEM((PAIRS, count, N), F32),
                pltpu.VMEM((PAIRS, count, N), BF),
                pltpu.VMEM((PAIRS, RIM, N), BF),
                pltpu.VMEM((PAIRS, RIM, N), BF),
                pltpu.VMEM((2, NI, PIECE, N), BF),
                pltpu.VMEM((2, NI, LP, count, N), F32),
                pltpu.VMEM((NI, LP, count, N), F32),
                pltpu.VMEM((LP, 2 * RIM + NI * count, N), BF),
                pltpu.VMEM((PAIRS, window, N), BF),
                pltpu.VMEM((PAIRS, RIM, N), BF),
                pltpu.VMEM((window, out_width), F32),
                pltpu.VMEM((window, out_width), F32),
                pltpu.SemaphoreType.DMA((10,)),
                pltpu.SemaphoreType.DMA((copies,)),
                pltpu.SemaphoreType.DMA((copies,)),
            ],
            compiler_params=pltpu.CompilerParams(
                collective_id=0, has_side_effects=True, vmem_limit_bytes=24 * 2**20
            ),
        )(
            *(
                pltpu.with_memory_space_constraint(a, pltpu.HBM)
                for a in (
                    x,
                    b,
                    c,
                    log_decay,
                    gain,
                    key_weight,
                    value_weight,
                    queries,
                    span_start,
                    span_len,
                )
            )
        )
        return pl.pallas_call(
            reader,
            out_shape=(
                jax.ShapeDtypeStruct((count, width), BF),
                jax.ShapeDtypeStruct(queries.shape, BF),
            ),
            in_specs=[vmem] * 5,
            out_specs=(hbm, hbm),
            scratch_shapes=[
                pltpu.VMEM((count, width), BF),
                pltpu.VMEM(queries.shape, BF),
                pltpu.SemaphoreType.DMA((out_width // (2 * DHD) + 1,)),
            ],
            compiler_params=pltpu.CompilerParams(vmem_limit_bytes=24 * 2**20),
        )(wide, keys, values, held, bias)

    placed = (
        P(("dp", "frames"), "tok"),
        P(("dp", "frames"), None),
        P(("dp", "frames"), None),
        P(None, "tok", ("dp", "frames")),
        P("tok"),
        P(None, "tok"),
        P(None, "tok"),
        P(("dp", "frames"), "tok"),
        P(("dp", "frames")),
        P(("dp", "frames")),
    )
    return jax.shard_map(
        local,
        mesh=mesh,
        in_specs=placed,
        out_specs=(P(("dp", "frames"), "tok"), P(("dp", "frames"), "tok")),
        check_vma=False,
    )
```

```python
import functools

import jax
import jax.numpy as jnp
from jax import lax
from jax.experimental import pallas as pl
from jax.experimental.pallas import tpu as pltpu
from jax.sharding import PartitionSpec as P

DHD = 64
F = 128
RIM = 64
N = 128
HD = 64
NI = 2
PAIRS = 4
HP = 2 * PAIRS // NI
LP = PAIRS // NI
PIECE = HP * HD
MESH = pl.DeviceIdType.MESH
HIGH = lax.Precision.HIGHEST
NT = (((1,), (1,)), ((), ()))
BF = jnp.bfloat16
F32 = jnp.float32


def dot(a, b):
    return jnp.dot(a, b, preferred_element_type=F32)


def dot_nt(a, b, precision=None):
    return lax.dot_general(a, b, NT, precision=precision, preferred_element_type=F32)


def thirds(a):
    high = a.astype(BF)
    rest = a - high.astype(F32)
    mid = rest.astype(BF)
    return high, mid, (rest - mid.astype(F32)).astype(BF)


def sum_rows(parts, mask):
    both = dot(jnp.concatenate(parts, axis=0), mask.astype(BF))
    n = parts[0].shape[0]
    return both[0:n] + both[n : 2 * n] + both[2 * n : 3 * n]


def sum_cols(mask, parts):
    return functools.reduce(jnp.add, [dot_nt(mask.astype(BF), p) for p in reversed(parts)])


def tall(tile, first):
    return jnp.concatenate(
        [jnp.broadcast_to(tile[first + k : first + k + 1], (HD, N)) for k in range(HP)], axis=0
    )


def mixer(
    dims,
    x_hbm,
    b_hbm,
    c_hbm,
    ld_hbm,
    gain_hbm,
    wk_hbm,
    wv_hbm,
    q_hbm,
    start_hbm,
    len_hbm,
    wide,
    keys,
    values,
    q_out,
    bias,
    xv,
    bv,
    cv,
    ldv,
    gain,
    starts,
    lens,
    wk,
    wv,
    lsend,
    lrecv,
    crx,
    ldrx,
    gsend,
    grecv,
    gtsend,
    gtrecv,
    ysend,
    yrecv,
    ytsend,
    ytrecv,
    csend,
    crecv,
    pre,
    prebf,
    rim_l,
    rim_r,
    within,
    grown,
    local_part,
    rwin,
    rin,
    rx,
    kacc,
    vacc,
    hsem,
    ssem,
    rsem,
):
    ny, ng, tok_count = dims
    heads = ldv.shape[1]
    half = xv.shape[1]
    sub = PIECE // ng
    frames = ny * ng * NI
    row = ng * NI
    me = lax.axis_index("frames")
    tok = lax.axis_index("tok")
    y = me // row
    g = lax.rem(me // NI, ng)
    i = lax.rem(me, NI)
    base = me - i

    def at_i(p):
        return base + p

    def at_g(p):
        return me + (p - g) * NI

    def at_y(p):
        return me + (p - y) * row

    prev = lax.rem(me + frames - 1, frames)
    succ = lax.rem(me + 1, frames)
    base_prev = lax.rem(base + frames - NI, frames)
    base_succ = lax.rem(base + NI, frames)

    fetched = {}

    def fetch(name, src, dst):
        copy = pltpu.make_async_copy(src, dst, hsem.at[len(fetched)])
        copy.start()
        fetched[name] = copy

    fetch("ld", ld_hbm, ldv)
    fetch("x", x_hbm, xv)
    fetch("b", b_hbm, bv)
    fetch("c", c_hbm, cv)
    fetch("gain", gain_hbm, gain)
    fetch("start", start_hbm, starts)
    fetch("len", len_hbm, lens)
    fetch("wk", wk_hbm, wk)
    fetch("wv", wv_hbm, wv)
    fetch("q", q_hbm, q_out)

    barrier = pltpu.get_barrier_semaphore()

    def greet(**device):
        pl.semaphore_signal(barrier, inc=1, device_id=device, device_id_type=MESH)

    greeted = 0
    for own, count, place in ((i, NI, at_i), (g, ng, at_g), (y, ny, at_y)):
        for k in range(1, count):
            greet(frames=place(lax.rem(own + k, count)))
            greeted += 1
    greet(frames=prev)
    greet(frames=succ)
    greeted += 2
    if tok_count > 1:
        greet(tok=1 - tok)
        greeted += 1

    @pl.when(i == 0)
    def _():
        for k in range(NI):
            greet(frames=base_prev + k)

    @pl.when(i == NI - 1)
    def _():
        for k in range(NI):
            greet(frames=base_succ + k)

    greeted += 2

    sent = []
    taken = [0]

    def take(n):
        first = taken[0]
        taken[0] += n
        return first

    def remote(src, dst, index, device, landing=None):
        return pltpu.make_async_remote_copy(
            src_ref=src,
            dst_ref=dst,
            send_sem=ssem.at[index],
            recv_sem=rsem.at[index if landing is None else landing],
            device_id=device,
            device_id_type=MESH,
        )

    def start(copy):
        copy.start()
        sent.append(copy)

    def far_first(count):
        return sorted(range(1, count), key=lambda k: -min(k, count - k))

    def scatter(own, count, place, src, dst, first):
        for k in far_first(count):
            p = lax.rem(own + k, count)
            start(remote(src.at[p], dst.at[own], first + k - 1, {"frames": place(p)}))

    def share(own, count, place, src, dst, first):
        for k in far_first(count):
            p = lax.rem(own + k, count)
            start(remote(src, dst.at[own], first + k - 1, {"frames": place(p)}))

    def arrive(own, count, place, src, dst, first):
        for k in range(1, count):
            q = lax.rem(own + count - k, count)
            remote(src, dst.at[q], first + k - 1, {"frames": place(q)}).wait_recv()

    sem_ld, sem_c = take(NI - 1), take(NI - 1)
    sem_l = (take(NI - 1), take(NI - 1))
    sem_gt = take(ng - 1)
    sem_g = (take(ng - 1), take(ng - 1))
    sem_yt = take(ny - 1)
    sem_y = (take(ny - 1), take(ny - 1))
    sem_b = (take(ng - 1), take(ng - 1))
    sem_rim = take(2)
    sem_r = take(NI - 1)
    sem_rx = take(NI)
    sem_w = take(NI)

    pl.semaphore_wait(barrier, greeted)
    share(i, NI, at_i, ld_hbm, ldrx, sem_ld)
    share(i, NI, at_i, c_hbm, crx, sem_c)

    r_id = lax.broadcasted_iota(jnp.int32, (F, F), 0)
    s_id = lax.broadcasted_iota(jnp.int32, (F, F), 1)
    fetched["ld"].wait()
    parts_f = thirds(ldv[0])
    to_end = [jnp.exp(sum_rows(parts_f, (r_id > s_id).astype(F32))), None]
    fetched["x"].wait()
    fetched["b"].wait()
    turned = []
    row_b = None
    for d in range(2):
        if d == 1:
            parts_b = thirds(ldv[1])
            row_b = sum_rows(parts_b, (r_id < s_id).astype(F32))
            to_end[1] = jnp.exp(row_b)
        for p in range(NI):
            if d == 0:
                turned.append(xv[:, p * PIECE : (p + 1) * PIECE].astype(F32).T)
            scaled = (turned[p] * tall(to_end[d], p * HP)).astype(BF)
            lsend[d, p] = dot(scaled, bv[...]).astype(BF)

            @pl.when(i != p)
            def _():
                slot = sem_l[d] + lax.rem(p - i + NI, NI) - 1
                remote(lsend.at[d, p], lrecv.at[d, i], slot, {"frames": at_i(p)}).start()

        for k in range(1, NI):
            p = lax.rem(i + k, NI)
            sent.append(remote(lsend.at[d, p], lrecv.at[d, i], sem_l[d] + k - 1, {"frames": at_i(p)}))
        lrecv[d, pl.ds(i, 1)] = lsend[d, pl.ds(i, 1)]

    ldrx[pl.ds(i, 1)] = ldv[...][None]
    rows, tots, decays = [], [], []
    state_of = [None, None]

    def group_states(d):
        if d == 0:
            arrive(i, NI, at_i, ld_hbm, ldrx, sem_ld)
            for j in range(NI):
                picked = jnp.concatenate(
                    [
                        functools.reduce(
                            lambda a, p: jnp.where(i == p, ldrx[j, e, HP * p : HP * p + HP, :], a),
                            range(1, NI),
                            ldrx[j, e, 0:HP, :],
                        )
                        for e in range(2)
                    ],
                    axis=0,
                )
                rows.append(picked)
                tots.append(
                    jnp.broadcast_to(jnp.sum(picked, axis=1, keepdims=True), (2 * HP, N))
                )
                decays.append(jnp.exp(tots[j]))
            gtsend[0 : 2 * HP] = functools.reduce(jnp.add, tots)
            if 2 * HP < 8:
                gtsend[2 * HP :] = jnp.zeros((8 - 2 * HP, N), F32)
            share(g, ng, at_g, gtsend, gtrecv, sem_gt)
            gtrecv[g] = gtsend[...]
        arrive(i, NI, at_i, lsend.at[d, 0], lrecv.at[d], sem_l[d])
        state = jnp.zeros((PIECE, N), F32)
        for j in range(NI) if d == 0 else reversed(range(NI)):
            within[d, j] = state.astype(BF)
            state = tall(decays[j], d * HP) * state + lrecv[d, j].astype(F32)
        for k in range(ng):
            gsend[d, k] = state[k * sub : (k + 1) * sub].astype(BF)
        scatter(g, ng, at_g, gsend.at[d], grecv.at[d], sem_g[d])
        grecv[d, pl.ds(g, 1)] = gsend[d, pl.ds(g, 1)]

    group_tots = [[], []]
    into = [[None] * ng, [None] * ng]
    ahead = [[None] * ng, [None] * ng]

    def row_states(d):
        if d == 0:
            arrive(g, ng, at_g, gtsend, gtrecv, sem_gt)
            head = (g * sub) // HD
            for k in range(ng):
                for e in range(2):
                    one = gtrecv[k, e * HP : e * HP + 1, :]
                    for h in range(1, HP):
                        one = jnp.where(head == h, gtrecv[k, e * HP + h : e * HP + h + 1, :], one)
                    group_tots[e].append(one)
            if ny > 1:
                ytsend[...] = jnp.concatenate(
                    [functools.reduce(jnp.add, group_tots[e]) for e in range(2)]
                    + [jnp.zeros((6, N), F32)],
                    axis=0,
                )
                share(y, ny, at_y, ytsend, ytrecv, sem_yt)
                ytrecv[y] = ytsend[...]
        arrive(g, ng, at_g, gsend.at[d, 0], grecv.at[d], sem_g[d])
        state, total = jnp.zeros((sub, N), F32), jnp.zeros((1, N), F32)
        for k in range(ng) if d == 0 else reversed(range(ng)):
            into[d][k], ahead[d][k] = state, jnp.exp(total)
            state = jnp.exp(group_tots[d][k]) * state + grecv[d, k].astype(F32)
            total = total + group_tots[d][k]
        if ny > 1:
            ysend[d] = state.astype(BF)
            share(y, ny, at_y, ysend.at[d], yrecv.at[d], sem_y[d])
            yrecv[d, pl.ds(y, 1)] = ysend[d][None]

    def entering(d):
        enter = jnp.zeros((sub, N), F32)
        if ny > 1:
            if d == 0:
                arrive(y, ny, at_y, ytsend, ytrecv, sem_yt)
            arrive(y, ny, at_y, ysend.at[d], yrecv.at[d], sem_y[d])
            state = jnp.zeros((sub, N), F32)
            for k in range(ny) if d == 0 else reversed(range(ny)):
                enter = jnp.where(y == k, state, enter)
                state = jnp.exp(ytrecv[k, d : d + 1, :]) * state + yrecv[d, k].astype(F32)
        for k in range(ng):
            csend[d, k] = (into[d][k] + ahead[d][k] * enter).astype(BF)
        scatter(g, ng, at_g, csend.at[d], crecv.at[d], sem_b[d])
        crecv[d, pl.ds(g, 1)] = csend[d, pl.ds(g, 1)]

    group_states(0)
    group_states(1)

    fetched["c"].wait()
    fetched["gain"].wait()
    crx[pl.ds(i, 1)] = cv[...][None]
    gram = dot_nt(cv[...], bv[...])
    gram = jnp.where(r_id == s_id, 2.0 * gram, gram)
    lower = s_id <= r_id
    row_f = sum_rows(parts_f, (r_id <= s_id).astype(F32))
    col_f = sum_cols(lower.astype(F32), parts_f)
    col_b = sum_cols((s_id < r_id).astype(F32), parts_b)
    left = s_id < HD
    for p in range(PAIRS):
        x_pair = xv[:, p * 2 * HD : (p + 1) * 2 * HD].astype(F32)
        weights = []
        for h in (2 * p, 2 * p + 1):
            at_f = jnp.broadcast_to(col_f[:, h : h + 1], (F, F))
            at_b = jnp.broadcast_to(col_b[:, h : h + 1], (F, F))
            exponent = jnp.where(lower, at_f - row_f[h : h + 1], row_b[h : h + 1] - at_b)
            weights.append((jnp.exp(exponent) * gram).astype(BF))
        apart = jnp.concatenate(
            [jnp.where(left, x_pair, 0.0), jnp.where(left, 0.0, x_pair)], axis=0
        ).astype(BF)
        intra = dot(jnp.concatenate(weights, axis=1), apart)
        inside = intra + jnp.where(left[0:1], gain[2 * p], gain[2 * p + 1]) * x_pair
        pre[p] = inside
        prebf[p] = inside.astype(BF)
    rims = (
        remote(prebf.at[:, 0:RIM], rim_r, sem_rim, {"frames": prev}),
        remote(prebf.at[:, RIM:F], rim_l, sem_rim + 1, {"frames": succ}),
    )
    for copy in rims:
        start(copy)

    row_states(0)
    row_states(1)

    arrive(i, NI, at_i, c_hbm, crx, sem_c)
    picked_f = jnp.concatenate([r[0:HP] for r in rows], axis=0)
    picked_b = jnp.concatenate([r[HP : 2 * HP] for r in rows], axis=0)
    cols = (
        sum_cols(lower.astype(F32), thirds(picked_f)),
        sum_cols((s_id >= r_id).astype(F32), thirds(picked_b)),
    )

    def group_terms(d):
        total = jnp.zeros((2 * HP, N), F32)
        for j in range(NI) if d == 0 else reversed(range(NI)):
            for e in range(LP):
                at = [
                    jnp.broadcast_to(cols[d][:, HP * j + 2 * e + h : HP * j + 2 * e + h + 1], (F, F))
                    for h in range(2)
                ]
                spread = jnp.exp(jnp.where(left, at[0], at[1]))
                h = d * HP + 2 * e
                lead = jnp.exp(jnp.where(left[0:1], total[h : h + 1], total[h + 1 : h + 2]))
                grown[d, j, e] = spread * lead
                part = spread * dot_nt(crx[j], within[d, j, e * N : (e + 1) * N])
                local_part[j, e] = part if d == 0 else local_part[j, e] + part
            total = total + tots[j]

    group_terms(0)
    group_terms(1)
    entering(0)
    entering(1)

    fetched["start"].wait()
    fetched["len"].wait()
    groups = starts.shape[0]
    tokens, window = bias.shape
    per_group = tokens // groups
    place = lax.broadcasted_iota(jnp.int32, (per_group, window), 1) + (me * F - RIM)
    for k in range(groups):
        allowed = (place >= starts[k]) & (place < starts[k] + lens[k])
        bias[k * per_group : (k + 1) * per_group, :] = jnp.where(allowed, 0.0, -jnp.inf)
    rwin[:, 0:RIM] = jnp.zeros((LP, RIM, N), BF)
    rwin[:, RIM + NI * F :] = jnp.zeros((LP, RIM, N), BF)

    for d in range(2):
        arrive(g, ng, at_g, csend.at[d, 0], crecv.at[d], sem_b[d])
        carried = crecv[d].reshape(PIECE, N)
        for j in range(NI):
            for e in range(LP):
                part = local_part[j, e] + grown[d, j, e] * dot_nt(crx[j], carried[e * N : (e + 1) * N])
                if d == 0:
                    local_part[j, e] = part
                else:
                    rwin[e, RIM + j * F : RIM + (j + 1) * F] = part.astype(BF)

    def pairs_of(q):
        return pl.ds(q * LP, LP)

    def window_of(p, q):
        if NI > 2:
            src = rwin.at[:, pl.ds(pl.multiple_of(p * F, F), 2 * F)]
            return src, rin.at[pairs_of(q)]
        src = rwin.at[:, pl.ds(pl.multiple_of((p + 1) * RIM, RIM), 3 * RIM)]
        return src, rin.at[pairs_of(q), pl.ds(pl.multiple_of((1 - p) * RIM, RIM), 3 * RIM)]

    for k in range(1, NI):
        p = lax.rem(i + k, NI)
        start(remote(*window_of(p, i), sem_r + k - 1, {"frames": at_i(p)}))
    rim_there = rx.at[pairs_of(i)]
    start(
        remote(rwin.at[:, RIM : 2 * RIM], rim_there, sem_rx, {"frames": base_prev + NI - 1}, sem_rx + i)
    )
    start(
        remote(
            rwin.at[:, NI * F : NI * F + RIM], rim_there, sem_rx + 1, {"frames": base_succ}, sem_rx + i
        )
    )
    rin[pairs_of(i)] = rwin[:, pl.ds(pl.multiple_of(i * F, F), 2 * F)]
    remote(prebf.at[:, 0:RIM], rim_r, sem_rim, {"frames": prev}).wait_recv()
    remote(prebf.at[:, RIM:F], rim_l, sem_rim + 1, {"frames": succ}).wait_recv()

    def rows_in(q):
        remote(
            rwin.at[:, 0:RIM], rx.at[pairs_of(q)], sem_rx, {"frames": prev}, sem_rx + q
        ).wait_recv()

    for k in range(NI):
        q = lax.rem(i + NI - k, NI)
        if k > 0:
            remote(*window_of(i, q), sem_r + k - 1, {"frames": at_i(q)}).wait_recv()

        @pl.when((i == 0) | (i == NI - 1))
        def _():
            rows_in(q)

        @pl.when(i == 0)
        def _():
            rin[pairs_of(q), 0:RIM] = rx[pairs_of(q)]

        @pl.when(i == NI - 1)
        def _():
            rin[pairs_of(q), RIM + F :] = rx[pairs_of(q)]

        for e in range(LP):
            m = q * LP + e
            wide[tok, m, 0:RIM] = (rim_l[m].astype(F32) + rin[m, 0:RIM].astype(F32)).astype(BF)
            wide[tok, m, RIM : RIM + F] = (pre[m] + rin[m, RIM : RIM + F].astype(F32)).astype(BF)
            wide[tok, m, RIM + F :] = (rim_r[m].astype(F32) + rin[m, RIM + F :].astype(F32)).astype(BF)
        if tok_count > 1:
            piece = wide.at[tok, pairs_of(q)]
            start(remote(piece, piece, sem_w + k, {"tok": 1 - tok}))

    fetched["wk"].wait()
    fetched["wv"].wait()

    def half_rows(t):
        return jnp.concatenate([wide[t, p] for p in range(PAIRS)], axis=1)

    mine = half_rows(tok)
    at = pl.ds(pl.multiple_of(tok * half, half), half)
    kacc[...] = dot(mine, wk[at, :])
    vacc[...] = dot(mine, wv[at, :])
    if tok_count > 1:
        other = 1 - tok
        for k in range(NI):
            q = lax.rem(i + NI - k, NI)
            piece = wide.at[other, pairs_of(q)]
            remote(piece, piece, sem_w + k, {"tok": other}).wait_recv()
        theirs = half_rows(other)
        at = pl.ds(pl.multiple_of(other * half, half), half)
        keys[...] = (kacc[...] + dot(theirs, wk[at, :])).astype(BF)
        values[...] = (vacc[...] + dot(theirs, wv[at, :])).astype(BF)
    else:
        keys[...] = kacc[...].astype(BF)
        values[...] = vacc[...].astype(BF)
    fetched["q"].wait()
    for copy in sent:
        copy.wait_send()


def reader(wide, keys, values, queries, bias, enc_hbm, out_hbm, enc, out, sem):
    tok = lax.axis_index("tok")
    for p in range(PAIRS):
        enc[:, p * 2 * HD : (p + 1) * 2 * HD] = wide[tok, p, RIM : RIM + F]
    copies = [pltpu.make_async_copy(enc, enc_hbm, sem.at[0])]
    copies[0].start()
    left = lax.broadcasted_iota(jnp.int32, (1, 2 * DHD), 1) < DHD
    for p in range(queries.shape[1] // (2 * DHD)):
        cols = slice(p * 2 * DHD, (p + 1) * 2 * DHD)
        q_pair = queries[:, cols]
        k_pair = keys[:, cols].astype(F32)
        v_pair = values[:, cols]
        both = []
        for only in (jnp.where(left, k_pair, 0.0), jnp.where(left, 0.0, k_pair)):
            scores = dot_nt(q_pair, only.astype(BF)) + bias[...]
            top = jnp.max(scores, axis=1, keepdims=True)
            raised = jnp.exp((scores - top) * DHD ** (-0.5))
            whole = 1.0 / jnp.sum(raised, axis=1, keepdims=True)
            both.append(dot(raised.astype(BF), v_pair) * whole)
        out[:, cols] = jnp.where(left, both[0], both[1]).astype(BF)
        copies.append(pltpu.make_async_copy(out.at[:, cols], out_hbm.at[:, cols], sem.at[p + 1]))
        copies[-1].start()
    for copy in copies:
        copy.wait()


def solution(mesh):
    frames = mesh.shape["frames"]
    tok_count = mesh.shape["tok"]
    ng = min(16 // NI, frames // NI)
    ny = frames // (NI * ng)
    sub = PIECE // ng
    vmem = pl.BlockSpec(memory_space=pltpu.VMEM)
    hbm = pl.BlockSpec(memory_space=pltpu.HBM)

    def local(x, b, c, log_decay, gain, key_weight, value_weight, queries, span_start, span_len):
        count, width = x.shape
        window = 2 * count
        tokens, out_width = queries.shape
        copies = 5 * (NI - 1) + 5 * (ng - 1) + 3 * (ny - 1) + 2 + 2 * NI
        wide, keys, values, held, bias = pl.pallas_call(
            functools.partial(mixer, (ny, ng, tok_count)),
            out_shape=(
                jax.ShapeDtypeStruct((tok_count, PAIRS, window, N), BF),
                jax.ShapeDtypeStruct((window, out_width), BF),
                jax.ShapeDtypeStruct((window, out_width), BF),
                jax.ShapeDtypeStruct(queries.shape, BF),
                jax.ShapeDtypeStruct((tokens, window), F32),
            ),
            in_specs=[hbm] * 10,
            out_specs=(vmem,) * 5,
            scratch_shapes=[
                pltpu.VMEM(x.shape, BF),
                pltpu.VMEM(b.shape, BF),
                pltpu.VMEM(c.shape, BF),
                pltpu.VMEM(log_decay.shape, F32),
                pltpu.SMEM(gain.shape, F32),
                pltpu.SMEM(span_start.shape, jnp.int32),
                pltpu.SMEM(span_len.shape, jnp.int32),
                pltpu.VMEM(key_weight.shape, BF),
                pltpu.VMEM(value_weight.shape, BF),
                pltpu.VMEM((2, NI, PIECE, N), BF),
                pltpu.VMEM((2, NI, PIECE, N), BF),
                pltpu.VMEM((NI,) + c.shape, BF),
                pltpu.VMEM((NI,) + log_decay.shape, F32),
                pltpu.VMEM((2, ng, sub, N), BF),
                pltpu.VMEM((2, ng, sub, N), BF),
                pltpu.VMEM((8, N), F32),
                pltpu.VMEM((ng, 8, N), F32),
                pltpu.VMEM((2, sub, N), BF),
                pltpu.VMEM((2, ny, sub, N), BF),
                pltpu.VMEM((8, N), F32),
                pltpu.VMEM((ny, 8, N), F32),
                pltpu.VMEM((2, ng, sub, N), BF),
                pltpu.VMEM((2, ng, sub, N), BF),
                pltpu.VMEM((PAIRS, count, N), F32),
                pltpu.VMEM((PAIRS, count, N), BF),
                pltpu.VMEM((PAIRS, RIM, N), BF),
                pltpu.VMEM((PAIRS, RIM, N), BF),
                pltpu.VMEM((2, NI, PIECE, N), BF),
                pltpu.VMEM((2, NI, LP, count, N), F32),
                pltpu.VMEM((NI, LP, count, N), F32),
                pltpu.VMEM((LP, 2 * RIM + NI * count, N), BF),
                pltpu.VMEM((PAIRS, window, N), BF),
                pltpu.VMEM((PAIRS, RIM, N), BF),
                pltpu.VMEM((window, out_width), F32),
                pltpu.VMEM((window, out_width), F32),
                pltpu.SemaphoreType.DMA((10,)),
                pltpu.SemaphoreType.DMA((copies,)),
                pltpu.SemaphoreType.DMA((copies,)),
            ],
            compiler_params=pltpu.CompilerParams(
                collective_id=0, has_side_effects=True, vmem_limit_bytes=24 * 2**20
            ),
        )(
            *(
                pltpu.with_memory_space_constraint(a, pltpu.HBM)
                for a in (
                    x,
                    b,
                    c,
                    log_decay,
                    gain,
                    key_weight,
                    value_weight,
                    queries,
                    span_start,
                    span_len,
                )
            )
        )
        return pl.pallas_call(
            reader,
            out_shape=(
                jax.ShapeDtypeStruct((count, width), BF),
                jax.ShapeDtypeStruct(queries.shape, BF),
            ),
            in_specs=[vmem] * 5,
            out_specs=(hbm, hbm),
            scratch_shapes=[
                pltpu.VMEM((count, width), BF),
                pltpu.VMEM(queries.shape, BF),
                pltpu.SemaphoreType.DMA((out_width // (2 * DHD) + 1,)),
            ],
            compiler_params=pltpu.CompilerParams(vmem_limit_bytes=24 * 2**20),
        )(wide, keys, values, held, bias)

    placed = (
        P(("dp", "frames"), "tok"),
        P(("dp", "frames"), None),
        P(("dp", "frames"), None),
        P(None, "tok", ("dp", "frames")),
        P("tok"),
        P(None, "tok"),
        P(None, "tok"),
        P(("dp", "frames"), "tok"),
        P(("dp", "frames")),
        P(("dp", "frames")),
    )
    return jax.shard_map(
        local,
        mesh=mesh,
        in_specs=placed,
        out_specs=(P(("dp", "frames"), "tok"), P(("dp", "frames"), "tok")),
        check_vma=False,
    )
```

```python
import functools

import jax
import jax.numpy as jnp
from jax import lax
from jax.experimental import pallas as pl
from jax.experimental.pallas import tpu as pltpu
from jax.sharding import PartitionSpec as P

DHD = 64
F = 128
RIM = 64
N = 128
HD = 64
NI = 2
PAIRS = 4
HP = 2 * PAIRS // NI
LP = PAIRS // NI
PIECE = HP * HD
MESH = pl.DeviceIdType.MESH
HIGH = lax.Precision.HIGHEST
NT = (((1,), (1,)), ((), ()))
BF = jnp.bfloat16
F32 = jnp.float32


def dot(a, b):
    return jnp.dot(a, b, preferred_element_type=F32)


def dot_nt(a, b, precision=None):
    return lax.dot_general(a, b, NT, precision=precision, preferred_element_type=F32)


def thirds(a):
    high = a.astype(BF)
    rest = a - high.astype(F32)
    mid = rest.astype(BF)
    return high, mid, (rest - mid.astype(F32)).astype(BF)


def sum_rows(parts, mask):
    both = dot(jnp.concatenate(parts, axis=0), mask.astype(BF))
    n = parts[0].shape[0]
    return both[0:n] + both[n : 2 * n] + both[2 * n : 3 * n]


def sum_cols(mask, parts):
    return functools.reduce(jnp.add, [dot_nt(mask.astype(BF), p) for p in reversed(parts)])


def tall(tile, first):
    return jnp.concatenate(
        [jnp.broadcast_to(tile[first + k : first + k + 1], (HD, N)) for k in range(HP)], axis=0
    )


def mixer(
    dims,
    x_hbm,
    b_hbm,
    c_hbm,
    ld_hbm,
    gain_hbm,
    wk_hbm,
    wv_hbm,
    q_hbm,
    start_hbm,
    len_hbm,
    wide,
    keys,
    values,
    q_out,
    bias,
    xv,
    bv,
    cv,
    ldv,
    gain,
    starts,
    lens,
    wk,
    wv,
    lsend,
    lrecv,
    crx,
    ldrx,
    gsend,
    grecv,
    gtsend,
    gtrecv,
    ysend,
    yrecv,
    ytsend,
    ytrecv,
    csend,
    crecv,
    pre,
    prebf,
    rim_l,
    rim_r,
    within,
    grown,
    local_part,
    rwin,
    rin,
    rx,
    kacc,
    vacc,
    hsem,
    ssem,
    rsem,
):
    ny, ng, tok_count = dims
    heads = ldv.shape[1]
    half = xv.shape[1]
    sub = PIECE // ng
    frames = ny * ng * NI
    row = ng * NI
    me = lax.axis_index("frames")
    tok = lax.axis_index("tok")
    y = me // row
    g = lax.rem(me // NI, ng)
    i = lax.rem(me, NI)
    base = me - i

    def at_i(p):
        return base + p

    def at_g(p):
        return me + (p - g) * NI

    def at_y(p):
        return me + (p - y) * row

    prev = lax.rem(me + frames - 1, frames)
    succ = lax.rem(me + 1, frames)
    base_prev = lax.rem(base + frames - NI, frames)
    base_succ = lax.rem(base + NI, frames)

    fetched = {}

    def fetch(name, src, dst):
        copy = pltpu.make_async_copy(src, dst, hsem.at[len(fetched)])
        copy.start()
        fetched[name] = copy

    fetch("ld", ld_hbm, ldv)
    fetch("x", x_hbm, xv)
    fetch("b", b_hbm, bv)
    fetch("c", c_hbm, cv)
    fetch("gain", gain_hbm, gain)
    fetch("start", start_hbm, starts)
    fetch("len", len_hbm, lens)
    fetch("wk", wk_hbm, wk)
    fetch("wv", wv_hbm, wv)
    fetch("q", q_hbm, q_out)

    barrier = pltpu.get_barrier_semaphore()

    def greet(**device):
        pl.semaphore_signal(barrier, inc=1, device_id=device, device_id_type=MESH)

    greeted = 0
    for own, count, place in ((i, NI, at_i), (g, ng, at_g), (y, ny, at_y)):
        for k in range(1, count):
            greet(frames=place(lax.rem(own + k, count)))
            greeted += 1
    greet(frames=prev)
    greet(frames=succ)
    greeted += 2
    if tok_count > 1:
        greet(tok=1 - tok)
        greeted += 1

    @pl.when(i == 0)
    def _():
        for k in range(NI):
            greet(frames=base_prev + k)

    @pl.when(i == NI - 1)
    def _():
        for k in range(NI):
            greet(frames=base_succ + k)

    greeted += 2

    sent = []
    taken = [0]

    def take(n):
        first = taken[0]
        taken[0] += n
        return first

    def remote(src, dst, index, device, landing=None):
        return pltpu.make_async_remote_copy(
            src_ref=src,
            dst_ref=dst,
            send_sem=ssem.at[index],
            recv_sem=rsem.at[index if landing is None else landing],
            device_id=device,
            device_id_type=MESH,
        )

    def start(copy):
        copy.start()
        sent.append(copy)

    def far_first(count):
        return sorted(range(1, count), key=lambda k: -min(k, count - k))

    def scatter(own, count, place, src, dst, first):
        for k in far_first(count):
            p = lax.rem(own + k, count)
            start(remote(src.at[p], dst.at[own], first + k - 1, {"frames": place(p)}))

    def share(own, count, place, src, dst, first):
        for k in far_first(count):
            p = lax.rem(own + k, count)
            start(remote(src, dst.at[own], first + k - 1, {"frames": place(p)}))

    def arrive(own, count, place, src, dst, first):
        for k in range(1, count):
            q = lax.rem(own + count - k, count)
            remote(src, dst.at[q], first + k - 1, {"frames": place(q)}).wait_recv()

    sem_ld, sem_c = take(NI - 1), take(NI - 1)
    sem_l = (take(NI - 1), take(NI - 1))
    sem_gt = take(ng - 1)
    sem_g = (take(ng - 1), take(ng - 1))
    sem_yt = take(ny - 1)
    sem_y = (take(ny - 1), take(ny - 1))
    sem_b = (take(ng - 1), take(ng - 1))
    sem_rim = take(2)
    sem_r = take(NI - 1)
    sem_rx = take(NI)
    sem_w = take(NI)

    pl.semaphore_wait(barrier, greeted)
    share(i, NI, at_i, ld_hbm, ldrx, sem_ld)
    share(i, NI, at_i, c_hbm, crx, sem_c)

    r_id = lax.broadcasted_iota(jnp.int32, (F, F), 0)
    s_id = lax.broadcasted_iota(jnp.int32, (F, F), 1)
    fetched["ld"].wait()
    parts_f = thirds(ldv[0])
    to_end = [jnp.exp(sum_rows(parts_f, (r_id > s_id).astype(F32))), None]
    fetched["x"].wait()
    fetched["b"].wait()
    turned = []
    row_b = None
    for d in range(2):
        if d == 1:
            parts_b = thirds(ldv[1])
            row_b = sum_rows(parts_b, (r_id < s_id).astype(F32))
            to_end[1] = jnp.exp(row_b)
        for p in range(NI):
            if d == 0:
                turned.append(xv[:, p * PIECE : (p + 1) * PIECE].astype(F32).T)
            scaled = (turned[p] * tall(to_end[d], p * HP)).astype(BF)
            lsend[d, p] = dot(scaled, bv[...]).astype(BF)

            @pl.when(i != p)
            def _():
                slot = sem_l[d] + lax.rem(p - i + NI, NI) - 1
                remote(lsend.at[d, p], lrecv.at[d, i], slot, {"frames": at_i(p)}).start()

        for k in range(1, NI):
            p = lax.rem(i + k, NI)
            sent.append(remote(lsend.at[d, p], lrecv.at[d, i], sem_l[d] + k - 1, {"frames": at_i(p)}))
        lrecv[d, pl.ds(i, 1)] = lsend[d, pl.ds(i, 1)]

    ldrx[pl.ds(i, 1)] = ldv[...][None]
    rows, tots, decays = [], [], []
    state_of = [None, None]

    def group_states(d):
        if d == 0:
            arrive(i, NI, at_i, ld_hbm, ldrx, sem_ld)
            for j in range(NI):
                picked = jnp.concatenate(
                    [
                        functools.reduce(
                            lambda a, p: jnp.where(i == p, ldrx[j, e, HP * p : HP * p + HP, :], a),
                            range(1, NI),
                            ldrx[j, e, 0:HP, :],
                        )
                        for e in range(2)
                    ],
                    axis=0,
                )
                rows.append(picked)
                tots.append(
                    jnp.broadcast_to(jnp.sum(picked, axis=1, keepdims=True), (2 * HP, N))
                )
                decays.append(jnp.exp(tots[j]))
            gtsend[0 : 2 * HP] = functools.reduce(jnp.add, tots)
            if 2 * HP < 8:
                gtsend[2 * HP :] = jnp.zeros((8 - 2 * HP, N), F32)
            share(g, ng, at_g, gtsend, gtrecv, sem_gt)
            gtrecv[g] = gtsend[...]
        arrive(i, NI, at_i, lsend.at[d, 0], lrecv.at[d], sem_l[d])
        state = jnp.zeros((PIECE, N), F32)
        for j in range(NI) if d == 0 else reversed(range(NI)):
            within[d, j] = state.astype(BF)
            state = tall(decays[j], d * HP) * state + lrecv[d, j].astype(F32)
        for k in range(ng):
            gsend[d, k] = state[k * sub : (k + 1) * sub].astype(BF)
        scatter(g, ng, at_g, gsend.at[d], grecv.at[d], sem_g[d])
        grecv[d, pl.ds(g, 1)] = gsend[d, pl.ds(g, 1)]

    group_tots = [[], []]
    into = [[None] * ng, [None] * ng]
    ahead = [[None] * ng, [None] * ng]

    def row_states(d):
        if d == 0:
            arrive(g, ng, at_g, gtsend, gtrecv, sem_gt)
            head = (g * sub) // HD
            for k in range(ng):
                for e in range(2):
                    one = gtrecv[k, e * HP : e * HP + 1, :]
                    for h in range(1, HP):
                        one = jnp.where(head == h, gtrecv[k, e * HP + h : e * HP + h + 1, :], one)
                    group_tots[e].append(one)
            if ny > 1:
                ytsend[...] = jnp.concatenate(
                    [functools.reduce(jnp.add, group_tots[e]) for e in range(2)]
                    + [jnp.zeros((6, N), F32)],
                    axis=0,
                )
                share(y, ny, at_y, ytsend, ytrecv, sem_yt)
                ytrecv[y] = ytsend[...]
        arrive(g, ng, at_g, gsend.at[d, 0], grecv.at[d], sem_g[d])
        state, total = jnp.zeros((sub, N), F32), jnp.zeros((1, N), F32)
        for k in range(ng) if d == 0 else reversed(range(ng)):
            into[d][k], ahead[d][k] = state, jnp.exp(total)
            state = jnp.exp(group_tots[d][k]) * state + grecv[d, k].astype(F32)
            total = total + group_tots[d][k]
        if ny > 1:
            ysend[d] = state.astype(BF)
            share(y, ny, at_y, ysend.at[d], yrecv.at[d], sem_y[d])
            yrecv[d, pl.ds(y, 1)] = ysend[d][None]

    def entering(d):
        enter = jnp.zeros((sub, N), F32)
        if ny > 1:
            if d == 0:
                arrive(y, ny, at_y, ytsend, ytrecv, sem_yt)
            arrive(y, ny, at_y, ysend.at[d], yrecv.at[d], sem_y[d])
            state = jnp.zeros((sub, N), F32)
            for k in range(ny) if d == 0 else reversed(range(ny)):
                enter = jnp.where(y == k, state, enter)
                state = jnp.exp(ytrecv[k, d : d + 1, :]) * state + yrecv[d, k].astype(F32)
        for k in range(ng):
            csend[d, k] = (into[d][k] + ahead[d][k] * enter).astype(BF)
        crecv[d, pl.ds(g, 1)] = csend[d, pl.ds(g, 1)]
        for p in early:
            send_back(d, p)

    early = [p for p in (0, ng - 1, 1) if p < ng][: max(1, ng - 1)]
    late = [p for p in [2, *range(3, ng - 1)] if p < ng and p not in early]

    def send_back(d, p):
        @pl.when(g != p)
        def _():
            slot = sem_b[d] + lax.rem(p - g + ng, ng) - 1
            remote(csend.at[d, p], crecv.at[d, g], slot, {"frames": at_g(p)}).start()

    group_states(0)
    group_states(1)

    fetched["c"].wait()
    fetched["gain"].wait()
    crx[pl.ds(i, 1)] = cv[...][None]
    gram = dot_nt(cv[...], bv[...])
    gram = jnp.where(r_id == s_id, 2.0 * gram, gram)
    lower = s_id <= r_id
    row_f = sum_rows(parts_f, (r_id <= s_id).astype(F32))
    col_f = sum_cols(lower.astype(F32), parts_f)
    col_b = sum_cols((s_id < r_id).astype(F32), parts_b)
    left = s_id < HD
    for p in range(PAIRS):
        x_pair = xv[:, p * 2 * HD : (p + 1) * 2 * HD].astype(F32)
        weights = []
        for h in (2 * p, 2 * p + 1):
            at_f = jnp.broadcast_to(col_f[:, h : h + 1], (F, F))
            at_b = jnp.broadcast_to(col_b[:, h : h + 1], (F, F))
            exponent = jnp.where(lower, at_f - row_f[h : h + 1], row_b[h : h + 1] - at_b)
            weights.append((jnp.exp(exponent) * gram).astype(BF))
        apart = jnp.concatenate(
            [jnp.where(left, x_pair, 0.0), jnp.where(left, 0.0, x_pair)], axis=0
        ).astype(BF)
        intra = dot(jnp.concatenate(weights, axis=1), apart)
        inside = intra + jnp.where(left[0:1], gain[2 * p], gain[2 * p + 1]) * x_pair
        pre[p] = inside
        prebf[p] = inside.astype(BF)
    rims = (
        remote(prebf.at[:, 0:RIM], rim_r, sem_rim, {"frames": prev}),
        remote(prebf.at[:, RIM:F], rim_l, sem_rim + 1, {"frames": succ}),
    )
    for copy in rims:
        start(copy)

    row_states(0)
    row_states(1)

    arrive(i, NI, at_i, c_hbm, crx, sem_c)
    picked_f = jnp.concatenate([r[0:HP] for r in rows], axis=0)
    picked_b = jnp.concatenate([r[HP : 2 * HP] for r in rows], axis=0)
    cols = (
        sum_cols(lower.astype(F32), thirds(picked_f)),
        sum_cols((s_id >= r_id).astype(F32), thirds(picked_b)),
    )

    def group_terms(d):
        total = jnp.zeros((2 * HP, N), F32)
        for j in range(NI) if d == 0 else reversed(range(NI)):
            for e in range(LP):
                at = [
                    jnp.broadcast_to(cols[d][:, HP * j + 2 * e + h : HP * j + 2 * e + h + 1], (F, F))
                    for h in range(2)
                ]
                spread = jnp.exp(jnp.where(left, at[0], at[1]))
                h = d * HP + 2 * e
                lead = jnp.exp(jnp.where(left[0:1], total[h : h + 1], total[h + 1 : h + 2]))
                grown[d, j, e] = spread * lead
                part = spread * dot_nt(crx[j], within[d, j, e * N : (e + 1) * N])
                local_part[j, e] = part if d == 0 else local_part[j, e] + part
            total = total + tots[j]

    group_terms(0)
    group_terms(1)
    entering(0)
    entering(1)
    for p in late:
        for d in range(2):
            send_back(d, p)
    for d in range(2):
        for k in range(1, ng):
            p = lax.rem(g + k, ng)
            sent.append(remote(csend.at[d, p], crecv.at[d, g], sem_b[d] + k - 1, {"frames": at_g(p)}))

    fetched["start"].wait()
    fetched["len"].wait()
    groups = starts.shape[0]
    tokens, window = bias.shape
    per_group = tokens // groups
    place = lax.broadcasted_iota(jnp.int32, (per_group, window), 1) + (me * F - RIM)
    for k in range(groups):
        allowed = (place >= starts[k]) & (place < starts[k] + lens[k])
        bias[k * per_group : (k + 1) * per_group, :] = jnp.where(allowed, 0.0, -jnp.inf)
    rwin[:, 0:RIM] = jnp.zeros((LP, RIM, N), BF)
    rwin[:, RIM + NI * F :] = jnp.zeros((LP, RIM, N), BF)

    for d in range(2):
        arrive(g, ng, at_g, csend.at[d, 0], crecv.at[d], sem_b[d])
        carried = crecv[d].reshape(PIECE, N)
        for j in range(NI):
            for e in range(LP):
                part = local_part[j, e] + grown[d, j, e] * dot_nt(crx[j], carried[e * N : (e + 1) * N])
                if d == 0:
                    local_part[j, e] = part
                else:
                    rwin[e, RIM + j * F : RIM + (j + 1) * F] = part.astype(BF)

    def pairs_of(q):
        return pl.ds(q * LP, LP)

    def window_of(p, q):
        if NI > 2:
            src = rwin.at[:, pl.ds(pl.multiple_of(p * F, F), 2 * F)]
            return src, rin.at[pairs_of(q)]
        src = rwin.at[:, pl.ds(pl.multiple_of((p + 1) * RIM, RIM), 3 * RIM)]
        return src, rin.at[pairs_of(q), pl.ds(pl.multiple_of((1 - p) * RIM, RIM), 3 * RIM)]

    rim_there = rx.at[pairs_of(i)]
    start(
        remote(rwin.at[:, RIM : 2 * RIM], rim_there, sem_rx, {"frames": base_prev + NI - 1}, sem_rx + i)
    )
    start(
        remote(
            rwin.at[:, NI * F : NI * F + RIM], rim_there, sem_rx + 1, {"frames": base_succ}, sem_rx + i
        )
    )
    for k in range(1, NI):
        p = lax.rem(i + k, NI)
        start(remote(*window_of(p, i), sem_r + k - 1, {"frames": at_i(p)}))
    rin[pairs_of(i)] = rwin[:, pl.ds(pl.multiple_of(i * F, F), 2 * F)]
    remote(prebf.at[:, 0:RIM], rim_r, sem_rim, {"frames": prev}).wait_recv()
    remote(prebf.at[:, RIM:F], rim_l, sem_rim + 1, {"frames": succ}).wait_recv()

    def rows_in(q):
        remote(
            rwin.at[:, 0:RIM], rx.at[pairs_of(q)], sem_rx, {"frames": prev}, sem_rx + q
        ).wait_recv()

    for k in range(NI):
        q = lax.rem(i + NI - k, NI)
        if k > 0:
            remote(*window_of(i, q), sem_r + k - 1, {"frames": at_i(q)}).wait_recv()

        @pl.when((i == 0) | (i == NI - 1))
        def _():
            rows_in(q)

        @pl.when(i == 0)
        def _():
            rin[pairs_of(q), 0:RIM] = rx[pairs_of(q)]

        @pl.when(i == NI - 1)
        def _():
            rin[pairs_of(q), RIM + F :] = rx[pairs_of(q)]

        for e in range(LP):
            m = q * LP + e
            wide[tok, m, 0:RIM] = (rim_l[m].astype(F32) + rin[m, 0:RIM].astype(F32)).astype(BF)
            wide[tok, m, RIM : RIM + F] = (pre[m] + rin[m, RIM : RIM + F].astype(F32)).astype(BF)
            wide[tok, m, RIM + F :] = (rim_r[m].astype(F32) + rin[m, RIM + F :].astype(F32)).astype(BF)
        if tok_count > 1:
            piece = wide.at[tok, pairs_of(q)]
            start(remote(piece, piece, sem_w + k, {"tok": 1 - tok}))

    fetched["wk"].wait()
    fetched["wv"].wait()

    def half_rows(t):
        return jnp.concatenate([wide[t, p] for p in range(PAIRS)], axis=1)

    mine = half_rows(tok)
    at = pl.ds(pl.multiple_of(tok * half, half), half)
    kacc[...] = dot(mine, wk[at, :])
    vacc[...] = dot(mine, wv[at, :])
    if tok_count > 1:
        other = 1 - tok
        for k in range(NI):
            q = lax.rem(i + NI - k, NI)
            piece = wide.at[other, pairs_of(q)]
            remote(piece, piece, sem_w + k, {"tok": other}).wait_recv()
        theirs = half_rows(other)
        at = pl.ds(pl.multiple_of(other * half, half), half)
        keys[...] = (kacc[...] + dot(theirs, wk[at, :])).astype(BF)
        values[...] = (vacc[...] + dot(theirs, wv[at, :])).astype(BF)
    else:
        keys[...] = kacc[...].astype(BF)
        values[...] = vacc[...].astype(BF)
    fetched["q"].wait()
    for copy in sent:
        copy.wait_send()


def reader(wide, keys, values, queries, bias, enc_hbm, out_hbm, enc, out, sem):
    tok = lax.axis_index("tok")
    for p in range(PAIRS):
        enc[:, p * 2 * HD : (p + 1) * 2 * HD] = wide[tok, p, RIM : RIM + F]
    copies = [pltpu.make_async_copy(enc, enc_hbm, sem.at[0])]
    copies[0].start()
    left = lax.broadcasted_iota(jnp.int32, (1, 2 * DHD), 1) < DHD
    for p in range(queries.shape[1] // (2 * DHD)):
        cols = slice(p * 2 * DHD, (p + 1) * 2 * DHD)
        q_pair = queries[:, cols]
        k_pair = keys[:, cols].astype(F32)
        v_pair = values[:, cols]
        both = []
        for only in (jnp.where(left, k_pair, 0.0), jnp.where(left, 0.0, k_pair)):
            scores = dot_nt(q_pair, only.astype(BF)) + bias[...]
            top = jnp.max(scores, axis=1, keepdims=True)
            raised = jnp.exp((scores - top) * DHD ** (-0.5))
            whole = 1.0 / jnp.sum(raised, axis=1, keepdims=True)
            both.append(dot(raised.astype(BF), v_pair) * whole)
        out[:, cols] = jnp.where(left, both[0], both[1]).astype(BF)
        copies.append(pltpu.make_async_copy(out.at[:, cols], out_hbm.at[:, cols], sem.at[p + 1]))
        copies[-1].start()
    for copy in copies:
        copy.wait()


def solution(mesh):
    frames = mesh.shape["frames"]
    tok_count = mesh.shape["tok"]
    ng = min(16 // NI, frames // NI)
    ny = frames // (NI * ng)
    sub = PIECE // ng
    vmem = pl.BlockSpec(memory_space=pltpu.VMEM)
    hbm = pl.BlockSpec(memory_space=pltpu.HBM)

    def local(x, b, c, log_decay, gain, key_weight, value_weight, queries, span_start, span_len):
        count, width = x.shape
        window = 2 * count
        tokens, out_width = queries.shape
        copies = 5 * (NI - 1) + 5 * (ng - 1) + 3 * (ny - 1) + 2 + 2 * NI
        wide, keys, values, held, bias = pl.pallas_call(
            functools.partial(mixer, (ny, ng, tok_count)),
            out_shape=(
                jax.ShapeDtypeStruct((tok_count, PAIRS, window, N), BF),
                jax.ShapeDtypeStruct((window, out_width), BF),
                jax.ShapeDtypeStruct((window, out_width), BF),
                jax.ShapeDtypeStruct(queries.shape, BF),
                jax.ShapeDtypeStruct((tokens, window), F32),
            ),
            in_specs=[hbm] * 10,
            out_specs=(vmem,) * 5,
            scratch_shapes=[
                pltpu.VMEM(x.shape, BF),
                pltpu.VMEM(b.shape, BF),
                pltpu.VMEM(c.shape, BF),
                pltpu.VMEM(log_decay.shape, F32),
                pltpu.SMEM(gain.shape, F32),
                pltpu.SMEM(span_start.shape, jnp.int32),
                pltpu.SMEM(span_len.shape, jnp.int32),
                pltpu.VMEM(key_weight.shape, BF),
                pltpu.VMEM(value_weight.shape, BF),
                pltpu.VMEM((2, NI, PIECE, N), BF),
                pltpu.VMEM((2, NI, PIECE, N), BF),
                pltpu.VMEM((NI,) + c.shape, BF),
                pltpu.VMEM((NI,) + log_decay.shape, F32),
                pltpu.VMEM((2, ng, sub, N), BF),
                pltpu.VMEM((2, ng, sub, N), BF),
                pltpu.VMEM((8, N), F32),
                pltpu.VMEM((ng, 8, N), F32),
                pltpu.VMEM((2, sub, N), BF),
                pltpu.VMEM((2, ny, sub, N), BF),
                pltpu.VMEM((8, N), F32),
                pltpu.VMEM((ny, 8, N), F32),
                pltpu.VMEM((2, ng, sub, N), BF),
                pltpu.VMEM((2, ng, sub, N), BF),
                pltpu.VMEM((PAIRS, count, N), F32),
                pltpu.VMEM((PAIRS, count, N), BF),
                pltpu.VMEM((PAIRS, RIM, N), BF),
                pltpu.VMEM((PAIRS, RIM, N), BF),
                pltpu.VMEM((2, NI, PIECE, N), BF),
                pltpu.VMEM((2, NI, LP, count, N), F32),
                pltpu.VMEM((NI, LP, count, N), F32),
                pltpu.VMEM((LP, 2 * RIM + NI * count, N), BF),
                pltpu.VMEM((PAIRS, window, N), BF),
                pltpu.VMEM((PAIRS, RIM, N), BF),
                pltpu.VMEM((window, out_width), F32),
                pltpu.VMEM((window, out_width), F32),
                pltpu.SemaphoreType.DMA((10,)),
                pltpu.SemaphoreType.DMA((copies,)),
                pltpu.SemaphoreType.DMA((copies,)),
            ],
            compiler_params=pltpu.CompilerParams(
                collective_id=0, has_side_effects=True, vmem_limit_bytes=24 * 2**20
            ),
        )(
            *(
                pltpu.with_memory_space_constraint(a, pltpu.HBM)
                for a in (
                    x,
                    b,
                    c,
                    log_decay,
                    gain,
                    key_weight,
                    value_weight,
                    queries,
                    span_start,
                    span_len,
                )
            )
        )
        return pl.pallas_call(
            reader,
            out_shape=(
                jax.ShapeDtypeStruct((count, width), BF),
                jax.ShapeDtypeStruct(queries.shape, BF),
            ),
            in_specs=[vmem] * 5,
            out_specs=(hbm, hbm),
            scratch_shapes=[
                pltpu.VMEM((count, width), BF),
                pltpu.VMEM(queries.shape, BF),
                pltpu.SemaphoreType.DMA((out_width // (2 * DHD) + 1,)),
            ],
            compiler_params=pltpu.CompilerParams(vmem_limit_bytes=24 * 2**20),
        )(wide, keys, values, held, bias)

    placed = (
        P(("dp", "frames"), "tok"),
        P(("dp", "frames"), None),
        P(("dp", "frames"), None),
        P(None, "tok", ("dp", "frames")),
        P("tok"),
        P(None, "tok"),
        P(None, "tok"),
        P(("dp", "frames"), "tok"),
        P(("dp", "frames")),
        P(("dp", "frames")),
    )
    return jax.shard_map(
        local,
        mesh=mesh,
        in_specs=placed,
        out_specs=(P(("dp", "frames"), "tok"), P(("dp", "frames"), "tok")),
        check_vma=False,
    )
```

```python
import functools

import jax
import jax.numpy as jnp
from jax import lax
from jax.experimental import pallas as pl
from jax.experimental.pallas import tpu as pltpu
from jax.sharding import PartitionSpec as P

DHD = 64
F = 128
RIM = 64
N = 128
HD = 64
NI = 2
PAIRS = 4
HP = 2 * PAIRS // NI
LP = PAIRS // NI
PIECE = HP * HD
MESH = pl.DeviceIdType.MESH
HIGH = lax.Precision.HIGHEST
NT = (((1,), (1,)), ((), ()))
BF = jnp.bfloat16
F32 = jnp.float32


def dot(a, b):
    return jnp.dot(a, b, preferred_element_type=F32)


def dot_nt(a, b, precision=None):
    return lax.dot_general(a, b, NT, precision=precision, preferred_element_type=F32)


def thirds(a):
    high = a.astype(BF)
    rest = a - high.astype(F32)
    mid = rest.astype(BF)
    return high, mid, (rest - mid.astype(F32)).astype(BF)


def sum_rows(parts, mask):
    both = dot(jnp.concatenate(parts, axis=0), mask.astype(BF))
    n = parts[0].shape[0]
    return both[0:n] + both[n : 2 * n] + both[2 * n : 3 * n]


def sum_cols(mask, parts):
    return functools.reduce(jnp.add, [dot_nt(mask.astype(BF), p) for p in reversed(parts)])


def tall(tile, first):
    return jnp.concatenate(
        [jnp.broadcast_to(tile[first + k : first + k + 1], (HD, N)) for k in range(HP)], axis=0
    )


def mixer(
    dims,
    x_hbm,
    b_hbm,
    c_hbm,
    ld_hbm,
    gain_hbm,
    wk_hbm,
    wv_hbm,
    q_hbm,
    start_hbm,
    len_hbm,
    wide,
    keys,
    values,
    q_out,
    bias,
    xv,
    bv,
    cv,
    ldv,
    gain,
    starts,
    lens,
    wk,
    wv,
    lsend,
    lrecv,
    crx,
    ldrx,
    gsend,
    grecv,
    gtsend,
    gtrecv,
    ysend,
    yrecv,
    ytsend,
    ytrecv,
    csend,
    crecv,
    pre,
    prebf,
    rim_l,
    rim_r,
    within,
    grown,
    local_part,
    rwin,
    rin,
    rx,
    kacc,
    vacc,
    hsem,
    ssem,
    rsem,
):
    ny, ng, tok_count = dims
    heads = ldv.shape[1]
    half = xv.shape[1]
    sub = PIECE // ng
    frames = ny * ng * NI
    row = ng * NI
    me = lax.axis_index("frames")
    tok = lax.axis_index("tok")
    y = me // row
    g = lax.rem(me // NI, ng)
    i = lax.rem(me, NI)
    base = me - i

    def at_i(p):
        return base + p

    def at_g(p):
        return me + (p - g) * NI

    def at_y(p):
        return me + (p - y) * row

    prev = lax.rem(me + frames - 1, frames)
    succ = lax.rem(me + 1, frames)
    base_prev = lax.rem(base + frames - NI, frames)
    base_succ = lax.rem(base + NI, frames)

    fetched = {}

    def fetch(name, src, dst):
        copy = pltpu.make_async_copy(src, dst, hsem.at[len(fetched)])
        copy.start()
        fetched[name] = copy

    fetch("ld", ld_hbm, ldv)
    fetch("x", x_hbm, xv)
    fetch("b", b_hbm, bv)
    fetch("c", c_hbm, cv)
    fetch("gain", gain_hbm, gain)
    fetch("start", start_hbm, starts)
    fetch("len", len_hbm, lens)
    fetch("wk", wk_hbm, wk)
    fetch("wv", wv_hbm, wv)
    fetch("q", q_hbm, q_out)

    barrier = pltpu.get_barrier_semaphore()

    def greet(**device):
        pl.semaphore_signal(barrier, inc=1, device_id=device, device_id_type=MESH)

    greeted = 0
    for own, count, place in ((i, NI, at_i), (g, ng, at_g), (y, ny, at_y)):
        for k in range(1, count):
            greet(frames=place(lax.rem(own + k, count)))
            greeted += 1
    greet(frames=prev)
    greet(frames=succ)
    greeted += 2
    if tok_count > 1:
        greet(tok=1 - tok)
        greeted += 1

    @pl.when(i == 0)
    def _():
        for k in range(NI):
            greet(frames=base_prev + k)

    @pl.when(i == NI - 1)
    def _():
        for k in range(NI):
            greet(frames=base_succ + k)

    greeted += 2

    sent = []
    taken = [0]

    def take(n):
        first = taken[0]
        taken[0] += n
        return first

    def remote(src, dst, index, device, landing=None):
        return pltpu.make_async_remote_copy(
            src_ref=src,
            dst_ref=dst,
            send_sem=ssem.at[index],
            recv_sem=rsem.at[index if landing is None else landing],
            device_id=device,
            device_id_type=MESH,
        )

    def start(copy):
        copy.start()
        sent.append(copy)

    def far_first(count):
        return sorted(range(1, count), key=lambda k: -min(k, count - k))

    def all_of(dst, count):
        return dst.at[pl.ds(0, count - 1)]

    def scatter(own, count, place, src, dst, index):
        for k in far_first(count):
            p = lax.rem(own + k, count)
            remote(src.at[p], dst.at[own], index, {"frames": place(p)}).start()
        sent.append(remote(all_of(dst, count), all_of(dst, count), index, {"frames": prev}))

    def share(own, count, place, src, dst, index):
        for k in far_first(count):
            p = lax.rem(own + k, count)
            remote(src, dst.at[own], index, {"frames": place(p)}).start()
        sent.append(remote(all_of(dst, count), all_of(dst, count), index, {"frames": prev}))

    def arrive(count, dst, index):
        remote(all_of(dst, count), all_of(dst, count), index, {"frames": prev}).wait_recv()

    sem_ld, sem_c, sem_gt, sem_yt = take(1), take(1), take(1), take(1)
    sem_l, sem_g, sem_y, sem_b = [(take(1), take(1)) for _ in range(4)]
    sem_rim = take(2)
    sem_r = take(NI - 1)
    sem_rx = take(NI)
    sem_w = take(NI)

    pl.semaphore_wait(barrier, greeted)
    share(i, NI, at_i, ld_hbm, ldrx, sem_ld)
    share(i, NI, at_i, c_hbm, crx, sem_c)

    r_id = lax.broadcasted_iota(jnp.int32, (F, F), 0)
    s_id = lax.broadcasted_iota(jnp.int32, (F, F), 1)
    fetched["ld"].wait()
    parts_f = thirds(ldv[0])
    to_end = [jnp.exp(sum_rows(parts_f, (r_id > s_id).astype(F32))), None]
    fetched["x"].wait()
    fetched["b"].wait()
    turned = []
    row_b = None
    for d in range(2):
        if d == 1:
            parts_b = thirds(ldv[1])
            row_b = sum_rows(parts_b, (r_id < s_id).astype(F32))
            to_end[1] = jnp.exp(row_b)
        for p in range(NI):
            if d == 0:
                turned.append(xv[:, p * PIECE : (p + 1) * PIECE].astype(F32).T)
            scaled = (turned[p] * tall(to_end[d], p * HP)).astype(BF)
            lsend[d, p] = dot(scaled, bv[...]).astype(BF)

            @pl.when(i != p)
            def _():
                remote(lsend.at[d, p], lrecv.at[d, i], sem_l[d], {"frames": at_i(p)}).start()

        ours = all_of(lrecv.at[d], NI)
        sent.append(remote(ours, ours, sem_l[d], {"frames": prev}))
        lrecv[d, pl.ds(i, 1)] = lsend[d, pl.ds(i, 1)]

    ldrx[pl.ds(i, 1)] = ldv[...][None]
    rows, tots, decays = [], [], []
    state_of = [None, None]

    def group_states(d):
        if d == 0:
            arrive(NI, ldrx, sem_ld)
            for j in range(NI):
                picked = jnp.concatenate(
                    [
                        functools.reduce(
                            lambda a, p: jnp.where(i == p, ldrx[j, e, HP * p : HP * p + HP, :], a),
                            range(1, NI),
                            ldrx[j, e, 0:HP, :],
                        )
                        for e in range(2)
                    ],
                    axis=0,
                )
                rows.append(picked)
                tots.append(
                    jnp.broadcast_to(jnp.sum(picked, axis=1, keepdims=True), (2 * HP, N))
                )
                decays.append(jnp.exp(tots[j]))
            gtsend[0 : 2 * HP] = functools.reduce(jnp.add, tots)
            if 2 * HP < 8:
                gtsend[2 * HP :] = jnp.zeros((8 - 2 * HP, N), F32)
            share(g, ng, at_g, gtsend, gtrecv, sem_gt)
            gtrecv[g] = gtsend[...]
        arrive(NI, lrecv.at[d], sem_l[d])
        state = jnp.zeros((PIECE, N), F32)
        for j in range(NI) if d == 0 else reversed(range(NI)):
            within[d, j] = state.astype(BF)
            state = tall(decays[j], d * HP) * state + lrecv[d, j].astype(F32)
        for k in range(ng):
            gsend[d, k] = state[k * sub : (k + 1) * sub].astype(BF)
        scatter(g, ng, at_g, gsend.at[d], grecv.at[d], sem_g[d])
        grecv[d, pl.ds(g, 1)] = gsend[d, pl.ds(g, 1)]

    group_tots = [[], []]
    into = [[None] * ng, [None] * ng]
    ahead = [[None] * ng, [None] * ng]

    def row_states(d):
        if d == 0:
            arrive(ng, gtrecv, sem_gt)
            head = (g * sub) // HD
            for k in range(ng):
                for e in range(2):
                    one = gtrecv[k, e * HP : e * HP + 1, :]
                    for h in range(1, HP):
                        one = jnp.where(head == h, gtrecv[k, e * HP + h : e * HP + h + 1, :], one)
                    group_tots[e].append(one)
            if ny > 1:
                ytsend[...] = jnp.concatenate(
                    [functools.reduce(jnp.add, group_tots[e]) for e in range(2)]
                    + [jnp.zeros((6, N), F32)],
                    axis=0,
                )
                share(y, ny, at_y, ytsend, ytrecv, sem_yt)
                ytrecv[y] = ytsend[...]
        arrive(ng, grecv.at[d], sem_g[d])
        state, total = jnp.zeros((sub, N), F32), jnp.zeros((1, N), F32)
        for k in range(ng) if d == 0 else reversed(range(ng)):
            into[d][k], ahead[d][k] = state, jnp.exp(total)
            state = jnp.exp(group_tots[d][k]) * state + grecv[d, k].astype(F32)
            total = total + group_tots[d][k]
        if ny > 1:
            ysend[d] = state.astype(BF)
            share(y, ny, at_y, ysend.at[d], yrecv.at[d], sem_y[d])
            yrecv[d, pl.ds(y, 1)] = ysend[d][None]

    def entering(d):
        enter = jnp.zeros((sub, N), F32)
        if ny > 1:
            if d == 0:
                arrive(ny, ytrecv, sem_yt)
            arrive(ny, yrecv.at[d], sem_y[d])
            state = jnp.zeros((sub, N), F32)
            for k in range(ny) if d == 0 else reversed(range(ny)):
                enter = jnp.where(y == k, state, enter)
                state = jnp.exp(ytrecv[k, d : d + 1, :]) * state + yrecv[d, k].astype(F32)
        for k in range(ng):
            csend[d, k] = (into[d][k] + ahead[d][k] * enter).astype(BF)
        crecv[d, pl.ds(g, 1)] = csend[d, pl.ds(g, 1)]
        for p in early:
            send_back(d, p)

    early = [p for p in (0, ng - 1, 1) if p < ng][: max(1, ng - 1)]
    late = [p for p in [2, *range(3, ng - 1)] if p < ng and p not in early]

    def send_back(d, p):
        @pl.when(g != p)
        def _():
            remote(csend.at[d, p], crecv.at[d, g], sem_b[d], {"frames": at_g(p)}).start()

    group_states(0)
    group_states(1)

    fetched["c"].wait()
    fetched["gain"].wait()
    crx[pl.ds(i, 1)] = cv[...][None]
    gram = dot_nt(cv[...], bv[...])
    gram = jnp.where(r_id == s_id, 2.0 * gram, gram)
    lower = s_id <= r_id
    row_f = sum_rows(parts_f, (r_id <= s_id).astype(F32))
    col_f = sum_cols(lower.astype(F32), parts_f)
    col_b = sum_cols((s_id < r_id).astype(F32), parts_b)
    left = s_id < HD
    for p in range(PAIRS):
        x_pair = xv[:, p * 2 * HD : (p + 1) * 2 * HD].astype(F32)
        weights = []
        for h in (2 * p, 2 * p + 1):
            at_f = jnp.broadcast_to(col_f[:, h : h + 1], (F, F))
            at_b = jnp.broadcast_to(col_b[:, h : h + 1], (F, F))
            exponent = jnp.where(lower, at_f - row_f[h : h + 1], row_b[h : h + 1] - at_b)
            weights.append((jnp.exp(exponent) * gram).astype(BF))
        apart = jnp.concatenate(
            [jnp.where(left, x_pair, 0.0), jnp.where(left, 0.0, x_pair)], axis=0
        ).astype(BF)
        intra = dot(jnp.concatenate(weights, axis=1), apart)
        inside = intra + jnp.where(left[0:1], gain[2 * p], gain[2 * p + 1]) * x_pair
        pre[p] = inside
        prebf[p] = inside.astype(BF)
    rims = (
        remote(prebf.at[:, 0:RIM], rim_r, sem_rim, {"frames": prev}),
        remote(prebf.at[:, RIM:F], rim_l, sem_rim + 1, {"frames": succ}),
    )
    for copy in rims:
        start(copy)

    row_states(0)
    row_states(1)

    arrive(NI, crx, sem_c)
    picked_f = jnp.concatenate([r[0:HP] for r in rows], axis=0)
    picked_b = jnp.concatenate([r[HP : 2 * HP] for r in rows], axis=0)
    cols = (
        sum_cols(lower.astype(F32), thirds(picked_f)),
        sum_cols((s_id >= r_id).astype(F32), thirds(picked_b)),
    )

    def group_terms(d):
        total = jnp.zeros((2 * HP, N), F32)
        for j in range(NI) if d == 0 else reversed(range(NI)):
            for e in range(LP):
                at = [
                    jnp.broadcast_to(cols[d][:, HP * j + 2 * e + h : HP * j + 2 * e + h + 1], (F, F))
                    for h in range(2)
                ]
                spread = jnp.exp(jnp.where(left, at[0], at[1]))
                h = d * HP + 2 * e
                lead = jnp.exp(jnp.where(left[0:1], total[h : h + 1], total[h + 1 : h + 2]))
                grown[d, j, e] = spread * lead
                part = spread * dot_nt(crx[j], within[d, j, e * N : (e + 1) * N])
                local_part[j, e] = part if d == 0 else local_part[j, e] + part
            total = total + tots[j]

    group_terms(0)
    group_terms(1)
    entering(0)
    entering(1)
    for p in late:
        for d in range(2):
            send_back(d, p)
    for d in range(2):
        ours = all_of(crecv.at[d], ng)
        sent.append(remote(ours, ours, sem_b[d], {"frames": prev}))

    fetched["start"].wait()
    fetched["len"].wait()
    groups = starts.shape[0]
    tokens, window = bias.shape
    per_group = tokens // groups
    place = lax.broadcasted_iota(jnp.int32, (per_group, window), 1) + (me * F - RIM)
    for k in range(groups):
        allowed = (place >= starts[k]) & (place < starts[k] + lens[k])
        bias[k * per_group : (k + 1) * per_group, :] = jnp.where(allowed, 0.0, -jnp.inf)
    rwin[:, 0:RIM] = jnp.zeros((LP, RIM, N), BF)
    rwin[:, RIM + NI * F :] = jnp.zeros((LP, RIM, N), BF)

    for d in range(2):
        arrive(ng, crecv.at[d], sem_b[d])
        carried = crecv[d].reshape(PIECE, N)
        for j in range(NI):
            for e in range(LP):
                part = local_part[j, e] + grown[d, j, e] * dot_nt(crx[j], carried[e * N : (e + 1) * N])
                if d == 0:
                    local_part[j, e] = part
                else:
                    rwin[e, RIM + j * F : RIM + (j + 1) * F] = part.astype(BF)

    def pairs_of(q):
        return pl.ds(q * LP, LP)

    def window_of(p, q):
        if NI > 2:
            src = rwin.at[:, pl.ds(pl.multiple_of(p * F, F), 2 * F)]
            return src, rin.at[pairs_of(q)]
        src = rwin.at[:, pl.ds(pl.multiple_of((p + 1) * RIM, RIM), 3 * RIM)]
        return src, rin.at[pairs_of(q), pl.ds(pl.multiple_of((1 - p) * RIM, RIM), 3 * RIM)]

    rim_there = rx.at[pairs_of(i)]
    start(
        remote(rwin.at[:, RIM : 2 * RIM], rim_there, sem_rx, {"frames": base_prev + NI - 1}, sem_rx + i)
    )
    start(
        remote(
            rwin.at[:, NI * F : NI * F + RIM], rim_there, sem_rx + 1, {"frames": base_succ}, sem_rx + i
        )
    )
    for k in range(1, NI):
        p = lax.rem(i + k, NI)
        start(remote(*window_of(p, i), sem_r + k - 1, {"frames": at_i(p)}))
    rin[pairs_of(i)] = rwin[:, pl.ds(pl.multiple_of(i * F, F), 2 * F)]
    remote(prebf.at[:, 0:RIM], rim_r, sem_rim, {"frames": prev}).wait_recv()
    remote(prebf.at[:, RIM:F], rim_l, sem_rim + 1, {"frames": succ}).wait_recv()

    def rows_in(q):
        remote(
            rwin.at[:, 0:RIM], rx.at[pairs_of(q)], sem_rx, {"frames": prev}, sem_rx + q
        ).wait_recv()

    for k in range(NI):
        q = lax.rem(i + NI - k, NI)
        if k > 0:
            remote(*window_of(i, q), sem_r + k - 1, {"frames": at_i(q)}).wait_recv()

        @pl.when((i == 0) | (i == NI - 1))
        def _():
            rows_in(q)

        @pl.when(i == 0)
        def _():
            rin[pairs_of(q), 0:RIM] = rx[pairs_of(q)]

        @pl.when(i == NI - 1)
        def _():
            rin[pairs_of(q), RIM + F :] = rx[pairs_of(q)]

        for e in range(LP):
            m = q * LP + e
            wide[tok, m, 0:RIM] = (rim_l[m].astype(F32) + rin[m, 0:RIM].astype(F32)).astype(BF)
            wide[tok, m, RIM : RIM + F] = (pre[m] + rin[m, RIM : RIM + F].astype(F32)).astype(BF)
            wide[tok, m, RIM + F :] = (rim_r[m].astype(F32) + rin[m, RIM + F :].astype(F32)).astype(BF)
        if tok_count > 1:
            piece = wide.at[tok, pairs_of(q)]
            start(remote(piece, piece, sem_w + k, {"tok": 1 - tok}))

    fetched["wk"].wait()
    fetched["wv"].wait()

    def half_rows(t):
        return jnp.concatenate([wide[t, p] for p in range(PAIRS)], axis=1)

    mine = half_rows(tok)
    at = pl.ds(pl.multiple_of(tok * half, half), half)
    kacc[...] = dot(mine, wk[at, :])
    vacc[...] = dot(mine, wv[at, :])
    fetched["q"].wait()
    for copy in sent:
        copy.wait_send()
    if tok_count > 1:
        other = 1 - tok
        for k in range(NI):
            q = lax.rem(i + NI - k, NI)
            piece = wide.at[other, pairs_of(q)]
            remote(piece, piece, sem_w + k, {"tok": other}).wait_recv()
        theirs = half_rows(other)
        at = pl.ds(pl.multiple_of(other * half, half), half)
        keys[...] = (kacc[...] + dot(theirs, wk[at, :])).astype(BF)
        values[...] = (vacc[...] + dot(theirs, wv[at, :])).astype(BF)
    else:
        keys[...] = kacc[...].astype(BF)
        values[...] = vacc[...].astype(BF)


def reader(wide, keys, values, queries, bias, enc_hbm, out_hbm, enc, out, sem):
    tok = lax.axis_index("tok")
    for p in range(PAIRS):
        enc[:, p * 2 * HD : (p + 1) * 2 * HD] = wide[tok, p, RIM : RIM + F]
    copies = [pltpu.make_async_copy(enc, enc_hbm, sem.at[0])]
    copies[0].start()
    left = lax.broadcasted_iota(jnp.int32, (1, 2 * DHD), 1) < DHD
    for p in range(queries.shape[1] // (2 * DHD)):
        cols = slice(p * 2 * DHD, (p + 1) * 2 * DHD)
        q_pair = queries[:, cols]
        k_pair = keys[:, cols].astype(F32)
        v_pair = values[:, cols]
        both = []
        for only in (jnp.where(left, k_pair, 0.0), jnp.where(left, 0.0, k_pair)):
            scores = dot_nt(q_pair, only.astype(BF)) + bias[...]
            top = jnp.max(scores, axis=1, keepdims=True)
            raised = jnp.exp((scores - top) * DHD ** (-0.5))
            whole = 1.0 / jnp.sum(raised, axis=1, keepdims=True)
            both.append(dot(raised.astype(BF), v_pair) * whole)
        out[:, cols] = jnp.where(left, both[0], both[1]).astype(BF)
        copies.append(pltpu.make_async_copy(out.at[:, cols], out_hbm.at[:, cols], sem.at[p + 1]))
        copies[-1].start()
    for copy in copies:
        copy.wait()


def solution(mesh):
    frames = mesh.shape["frames"]
    tok_count = mesh.shape["tok"]
    ng = min(16 // NI, frames // NI)
    ny = frames // (NI * ng)
    sub = PIECE // ng
    vmem = pl.BlockSpec(memory_space=pltpu.VMEM)
    hbm = pl.BlockSpec(memory_space=pltpu.HBM)

    def local(x, b, c, log_decay, gain, key_weight, value_weight, queries, span_start, span_len):
        count, width = x.shape
        window = 2 * count
        tokens, out_width = queries.shape
        copies = 14 + 3 * NI
        wide, keys, values, held, bias = pl.pallas_call(
            functools.partial(mixer, (ny, ng, tok_count)),
            out_shape=(
                jax.ShapeDtypeStruct((tok_count, PAIRS, window, N), BF),
                jax.ShapeDtypeStruct((window, out_width), BF),
                jax.ShapeDtypeStruct((window, out_width), BF),
                jax.ShapeDtypeStruct(queries.shape, BF),
                jax.ShapeDtypeStruct((tokens, window), F32),
            ),
            in_specs=[hbm] * 10,
            out_specs=(vmem,) * 5,
            scratch_shapes=[
                pltpu.VMEM(x.shape, BF),
                pltpu.VMEM(b.shape, BF),
                pltpu.VMEM(c.shape, BF),
                pltpu.VMEM(log_decay.shape, F32),
                pltpu.SMEM(gain.shape, F32),
                pltpu.SMEM(span_start.shape, jnp.int32),
                pltpu.SMEM(span_len.shape, jnp.int32),
                pltpu.VMEM(key_weight.shape, BF),
                pltpu.VMEM(value_weight.shape, BF),
                pltpu.VMEM((2, NI, PIECE, N), BF),
                pltpu.VMEM((2, NI, PIECE, N), BF),
                pltpu.VMEM((NI,) + c.shape, BF),
                pltpu.VMEM((NI,) + log_decay.shape, F32),
                pltpu.VMEM((2, ng, sub, N), BF),
                pltpu.VMEM((2, ng, sub, N), BF),
                pltpu.VMEM((8, N), F32),
                pltpu.VMEM((ng, 8, N), F32),
                pltpu.VMEM((2, sub, N), BF),
                pltpu.VMEM((2, ny, sub, N), BF),
                pltpu.VMEM((8, N), F32),
                pltpu.VMEM((ny, 8, N), F32),
                pltpu.VMEM((2, ng, sub, N), BF),
                pltpu.VMEM((2, ng, sub, N), BF),
                pltpu.VMEM((PAIRS, count, N), F32),
                pltpu.VMEM((PAIRS, count, N), BF),
                pltpu.VMEM((PAIRS, RIM, N), BF),
                pltpu.VMEM((PAIRS, RIM, N), BF),
                pltpu.VMEM((2, NI, PIECE, N), BF),
                pltpu.VMEM((2, NI, LP, count, N), F32),
                pltpu.VMEM((NI, LP, count, N), F32),
                pltpu.VMEM((LP, 2 * RIM + NI * count, N), BF),
                pltpu.VMEM((PAIRS, window, N), BF),
                pltpu.VMEM((PAIRS, RIM, N), BF),
                pltpu.VMEM((window, out_width), F32),
                pltpu.VMEM((window, out_width), F32),
                pltpu.SemaphoreType.DMA((10,)),
                pltpu.SemaphoreType.DMA((copies,)),
                pltpu.SemaphoreType.DMA((copies,)),
            ],
            compiler_params=pltpu.CompilerParams(
                collective_id=0, has_side_effects=True, vmem_limit_bytes=24 * 2**20
            ),
        )(
            *(
                pltpu.with_memory_space_constraint(a, pltpu.HBM)
                for a in (
                    x,
                    b,
                    c,
                    log_decay,
                    gain,
                    key_weight,
                    value_weight,
                    queries,
                    span_start,
                    span_len,
                )
            )
        )
        return pl.pallas_call(
            reader,
            out_shape=(
                jax.ShapeDtypeStruct((count, width), BF),
                jax.ShapeDtypeStruct(queries.shape, BF),
            ),
            in_specs=[vmem] * 5,
            out_specs=(hbm, hbm),
            scratch_shapes=[
                pltpu.VMEM((count, width), BF),
                pltpu.VMEM(queries.shape, BF),
                pltpu.SemaphoreType.DMA((out_width // (2 * DHD) + 1,)),
            ],
            compiler_params=pltpu.CompilerParams(vmem_limit_bytes=24 * 2**20),
        )(wide, keys, values, held, bias)

    placed = (
        P(("dp", "frames"), "tok"),
        P(("dp", "frames"), None),
        P(("dp", "frames"), None),
        P(None, "tok", ("dp", "frames")),
        P("tok"),
        P(None, "tok"),
        P(None, "tok"),
        P(("dp", "frames"), "tok"),
        P(("dp", "frames")),
        P(("dp", "frames")),
    )
    return jax.shard_map(
        local,
        mesh=mesh,
        in_specs=placed,
        out_specs=(P(("dp", "frames"), "tok"), P(("dp", "frames"), "tok")),
        check_vma=False,
    )
```

```python
import functools

import jax
import jax.numpy as jnp
from jax import lax
from jax.experimental import pallas as pl
from jax.experimental.pallas import tpu as pltpu
from jax.sharding import PartitionSpec as P

DHD = 64
F = 128
RIM = 64
N = 128
HD = 64
NI = 2
PAIRS = 4
HP = 2 * PAIRS // NI
LP = PAIRS // NI
PIECE = HP * HD
MESH = pl.DeviceIdType.MESH
HIGH = lax.Precision.HIGHEST
NT = (((1,), (1,)), ((), ()))
BF = jnp.bfloat16
F32 = jnp.float32


def dot(a, b):
    return jnp.dot(a, b, preferred_element_type=F32)


def dot_nt(a, b, precision=None):
    return lax.dot_general(a, b, NT, precision=precision, preferred_element_type=F32)


def thirds(a):
    high = a.astype(BF)
    rest = a - high.astype(F32)
    mid = rest.astype(BF)
    return high, mid, (rest - mid.astype(F32)).astype(BF)


def sum_rows(parts, mask):
    both = dot(jnp.concatenate(parts, axis=0), mask.astype(BF))
    n = parts[0].shape[0]
    return both[0:n] + both[n : 2 * n] + both[2 * n : 3 * n]


def sum_cols(mask, parts):
    return functools.reduce(jnp.add, [dot_nt(mask.astype(BF), p) for p in reversed(parts)])


def tall(tile, first):
    return jnp.concatenate(
        [jnp.broadcast_to(tile[first + k : first + k + 1], (HD, N)) for k in range(HP)], axis=0
    )


def mixer(
    dims,
    x_hbm,
    b_hbm,
    c_hbm,
    ld_hbm,
    gain_hbm,
    wk_hbm,
    wv_hbm,
    q_hbm,
    start_hbm,
    len_hbm,
    wide,
    keys,
    values,
    q_out,
    bias,
    xv,
    gain,
    starts,
    lens,
    wk,
    wv,
    xrx,
    brx,
    crx,
    ldrx,
    states,
    gsend,
    grecv,
    gtsend,
    gtrecv,
    ysend,
    yrecv,
    ytsend,
    ytrecv,
    csend,
    crecv,
    entered,
    pre,
    prebf,
    rim_l,
    rim_r,
    within,
    grown,
    local_part,
    rwin,
    rin,
    rx,
    kacc,
    vacc,
    hsem,
    ssem,
    rsem,
):
    ny, ng, tok_count = dims
    heads = ldrx.shape[2]
    half = xv.shape[1]
    sub = PIECE // ng
    frames = ny * ng * NI
    row = ng * NI
    me = lax.axis_index("frames")
    tok = lax.axis_index("tok")
    y = me // row
    g = lax.rem(me // NI, ng)
    i = lax.rem(me, NI)
    base = me - i

    def at_i(p):
        return base + p

    def at_g(p):
        return me + (p - g) * NI

    def at_y(p):
        return me + (p - y) * row

    prev = lax.rem(me + frames - 1, frames)
    succ = lax.rem(me + 1, frames)
    base_prev = lax.rem(base + frames - NI, frames)
    base_succ = lax.rem(base + NI, frames)

    fetched = {}

    def fetch(name, src, dst):
        copy = pltpu.make_async_copy(src, dst, hsem.at[len(fetched)])
        copy.start()
        fetched[name] = copy

    def piece_of(p):
        return x_hbm.at[:, pl.ds(pl.multiple_of(p * PIECE, PIECE), PIECE)]

    fetch("ld", ld_hbm, ldrx.at[i])
    fetch("piece", piece_of(i), xrx.at[i])
    fetch("b", b_hbm, brx.at[i])
    fetch("c", c_hbm, crx.at[i])
    fetch("x", x_hbm, xv)
    fetch("gain", gain_hbm, gain)
    fetch("start", start_hbm, starts)
    fetch("len", len_hbm, lens)
    fetch("wk", wk_hbm, wk)
    fetch("wv", wv_hbm, wv)
    fetch("q", q_hbm, q_out)

    barrier = pltpu.get_barrier_semaphore()

    def greet(**device):
        pl.semaphore_signal(barrier, inc=1, device_id=device, device_id_type=MESH)

    greeted = 0
    for own, count, place in ((i, NI, at_i), (g, ng, at_g), (y, ny, at_y)):
        for k in range(1, count):
            greet(frames=place(lax.rem(own + k, count)))
            greeted += 1
    greet(frames=prev)
    greet(frames=succ)
    greeted += 2
    if tok_count > 1:
        greet(tok=1 - tok)
        greeted += 1

    @pl.when(i == 0)
    def _():
        for k in range(NI):
            greet(frames=base_prev + k)

    @pl.when(i == NI - 1)
    def _():
        for k in range(NI):
            greet(frames=base_succ + k)

    greeted += 2

    sent = []
    taken = [0]

    def take(n):
        first = taken[0]
        taken[0] += n
        return first

    def remote(src, dst, index, device, landing=None):
        return pltpu.make_async_remote_copy(
            src_ref=src,
            dst_ref=dst,
            send_sem=ssem.at[index],
            recv_sem=rsem.at[index if landing is None else landing],
            device_id=device,
            device_id_type=MESH,
        )

    def start(copy):
        copy.start()
        sent.append(copy)

    def far_first(count):
        return sorted(range(1, count), key=lambda k: -min(k, count - k))

    def all_of(dst, count):
        return dst.at[pl.ds(0, count - 1)]

    def scatter(own, count, place, src, dst, index):
        for k in far_first(count):
            p = lax.rem(own + k, count)
            remote(src.at[p], dst.at[own], index, {"frames": place(p)}).start()
        sent.append(remote(all_of(dst, count), all_of(dst, count), index, {"frames": prev}))

    def share(own, count, place, src, dst, index):
        for k in far_first(count):
            p = lax.rem(own + k, count)
            remote(src, dst.at[own], index, {"frames": place(p)}).start()
        sent.append(remote(all_of(dst, count), all_of(dst, count), index, {"frames": prev}))

    def arrive(count, dst, index):
        remote(all_of(dst, count), all_of(dst, count), index, {"frames": prev}).wait_recv()

    sem_ld, sem_c, sem_gt, sem_yt = take(1), take(1), take(1), take(1)
    sem_x, sem_wr = take(1), take(1)
    sem_g, sem_y, sem_b = [(take(1), take(1)) for _ in range(3)]
    sem_rim = take(2)
    sem_r = take(NI - 1)
    sem_rx = take(NI)
    sem_w = take(NI)

    pl.semaphore_wait(barrier, greeted)
    share(i, NI, at_i, ld_hbm, ldrx, sem_ld)
    for k in range(1, NI):
        p = lax.rem(i + k, NI)
        remote(piece_of(p), xrx.at[i], sem_x, {"frames": at_i(p)}).start()
    sent.append(remote(all_of(xrx, NI), all_of(xrx, NI), sem_x, {"frames": prev}))
    share(i, NI, at_i, b_hbm, brx, sem_wr)
    share(i, NI, at_i, c_hbm, crx, sem_c)

    r_id = lax.broadcasted_iota(jnp.int32, (F, F), 0)
    s_id = lax.broadcasted_iota(jnp.int32, (F, F), 1)

    sides = jnp.concatenate([(r_id > s_id).astype(F32), (r_id < s_id).astype(F32)], axis=1)

    def rates_of(j):
        return jnp.concatenate(
            [
                functools.reduce(
                    lambda a, p: jnp.where(i == p, ldrx[j, e, HP * p : HP * p + HP, :], a),
                    range(1, NI),
                    ldrx[j, e, 0:HP, :],
                )
                for e in range(2)
            ],
            axis=0,
        )

    def ends_of(j):
        ends = jnp.exp(sum_rows(thirds(rates_of(j)), sides))
        return ends[:, 0:F], ends[:, F : 2 * F]

    def block_state(d, j, turned, ends):
        scaled = (turned * tall(ends[d], d * HP)).astype(BF)
        states[d, j] = dot(scaled, brx[j])

    fetched["ld"].wait()
    own_ends = ends_of(i)
    fetched["piece"].wait()
    fetched["b"].wait()
    own_turned = xrx[i].astype(F32).T
    for d in range(2):
        block_state(d, i, own_turned, own_ends)
    arrive(NI, ldrx, sem_ld)
    rows = [rates_of(j) for j in range(NI)]
    tots = [jnp.broadcast_to(jnp.sum(r, axis=1, keepdims=True), (2 * HP, N)) for r in rows]
    decays = [jnp.exp(t) for t in tots]
    gtsend[0 : 2 * HP] = functools.reduce(jnp.add, tots)
    if 2 * HP < 8:
        gtsend[2 * HP :] = jnp.zeros((8 - 2 * HP, N), F32)
    share(g, ng, at_g, gtsend, gtrecv, sem_gt)
    gtrecv[g] = gtsend[...]
    others = [lax.rem(i + k, NI) for k in range(1, NI)]
    ends = [ends_of(q) for q in others]
    arrive(NI, xrx, sem_x)
    turned = [xrx[q].astype(F32).T for q in others]
    arrive(NI, brx, sem_wr)

    def group_states(d):
        for k, q in enumerate(others):
            block_state(d, q, turned[k], ends[k])
        state = jnp.zeros((PIECE, N), F32)
        for j in range(NI) if d == 0 else reversed(range(NI)):
            within[d, j] = state.astype(BF)
            state = tall(decays[j], d * HP) * state + states[d, j]
        for k in range(ng):
            gsend[d, k] = state[k * sub : (k + 1) * sub].astype(BF)
        scatter(g, ng, at_g, gsend.at[d], grecv.at[d], sem_g[d])
        grecv[d, pl.ds(g, 1)] = gsend[d, pl.ds(g, 1)]

    group_tots = [[], []]
    into = [[None] * ng, [None] * ng]
    ahead = [[None] * ng, [None] * ng]

    def row_states(d):
        if d == 1:
            arrive(ng, gtrecv, sem_gt)
            head = (g * sub) // HD
            for k in range(ng):
                for e in range(2):
                    one = gtrecv[k, e * HP : e * HP + 1, :]
                    for h in range(1, HP):
                        one = jnp.where(head == h, gtrecv[k, e * HP + h : e * HP + h + 1, :], one)
                    group_tots[e].append(one)
            if ny > 1:
                ytsend[...] = jnp.concatenate(
                    [functools.reduce(jnp.add, group_tots[e]) for e in range(2)]
                    + [jnp.zeros((6, N), F32)],
                    axis=0,
                )
                share(y, ny, at_y, ytsend, ytrecv, sem_yt)
                ytrecv[y] = ytsend[...]
        arrive(ng, grecv.at[d], sem_g[d])
        state, total = jnp.zeros((sub, N), F32), jnp.zeros((1, N), F32)
        for k in range(ng) if d == 0 else reversed(range(ng)):
            into[d][k], ahead[d][k] = state, jnp.exp(total)
            state = jnp.exp(group_tots[d][k]) * state + grecv[d, k].astype(F32)
            total = total + group_tots[d][k]
        if ny > 1:
            ysend[d] = state.astype(BF)
            share(y, ny, at_y, ysend.at[d], yrecv.at[d], sem_y[d])
            yrecv[d, pl.ds(y, 1)] = ysend[d][None]

    def entering(d):
        enter = jnp.zeros((sub, N), F32)
        if ny > 1:
            if d == 1:
                arrive(ny, ytrecv, sem_yt)
            arrive(ny, yrecv.at[d], sem_y[d])
            state = jnp.zeros((sub, N), F32)
            for k in range(ny) if d == 0 else reversed(range(ny)):
                enter = jnp.where(y == k, state, enter)
                state = jnp.exp(ytrecv[k, d : d + 1, :]) * state + yrecv[d, k].astype(F32)
        for k in range(ng):
            csend[d, k] = (into[d][k] + ahead[d][k] * enter).astype(BF)
        crecv[d, pl.ds(g, 1)] = csend[d, pl.ds(g, 1)]
        for p in early:
            send_back(d, p)

    early = [p for p in (0, ng - 1, 1) if p < ng][: max(1, ng - 1)]
    late = [p for p in [2, *range(3, ng - 1)] if p < ng and p not in early]

    def send_back(d, p):
        @pl.when(g != p)
        def _():
            remote(csend.at[d, p], crecv.at[d, g], sem_b[d], {"frames": at_g(p)}).start()

    group_states(1)
    group_states(0)

    fetched["c"].wait()
    fetched["gain"].wait()
    fetched["x"].wait()
    gram = dot_nt(crx[i], brx[i])
    parts_f = thirds(ldrx[i, 0])
    parts_b = thirds(ldrx[i, 1])
    row_b = sum_rows(parts_b, (r_id < s_id).astype(F32))
    gram = jnp.where(r_id == s_id, 2.0 * gram, gram)
    lower = s_id <= r_id
    row_f = sum_rows(parts_f, (r_id <= s_id).astype(F32))
    col_f = sum_cols(lower.astype(F32), parts_f)
    col_b = sum_cols((s_id < r_id).astype(F32), parts_b)
    left = s_id < HD
    for p in range(PAIRS):
        x_pair = xv[:, p * 2 * HD : (p + 1) * 2 * HD].astype(F32)
        weights = []
        for h in (2 * p, 2 * p + 1):
            at_f = jnp.broadcast_to(col_f[:, h : h + 1], (F, F))
            at_b = jnp.broadcast_to(col_b[:, h : h + 1], (F, F))
            exponent = jnp.where(lower, at_f - row_f[h : h + 1], row_b[h : h + 1] - at_b)
            weights.append((jnp.exp(exponent) * gram).astype(BF))
        apart = jnp.concatenate(
            [jnp.where(left, x_pair, 0.0), jnp.where(left, 0.0, x_pair)], axis=0
        ).astype(BF)
        intra = dot(jnp.concatenate(weights, axis=1), apart)
        inside = intra + jnp.where(left[0:1], gain[2 * p], gain[2 * p + 1]) * x_pair
        pre[p] = inside
        prebf[p] = inside.astype(BF)
    rims = (
        remote(prebf.at[:, 0:RIM], rim_r, sem_rim, {"frames": prev}),
        remote(prebf.at[:, RIM:F], rim_l, sem_rim + 1, {"frames": succ}),
    )
    for copy in rims:
        start(copy)

    row_states(1)
    row_states(0)

    arrive(NI, crx, sem_c)
    picked_f = jnp.concatenate([r[0:HP] for r in rows], axis=0)
    picked_b = jnp.concatenate([r[HP : 2 * HP] for r in rows], axis=0)
    cols = (
        sum_cols(lower.astype(F32), thirds(picked_f)),
        sum_cols((s_id >= r_id).astype(F32), thirds(picked_b)),
    )

    def group_terms(d):
        total = jnp.zeros((2 * HP, N), F32)
        for j in range(NI) if d == 0 else reversed(range(NI)):
            for e in range(LP):
                at = [
                    jnp.broadcast_to(cols[d][:, HP * j + 2 * e + h : HP * j + 2 * e + h + 1], (F, F))
                    for h in range(2)
                ]
                spread = jnp.exp(jnp.where(left, at[0], at[1]))
                h = d * HP + 2 * e
                lead = jnp.exp(jnp.where(left[0:1], total[h : h + 1], total[h + 1 : h + 2]))
                grown[d, j, e] = spread * lead
                part = spread * dot_nt(crx[j], within[d, j, e * N : (e + 1) * N])
                local_part[j, e] = part if d == 0 else local_part[j, e] + part
            total = total + tots[j]

    group_terms(0)
    group_terms(1)
    entering(1)
    entering(0)
    for p in late:
        for d in (1, 0):
            send_back(d, p)
    for d in range(2):
        ours = all_of(crecv.at[d], ng)
        sent.append(remote(ours, ours, sem_b[d], {"frames": prev}))

    fetched["start"].wait()
    fetched["len"].wait()
    groups = starts.shape[0]
    tokens, window = bias.shape
    per_group = tokens // groups
    place = lax.broadcasted_iota(jnp.int32, (per_group, window), 1) + (me * F - RIM)
    for k in range(groups):
        allowed = (place >= starts[k]) & (place < starts[k] + lens[k])
        bias[k * per_group : (k + 1) * per_group, :] = jnp.where(allowed, 0.0, -jnp.inf)
    rwin[:, 0:RIM] = jnp.zeros((LP, RIM, N), BF)
    rwin[:, RIM + NI * F :] = jnp.zeros((LP, RIM, N), BF)

    opening = base == 0
    for d in (1, 0):
        carried = crecv.at[d]
        if d == 1:
            arrive(ng, carried, sem_b[d])
            carried = carried[...].reshape(PIECE, N)
        else:

            @pl.when(jnp.logical_not(opening))
            def _():
                arrive(ng, crecv.at[0], sem_b[0])

            @pl.when(opening)
            def _():
                entered[...] = jnp.zeros_like(entered)

            @pl.when(jnp.logical_not(opening))
            def _():
                entered[...] = crecv[0].reshape(PIECE, N)

            carried = entered[...]
        for j in range(NI):
            for e in range(LP):
                part = local_part[j, e] + grown[d, j, e] * dot_nt(crx[j], carried[e * N : (e + 1) * N])
                if d == 1:
                    local_part[j, e] = part
                else:
                    rwin[e, RIM + j * F : RIM + (j + 1) * F] = part.astype(BF)

    def pairs_of(q):
        return pl.ds(q * LP, LP)

    def window_of(p, q):
        if NI > 2:
            src = rwin.at[:, pl.ds(pl.multiple_of(p * F, F), 2 * F)]
            return src, rin.at[pairs_of(q)]
        src = rwin.at[:, pl.ds(pl.multiple_of((p + 1) * RIM, RIM), 3 * RIM)]
        return src, rin.at[pairs_of(q), pl.ds(pl.multiple_of((1 - p) * RIM, RIM), 3 * RIM)]

    rim_there = rx.at[pairs_of(i)]
    start(
        remote(rwin.at[:, RIM : 2 * RIM], rim_there, sem_rx, {"frames": base_prev + NI - 1}, sem_rx + i)
    )
    start(
        remote(
            rwin.at[:, NI * F : NI * F + RIM], rim_there, sem_rx + 1, {"frames": base_succ}, sem_rx + i
        )
    )
    for k in range(1, NI):
        p = lax.rem(i + k, NI)
        start(remote(*window_of(p, i), sem_r + k - 1, {"frames": at_i(p)}))
    rin[pairs_of(i)] = rwin[:, pl.ds(pl.multiple_of(i * F, F), 2 * F)]
    remote(prebf.at[:, 0:RIM], rim_r, sem_rim, {"frames": prev}).wait_recv()
    remote(prebf.at[:, RIM:F], rim_l, sem_rim + 1, {"frames": succ}).wait_recv()

    def rows_in(q):
        remote(
            rwin.at[:, 0:RIM], rx.at[pairs_of(q)], sem_rx, {"frames": prev}, sem_rx + q
        ).wait_recv()

    for k in range(NI):
        q = lax.rem(i + NI - k, NI)
        if k > 0:
            remote(*window_of(i, q), sem_r + k - 1, {"frames": at_i(q)}).wait_recv()

        @pl.when((i == 0) & (me > 0))
        def _():
            rows_in(q)
            rin[pairs_of(q), 0:RIM] = rx[pairs_of(q)]

        @pl.when((i == NI - 1) & (me < frames - 1))
        def _():
            rows_in(q)
            rin[pairs_of(q), RIM + F :] = rx[pairs_of(q)]

        @pl.when(me == 0)
        def _():
            rin[pairs_of(q), 0:RIM] = jnp.zeros((LP, RIM, N), BF)

        @pl.when(me == frames - 1)
        def _():
            rin[pairs_of(q), RIM + F :] = jnp.zeros((LP, RIM, N), BF)

        for e in range(LP):
            m = q * LP + e
            wide[tok, m, 0:RIM] = (rim_l[m].astype(F32) + rin[m, 0:RIM].astype(F32)).astype(BF)
            wide[tok, m, RIM : RIM + F] = (pre[m] + rin[m, RIM : RIM + F].astype(F32)).astype(BF)
            wide[tok, m, RIM + F :] = (rim_r[m].astype(F32) + rin[m, RIM + F :].astype(F32)).astype(BF)
        if tok_count > 1:
            piece = wide.at[tok, pairs_of(q)]
            start(remote(piece, piece, sem_w + k, {"tok": 1 - tok}))

    fetched["wk"].wait()
    fetched["wv"].wait()

    def half_rows(t):
        return jnp.concatenate([wide[t, p] for p in range(PAIRS)], axis=1)

    mine = half_rows(tok)
    at = pl.ds(pl.multiple_of(tok * half, half), half)
    kacc[...] = dot(mine, wk[at, :])
    vacc[...] = dot(mine, wv[at, :])
    fetched["q"].wait()
    for copy in sent:
        copy.wait_send()
    if tok_count > 1:
        other = 1 - tok
        for k in range(NI):
            q = lax.rem(i + NI - k, NI)
            piece = wide.at[other, pairs_of(q)]
            remote(piece, piece, sem_w + k, {"tok": other}).wait_recv()
        theirs = half_rows(other)
        at = pl.ds(pl.multiple_of(other * half, half), half)
        keys[...] = (kacc[...] + dot(theirs, wk[at, :])).astype(BF)
        values[...] = (vacc[...] + dot(theirs, wv[at, :])).astype(BF)
    else:
        keys[...] = kacc[...].astype(BF)
        values[...] = vacc[...].astype(BF)

    @pl.when((me == 0) | (me == frames - 1))
    def _():
        for q in range(NI):
            rows_in(q)

    @pl.when(opening)
    def _():
        arrive(ng, crecv.at[0], sem_b[0])


def reader(wide, keys, values, queries, bias, enc_hbm, out_hbm, enc, out, sem):
    tok = lax.axis_index("tok")
    for p in range(PAIRS):
        enc[:, p * 2 * HD : (p + 1) * 2 * HD] = wide[tok, p, RIM : RIM + F]
    copies = [pltpu.make_async_copy(enc, enc_hbm, sem.at[0])]
    copies[0].start()
    left = lax.broadcasted_iota(jnp.int32, (1, 2 * DHD), 1) < DHD
    for p in range(queries.shape[1] // (2 * DHD)):
        cols = slice(p * 2 * DHD, (p + 1) * 2 * DHD)
        q_pair = queries[:, cols]
        k_pair = keys[:, cols].astype(F32)
        v_pair = values[:, cols]
        both = []
        for only in (jnp.where(left, k_pair, 0.0), jnp.where(left, 0.0, k_pair)):
            scores = dot_nt(q_pair, only.astype(BF)) + bias[...]
            top = jnp.max(scores, axis=1, keepdims=True)
            raised = jnp.exp((scores - top) * DHD ** (-0.5))
            whole = 1.0 / jnp.sum(raised, axis=1, keepdims=True)
            both.append(dot(raised.astype(BF), v_pair) * whole)
        out[:, cols] = jnp.where(left, both[0], both[1]).astype(BF)
        copies.append(pltpu.make_async_copy(out.at[:, cols], out_hbm.at[:, cols], sem.at[p + 1]))
        copies[-1].start()
    for copy in copies:
        copy.wait()


def solution(mesh):
    frames = mesh.shape["frames"]
    tok_count = mesh.shape["tok"]
    ng = min(16 // NI, frames // NI)
    ny = frames // (NI * ng)
    sub = PIECE // ng
    vmem = pl.BlockSpec(memory_space=pltpu.VMEM)
    hbm = pl.BlockSpec(memory_space=pltpu.HBM)

    def local(x, b, c, log_decay, gain, key_weight, value_weight, queries, span_start, span_len):
        count, width = x.shape
        window = 2 * count
        tokens, out_width = queries.shape
        copies = 14 + 3 * NI
        wide, keys, values, held, bias = pl.pallas_call(
            functools.partial(mixer, (ny, ng, tok_count)),
            out_shape=(
                jax.ShapeDtypeStruct((tok_count, PAIRS, window, N), BF),
                jax.ShapeDtypeStruct((window, out_width), BF),
                jax.ShapeDtypeStruct((window, out_width), BF),
                jax.ShapeDtypeStruct(queries.shape, BF),
                jax.ShapeDtypeStruct((tokens, window), F32),
            ),
            in_specs=[hbm] * 10,
            out_specs=(vmem,) * 5,
            scratch_shapes=[
                pltpu.VMEM(x.shape, BF),
                pltpu.SMEM(gain.shape, F32),
                pltpu.SMEM(span_start.shape, jnp.int32),
                pltpu.SMEM(span_len.shape, jnp.int32),
                pltpu.VMEM(key_weight.shape, BF),
                pltpu.VMEM(value_weight.shape, BF),
                pltpu.VMEM((NI, count, PIECE), BF),
                pltpu.VMEM((NI,) + b.shape, BF),
                pltpu.VMEM((NI,) + c.shape, BF),
                pltpu.VMEM((NI,) + log_decay.shape, F32),
                pltpu.VMEM((2, NI, PIECE, N), F32),
                pltpu.VMEM((2, ng, sub, N), BF),
                pltpu.VMEM((2, ng, sub, N), BF),
                pltpu.VMEM((8, N), F32),
                pltpu.VMEM((ng, 8, N), F32),
                pltpu.VMEM((2, sub, N), BF),
                pltpu.VMEM((2, ny, sub, N), BF),
                pltpu.VMEM((8, N), F32),
                pltpu.VMEM((ny, 8, N), F32),
                pltpu.VMEM((2, ng, sub, N), BF),
                pltpu.VMEM((2, ng, sub, N), BF),
                pltpu.VMEM((PIECE, N), BF),
                pltpu.VMEM((PAIRS, count, N), F32),
                pltpu.VMEM((PAIRS, count, N), BF),
                pltpu.VMEM((PAIRS, RIM, N), BF),
                pltpu.VMEM((PAIRS, RIM, N), BF),
                pltpu.VMEM((2, NI, PIECE, N), BF),
                pltpu.VMEM((2, NI, LP, count, N), F32),
                pltpu.VMEM((NI, LP, count, N), F32),
                pltpu.VMEM((LP, 2 * RIM + NI * count, N), BF),
                pltpu.VMEM((PAIRS, window, N), BF),
                pltpu.VMEM((PAIRS, RIM, N), BF),
                pltpu.VMEM((window, out_width), F32),
                pltpu.VMEM((window, out_width), F32),
                pltpu.SemaphoreType.DMA((11,)),
                pltpu.SemaphoreType.DMA((copies,)),
                pltpu.SemaphoreType.DMA((copies,)),
            ],
            compiler_params=pltpu.CompilerParams(
                collective_id=0, has_side_effects=True, vmem_limit_bytes=24 * 2**20
            ),
        )(
            *(
                pltpu.with_memory_space_constraint(a, pltpu.HBM)
                for a in (
                    x,
                    b,
                    c,
                    log_decay,
                    gain,
                    key_weight,
                    value_weight,
                    queries,
                    span_start,
                    span_len,
                )
            )
        )
        return pl.pallas_call(
            reader,
            out_shape=(
                jax.ShapeDtypeStruct((count, width), BF),
                jax.ShapeDtypeStruct(queries.shape, BF),
            ),
            in_specs=[vmem] * 5,
            out_specs=(hbm, hbm),
            scratch_shapes=[
                pltpu.VMEM((count, width), BF),
                pltpu.VMEM(queries.shape, BF),
                pltpu.SemaphoreType.DMA((out_width // (2 * DHD) + 1,)),
            ],
            compiler_params=pltpu.CompilerParams(vmem_limit_bytes=24 * 2**20),
        )(wide, keys, values, held, bias)

    placed = (
        P(("dp", "frames"), "tok"),
        P(("dp", "frames"), None),
        P(("dp", "frames"), None),
        P(None, "tok", ("dp", "frames")),
        P("tok"),
        P(None, "tok"),
        P(None, "tok"),
        P(("dp", "frames"), "tok"),
        P(("dp", "frames")),
        P(("dp", "frames")),
    )
    return jax.shard_map(
        local,
        mesh=mesh,
        in_specs=placed,
        out_specs=(P(("dp", "frames"), "tok"), P(("dp", "frames"), "tok")),
        check_vma=False,
    )
```

```python
import functools

import jax
import jax.numpy as jnp
from jax import lax
from jax.experimental import pallas as pl
from jax.experimental.pallas import tpu as pltpu
from jax.sharding import PartitionSpec as P

DHD = 64
F = 128
RIM = 64
N = 128
HD = 64
NI = 2
PAIRS = 4
HP = 2 * PAIRS // NI
LP = PAIRS // NI
PIECE = HP * HD
LOG2E = 1.4426950408889634
MESH = pl.DeviceIdType.MESH
HIGH = lax.Precision.HIGHEST
NT = (((1,), (1,)), ((), ()))
BF = jnp.bfloat16
F32 = jnp.float32


def dot(a, b):
    return jnp.dot(a, b, preferred_element_type=F32)


def dot_nt(a, b, precision=None):
    return lax.dot_general(a, b, NT, precision=precision, preferred_element_type=F32)


def thirds(a):
    high = a.astype(BF)
    rest = a - high.astype(F32)
    mid = rest.astype(BF)
    return high, mid, (rest - mid.astype(F32)).astype(BF)


def sum_rows(parts, mask):
    both = dot(jnp.concatenate(parts, axis=0), mask.astype(BF))
    n = parts[0].shape[0]
    return both[0:n] + both[n : 2 * n] + both[2 * n : 3 * n]


def sum_cols(mask, parts):
    return functools.reduce(jnp.add, [dot_nt(mask.astype(BF), p) for p in reversed(parts)])


def tall(tile, first):
    return jnp.concatenate(
        [jnp.broadcast_to(tile[first + k : first + k + 1], (HD, N)) for k in range(HP)], axis=0
    )


def mixer(
    dims,
    x_hbm,
    b_hbm,
    c_hbm,
    ld_hbm,
    gain_hbm,
    wk_hbm,
    wv_hbm,
    q_hbm,
    start_hbm,
    len_hbm,
    wide,
    keys,
    values,
    q_out,
    bias,
    xv,
    gain,
    starts,
    lens,
    wk,
    wv,
    xrx,
    brx,
    crx,
    ldrx,
    states,
    gsend,
    grecv,
    gtsend,
    gtrecv,
    ysend,
    yrecv,
    ytsend,
    ytrecv,
    csend,
    crecv,
    pre,
    prebf,
    rim_near,
    rim_far,
    within,
    grown,
    local_part,
    rwin,
    rin,
    rx,
    kacc,
    vacc,
    hsem,
    ssem,
    rsem,
):
    ny, ng, tok_count = dims
    heads = ldrx.shape[2]
    half = xv.shape[1]
    sub = PIECE // ng
    frames = ny * ng * NI
    row = ng * NI
    me = lax.axis_index("frames")
    tok = lax.axis_index("tok")
    y = me // row
    g = lax.rem(me // NI, ng)
    i = lax.rem(me, NI)
    base = me - i

    def at_i(p):
        return base + p

    def at_g(p):
        return me + (p - g) * NI

    def at_y(p):
        return me + (p - y) * row

    prev = lax.rem(me + frames - 1, frames)
    succ = lax.rem(me + 1, frames)
    base_prev = lax.rem(base + frames - NI, frames)
    base_succ = lax.rem(base + NI, frames)

    fetched = {}

    def fetch(name, src, dst):
        copy = pltpu.make_async_copy(src, dst, hsem.at[len(fetched)])
        copy.start()
        fetched[name] = copy

    def piece_of(p):
        return x_hbm.at[:, pl.ds(pl.multiple_of(p * PIECE, PIECE), PIECE)]

    fetch("ld", ld_hbm, ldrx.at[i])
    fetch("piece", piece_of(i), xrx.at[i])
    fetch("b", b_hbm, brx.at[i])
    fetch("c", c_hbm, crx.at[i])

    barrier = pltpu.get_barrier_semaphore()

    def greet(**device):
        pl.semaphore_signal(barrier, inc=1, device_id=device, device_id_type=MESH)

    greeted = 0
    for own, count, place in ((i, NI, at_i), (g, ng, at_g), (y, ny, at_y)):
        for k in range(1, count):
            greet(frames=place(lax.rem(own + k, count)))
            greeted += 1
    cross = jnp.where(i == 0, prev, succ)
    partner = base + NI - 1 - i
    group_there = jnp.where(i == 0, base_prev, base_succ)
    for t in range(tok_count):
        greet(frames=cross, tok=t)
        for k in range(NI):
            greet(frames=group_there + k, tok=t)
    greeted += tok_count + 2 * tok_count
    if tok_count > 1:
        greet(tok=1 - tok)
        greeted += 1

    sent = []
    taken = [0]

    def take(n):
        first = taken[0]
        taken[0] += n
        return first

    def remote(src, dst, index, device, landing=None):
        return pltpu.make_async_remote_copy(
            src_ref=src,
            dst_ref=dst,
            send_sem=ssem.at[index],
            recv_sem=rsem.at[index if landing is None else landing],
            device_id=device,
            device_id_type=MESH,
        )

    def start(copy):
        copy.start()
        sent.append(copy)

    def far_first(count):
        return sorted(range(1, count), key=lambda k: -min(k, count - k))

    def all_of(dst, count):
        return dst.at[pl.ds(0, count - 1)]

    def scatter(own, count, place, src, dst, index):
        for k in far_first(count):
            p = lax.rem(own + k, count)
            remote(src.at[p], dst.at[own], index, {"frames": place(p)}).start()
        sent.append(remote(all_of(dst, count), all_of(dst, count), index, {"frames": prev}))

    def share(own, count, place, src, dst, index):
        for k in far_first(count):
            p = lax.rem(own + k, count)
            remote(src, dst.at[own], index, {"frames": place(p)}).start()
        sent.append(remote(all_of(dst, count), all_of(dst, count), index, {"frames": prev}))

    def arrive(count, dst, index):
        remote(all_of(dst, count), all_of(dst, count), index, {"frames": prev}).wait_recv()

    sem_ld, sem_c, sem_gt, sem_yt = take(1), take(1), take(1), take(1)
    sem_x, sem_wr = take(1), take(1)
    sem_g, sem_y, sem_b = [(take(1), take(1)) for _ in range(3)]
    sem_rim, sem_far = take(1), take(tok_count)
    sem_r = take(NI - 1)
    sem_rx = take(2 * NI * tok_count)
    sem_w = take(NI)

    pl.semaphore_wait(barrier, greeted)
    for k in range(1, NI):
        p = lax.rem(i + k, NI)
        remote(piece_of(p), xrx.at[i], sem_x, {"frames": at_i(p)}).start()
    sent.append(remote(all_of(xrx, NI), all_of(xrx, NI), sem_x, {"frames": prev}))
    share(i, NI, at_i, b_hbm, brx, sem_wr)
    share(i, NI, at_i, ld_hbm, ldrx, sem_ld)
    share(i, NI, at_i, c_hbm, crx, sem_c)
    fetch("x", x_hbm, xv)
    fetch("gain", gain_hbm, gain)
    fetch("start", start_hbm, starts)
    fetch("len", len_hbm, lens)
    fetch("wk", wk_hbm, wk)
    fetch("wv", wv_hbm, wv)
    fetch("q", q_hbm, q_out)

    r_id = lax.broadcasted_iota(jnp.int32, (F, F), 0)
    s_id = lax.broadcasted_iota(jnp.int32, (F, F), 1)

    both_sides = jnp.concatenate([(r_id > s_id).astype(F32), (r_id < s_id).astype(F32)], axis=1)

    def rates_of(j):
        return jnp.concatenate(
            [
                functools.reduce(
                    lambda a, p: jnp.where(i == p, ldrx[j, e, HP * p : HP * p + HP, :], a),
                    range(1, NI),
                    ldrx[j, e, 0:HP, :],
                )
                for e in range(2)
            ],
            axis=0,
        )

    def ends_of(j):
        ends = jnp.exp(sum_rows(thirds(rates_of(j)), both_sides))
        return ends[:, 0:F], ends[:, F : 2 * F]

    def block_state(d, j, turned, ends):
        scaled = (turned * tall(ends[d], d * HP)).astype(BF)
        states[d, j] = dot(scaled, brx[j])

    fetched["ld"].wait()
    own_ends = ends_of(i)
    fetched["piece"].wait()
    fetched["b"].wait()
    own_turned = xrx[i].astype(F32).T
    for d in range(2):
        block_state(d, i, own_turned, own_ends)
    arrive(NI, ldrx, sem_ld)
    rows = [rates_of(j) for j in range(NI)]
    tots = [jnp.broadcast_to(jnp.sum(r, axis=1, keepdims=True), (2 * HP, N)) for r in rows]
    decays = [jnp.exp(t) for t in tots]
    gtsend[0 : 2 * HP] = functools.reduce(jnp.add, tots)
    if 2 * HP < 8:
        gtsend[2 * HP :] = jnp.zeros((8 - 2 * HP, N), F32)
    share(g, ng, at_g, gtsend, gtrecv, sem_gt)
    gtrecv[g] = gtsend[...]
    others = [lax.rem(i + k, NI) for k in range(1, NI)]
    ends = [ends_of(q) for q in others]
    arrive(NI, xrx, sem_x)
    turned = [xrx[q].astype(F32).T for q in others]
    arrive(NI, brx, sem_wr)

    def group_states(d):
        for k, q in enumerate(others):
            block_state(d, q, turned[k], ends[k])
        state = jnp.zeros((PIECE, N), F32)
        for j in range(NI) if d == 0 else reversed(range(NI)):
            within[d, j] = state.astype(BF)
            state = tall(decays[j], d * HP) * state + states[d, j]
        for k in range(ng):
            gsend[d, k] = state[k * sub : (k + 1) * sub].astype(BF)
        scatter(g, ng, at_g, gsend.at[d], grecv.at[d], sem_g[d])
        grecv[d, pl.ds(g, 1)] = gsend[d, pl.ds(g, 1)]

    group_tots = [[], []]
    into = [[None] * ng, [None] * ng]
    ahead = [[None] * ng, [None] * ng]

    def row_states(d):
        if d == 1:
            arrive(ng, gtrecv, sem_gt)
            head = (g * sub) // HD
            for k in range(ng):
                for e in range(2):
                    one = gtrecv[k, e * HP : e * HP + 1, :]
                    for h in range(1, HP):
                        one = jnp.where(head == h, gtrecv[k, e * HP + h : e * HP + h + 1, :], one)
                    group_tots[e].append(one)
            if ny > 1:
                ytsend[...] = jnp.concatenate(
                    [functools.reduce(jnp.add, group_tots[e]) for e in range(2)]
                    + [jnp.zeros((6, N), F32)],
                    axis=0,
                )
                share(y, ny, at_y, ytsend, ytrecv, sem_yt)
                ytrecv[y] = ytsend[...]
        arrive(ng, grecv.at[d], sem_g[d])
        state, total = jnp.zeros((sub, N), F32), jnp.zeros((1, N), F32)
        for k in range(ng) if d == 0 else reversed(range(ng)):
            into[d][k], ahead[d][k] = state, jnp.exp(total)
            state = jnp.exp(group_tots[d][k]) * state + grecv[d, k].astype(F32)
            total = total + group_tots[d][k]
        if ny > 1:
            ysend[d] = state.astype(BF)
            share(y, ny, at_y, ysend.at[d], yrecv.at[d], sem_y[d])
            yrecv[d, pl.ds(y, 1)] = ysend[d][None]

    def entering(d):
        enter = jnp.zeros((sub, N), F32)
        if ny > 1:
            if d == 1:
                arrive(ny, ytrecv, sem_yt)
            arrive(ny, yrecv.at[d], sem_y[d])
            state = jnp.zeros((sub, N), F32)
            for k in range(ny) if d == 0 else reversed(range(ny)):
                enter = jnp.where(y == k, state, enter)
                state = jnp.exp(ytrecv[k, d : d + 1, :]) * state + yrecv[d, k].astype(F32)
        for k in range(ng):
            csend[d, k] = (into[d][k] + ahead[d][k] * enter).astype(BF)
        crecv[d, pl.ds(g, 1)] = csend[d, pl.ds(g, 1)]
        for p in early:
            send_back(d, p)

    early = (0, ng - 1)
    late = range(1, ng - 1)

    def send_back(d, p):
        @pl.when(g != p)
        def _():
            remote(csend.at[d, p], crecv.at[d, g], sem_b[d], {"frames": at_g(p)}).start()

    group_states(1)
    group_states(0)

    fetched["c"].wait()
    fetched["gain"].wait()
    fetched["x"].wait()
    gram = dot_nt(crx[i], brx[i])
    parts_f = thirds(ldrx[i, 0])
    parts_b = thirds(ldrx[i, 1])
    row_b = sum_rows(parts_b, (r_id < s_id).astype(F32))
    gram = jnp.where(r_id == s_id, 2.0 * gram, gram)
    lower = s_id <= r_id
    row_f = sum_rows(parts_f, (r_id <= s_id).astype(F32))
    col_f = sum_cols(lower.astype(F32), parts_f)
    col_b = sum_cols((s_id < r_id).astype(F32), parts_b)
    left = s_id < HD
    for p in range(PAIRS):
        x_pair = xv[:, p * 2 * HD : (p + 1) * 2 * HD].astype(F32)
        weights = []
        for h in (2 * p, 2 * p + 1):
            at_f = jnp.broadcast_to(col_f[:, h : h + 1], (F, F))
            at_b = jnp.broadcast_to(col_b[:, h : h + 1], (F, F))
            exponent = jnp.where(lower, at_f - row_f[h : h + 1], row_b[h : h + 1] - at_b)
            weights.append((jnp.exp(exponent) * gram).astype(BF))
        apart = jnp.concatenate(
            [jnp.where(left, x_pair, 0.0), jnp.where(left, 0.0, x_pair)], axis=0
        ).astype(BF)
        intra = dot(jnp.concatenate(weights, axis=1), apart)
        inside = intra + jnp.where(left[0:1], gain[2 * p], gain[2 * p + 1]) * x_pair
        pre[p] = inside
        prebf[p] = inside.astype(BF)
    near_rows = prebf.at[:, pl.ds(pl.multiple_of((1 - i) * RIM, RIM), RIM)]
    far_rows = prebf.at[:, pl.ds(pl.multiple_of(i * RIM, RIM), RIM)]
    row_states(1)
    row_states(0)
    start(remote(near_rows, rim_near, sem_rim, {"frames": partner}))
    for t in range(tok_count):
        start(remote(far_rows, rim_far.at[tok], sem_far + t, {"frames": cross, "tok": t}, sem_far + tok))

    arrive(NI, crx, sem_c)
    picked_f = jnp.concatenate([r[0:HP] for r in rows], axis=0)
    picked_b = jnp.concatenate([r[HP : 2 * HP] for r in rows], axis=0)
    cols = (
        sum_cols(lower.astype(F32), thirds(picked_f)),
        sum_cols((s_id >= r_id).astype(F32), thirds(picked_b)),
    )

    def group_terms(d):
        total = jnp.zeros((2 * HP, N), F32)
        for j in range(NI) if d == 0 else reversed(range(NI)):
            for e in range(LP):
                at = [
                    jnp.broadcast_to(cols[d][:, HP * j + 2 * e + h : HP * j + 2 * e + h + 1], (F, F))
                    for h in range(2)
                ]
                spread = jnp.exp(jnp.where(left, at[0], at[1]))
                h = d * HP + 2 * e
                lead = jnp.exp(jnp.where(left[0:1], total[h : h + 1], total[h + 1 : h + 2]))
                grown[d, j, e] = spread * lead
                part = spread * dot_nt(crx[j], within[d, j, e * N : (e + 1) * N])
                local_part[j, e] = part if d == 0 else local_part[j, e] + part
            total = total + tots[j]

    entering(1)
    entering(0)
    for p in late:
        for d in (1, 0):
            send_back(d, p)
    for d in range(2):
        ours = all_of(crecv.at[d], ng)
        sent.append(remote(ours, ours, sem_b[d], {"frames": prev}))

    group_terms(0)
    group_terms(1)

    fetched["start"].wait()
    fetched["len"].wait()
    groups = starts.shape[0]
    tokens, window = bias.shape
    per_group = tokens // groups
    place = lax.broadcasted_iota(jnp.int32, (per_group, window), 1) + (me * F - RIM)
    for k in range(groups):
        allowed = (place >= starts[k]) & (place < starts[k] + lens[k])
        bias[k * per_group : (k + 1) * per_group, :] = jnp.where(allowed, 0.0, -jnp.inf)
    rwin[:, 0:RIM] = jnp.zeros((LP, RIM, N), BF)
    rwin[:, RIM + NI * F :] = jnp.zeros((LP, RIM, N), BF)

    opening = base == 0

    def carry_terms(d):
        arrive(ng, crecv.at[d], sem_b[d])
        carried = crecv[d].reshape(PIECE, N)
        for j in range(NI):
            for e in range(LP):
                part = local_part[j, e] + grown[d, j, e] * dot_nt(crx[j], carried[e * N : (e + 1) * N])
                if d == 1:
                    local_part[j, e] = part
                rwin[e, RIM + j * F : RIM + (j + 1) * F] = part.astype(BF)

    carry_terms(1)

    @pl.when(jnp.logical_not(opening))
    def _():
        carry_terms(0)

    def pairs_of(q):
        return pl.ds(q * LP, LP)

    def window_of(p, q):
        src = rwin.at[:, pl.ds(pl.multiple_of((p + 1) * RIM, RIM), 3 * RIM)]
        return src, rin.at[pairs_of(q), pl.ds(pl.multiple_of((1 - p) * RIM, RIM), 3 * RIM)]

    windows = []
    for k in range(1, NI):
        p = lax.rem(i + k, NI)
        windows.append(remote(*window_of(p, i), sem_r + k - 1, {"frames": at_i(p)}))
    for copy in windows:
        start(copy)
    rim_there = rx.at[tok, pairs_of(i)]
    for t in range(tok_count):
        for k, (first, there) in enumerate(((NI * F, base_succ), (RIM, base_prev + NI - 1))):
            start(
                remote(
                    rwin.at[:, first : first + RIM],
                    rim_there,
                    sem_rx + 2 * t + k,
                    {"frames": there, "tok": t},
                    sem_rx + NI * tok + i,
                )
            )
    rin[pairs_of(i)] = rwin[:, pl.ds(pl.multiple_of(i * F, F), 2 * F)]
    remote(near_rows, rim_near, sem_rim, {"frames": partner}).wait_recv()
    span = pl.ds(pl.multiple_of((1 - i) * RIM, RIM), 3 * RIM)
    near = pl.ds(pl.multiple_of((1 - i) * 3 * RIM, RIM), RIM)
    far = pl.ds(pl.multiple_of(i * 3 * RIM, RIM), RIM)

    def far_in():
        for t in range(tok_count):
            for q in range(NI):
                remote(
                    rwin.at[:, 0:RIM], rx.at[t, pairs_of(q)], sem_rx, {"frames": prev}, sem_rx + NI * t + q
                ).wait_recv()

    for k in range(NI):
        q = lax.rem(i + NI - k, NI)
        if k > 0:
            remote(*window_of(i, q), sem_r + k - 1, {"frames": at_i(q)}).wait_recv()
        for e in range(LP):
            m = q * LP + e
            wide[tok, m, near] = (rim_near[m].astype(F32) + rin[m, near].astype(F32)).astype(BF)
            wide[tok, m, RIM : RIM + F] = (pre[m] + rin[m, RIM : RIM + F].astype(F32)).astype(BF)
        if tok_count > 1:
            piece = wide.at[tok, pairs_of(q), span]
            start(remote(piece, piece, sem_w + k, {"tok": 1 - tok}))
    for t in range(tok_count):
        remote(far_rows, rim_far.at[t], sem_far, {"frames": cross}, sem_far + t).wait_recv()
    ends_here = (me == 0) | (me == frames - 1)

    @pl.when(ends_here)
    def _():
        for t in range(tok_count):
            for m in range(PAIRS):
                wide[t, m, far] = jnp.zeros((RIM, N), BF)

    @pl.when(jnp.logical_not(ends_here))
    def _():
        far_in()
        for t in range(tok_count):
            for m in range(PAIRS):
                wide[t, m, far] = (rim_far[t, m].astype(F32) + rx[t, m].astype(F32)).astype(BF)

    fetched["q"].wait()
    fetched["wk"].wait()
    fetched["wv"].wait()

    def half_rows(t):
        return jnp.concatenate([wide[t, p] for p in range(PAIRS)], axis=1)

    mine = half_rows(tok)
    at = pl.ds(pl.multiple_of(tok * half, half), half)
    kacc[...] = dot(mine, wk[at, :])
    vacc[...] = dot(mine, wv[at, :])
    for copy in sent:
        copy.wait_send()
    if tok_count > 1:
        other = 1 - tok
        for k in range(NI):
            q = lax.rem(i + NI - k, NI)
            piece = wide.at[other, pairs_of(q), span]
            remote(piece, piece, sem_w + k, {"tok": other}).wait_recv()
        theirs = half_rows(other)
        at = pl.ds(pl.multiple_of(other * half, half), half)
        keys[...] = (kacc[...] + dot(theirs, wk[at, :])).astype(BF)
        values[...] = (vacc[...] + dot(theirs, wv[at, :])).astype(BF)
    else:
        keys[...] = kacc[...].astype(BF)
        values[...] = vacc[...].astype(BF)

    @pl.when(ends_here)
    def _():
        far_in()

    @pl.when(opening)
    def _():
        arrive(ng, crecv.at[0], sem_b[0])


def reader(wide, keys, values, queries, bias, enc_hbm, out_hbm, enc, out, sem):
    tok = lax.axis_index("tok")
    for p in range(PAIRS):
        enc[:, p * 2 * HD : (p + 1) * 2 * HD] = wide[tok, p, RIM : RIM + F]
    copies = [pltpu.make_async_copy(enc, enc_hbm, sem.at[0])]
    copies[0].start()
    left = lax.broadcasted_iota(jnp.int32, (1, 2 * DHD), 1) < DHD
    for p in range(queries.shape[1] // (2 * DHD)):
        cols = slice(p * 2 * DHD, (p + 1) * 2 * DHD)
        q_pair = queries[:, cols]
        k_pair = keys[:, cols].astype(F32)
        v_pair = values[:, cols]
        both = []
        for only in (jnp.where(left, k_pair, 0.0), jnp.where(left, 0.0, k_pair)):
            scores = dot_nt(q_pair, only.astype(BF)) + bias[...]
            top = jnp.max(scores, axis=1, keepdims=True)
            raised = jnp.exp2((scores - top) * (DHD ** (-0.5) * LOG2E))
            whole = 1.0 / jnp.sum(raised, axis=1, keepdims=True)
            both.append(dot(raised.astype(BF), v_pair) * whole)
        out[:, cols] = jnp.where(left, both[0], both[1]).astype(BF)
        copies.append(pltpu.make_async_copy(out.at[:, cols], out_hbm.at[:, cols], sem.at[p + 1]))
        copies[-1].start()
    for copy in copies:
        copy.wait()


def solution(mesh):
    frames = mesh.shape["frames"]
    tok_count = mesh.shape["tok"]
    ng = min(16 // NI, frames // NI)
    ny = frames // (NI * ng)
    sub = PIECE // ng
    vmem = pl.BlockSpec(memory_space=pltpu.VMEM)
    hbm = pl.BlockSpec(memory_space=pltpu.HBM)

    def local(x, b, c, log_decay, gain, key_weight, value_weight, queries, span_start, span_len):
        count, width = x.shape
        window = 2 * count
        tokens, out_width = queries.shape
        copies = 14 + 2 * NI + (2 * NI + 1) * tok_count
        wide, keys, values, held, bias = pl.pallas_call(
            functools.partial(mixer, (ny, ng, tok_count)),
            out_shape=(
                jax.ShapeDtypeStruct((tok_count, PAIRS, window, N), BF),
                jax.ShapeDtypeStruct((window, out_width), BF),
                jax.ShapeDtypeStruct((window, out_width), BF),
                jax.ShapeDtypeStruct(queries.shape, BF),
                jax.ShapeDtypeStruct((tokens, window), F32),
            ),
            in_specs=[hbm] * 10,
            out_specs=(vmem,) * 5,
            scratch_shapes=[
                pltpu.VMEM(x.shape, BF),
                pltpu.SMEM(gain.shape, F32),
                pltpu.SMEM(span_start.shape, jnp.int32),
                pltpu.SMEM(span_len.shape, jnp.int32),
                pltpu.VMEM(key_weight.shape, BF),
                pltpu.VMEM(value_weight.shape, BF),
                pltpu.VMEM((NI, count, PIECE), BF),
                pltpu.VMEM((NI,) + b.shape, BF),
                pltpu.VMEM((NI,) + c.shape, BF),
                pltpu.VMEM((NI,) + log_decay.shape, F32),
                pltpu.VMEM((2, NI, PIECE, N), F32),
                pltpu.VMEM((2, ng, sub, N), BF),
                pltpu.VMEM((2, ng, sub, N), BF),
                pltpu.VMEM((8, N), F32),
                pltpu.VMEM((ng, 8, N), F32),
                pltpu.VMEM((2, sub, N), BF),
                pltpu.VMEM((2, ny, sub, N), BF),
                pltpu.VMEM((8, N), F32),
                pltpu.VMEM((ny, 8, N), F32),
                pltpu.VMEM((2, ng, sub, N), BF),
                pltpu.VMEM((2, ng, sub, N), BF),
                pltpu.VMEM((PAIRS, count, N), F32),
                pltpu.VMEM((PAIRS, count, N), BF),
                pltpu.VMEM((PAIRS, RIM, N), BF),
                pltpu.VMEM((tok_count, PAIRS, RIM, N), BF),
                pltpu.VMEM((2, NI, PIECE, N), BF),
                pltpu.VMEM((2, NI, LP, count, N), F32),
                pltpu.VMEM((NI, LP, count, N), F32),
                pltpu.VMEM((LP, 2 * RIM + NI * count, N), BF),
                pltpu.VMEM((PAIRS, window, N), BF),
                pltpu.VMEM((tok_count, PAIRS, RIM, N), BF),
                pltpu.VMEM((window, out_width), F32),
                pltpu.VMEM((window, out_width), F32),
                pltpu.SemaphoreType.DMA((11,)),
                pltpu.SemaphoreType.DMA((copies,)),
                pltpu.SemaphoreType.DMA((copies,)),
            ],
            compiler_params=pltpu.CompilerParams(
                collective_id=0, has_side_effects=True, vmem_limit_bytes=24 * 2**20
            ),
        )(
            *(
                pltpu.with_memory_space_constraint(a, pltpu.HBM)
                for a in (
                    x,
                    b,
                    c,
                    log_decay,
                    gain,
                    key_weight,
                    value_weight,
                    queries,
                    span_start,
                    span_len,
                )
            )
        )
        return pl.pallas_call(
            reader,
            out_shape=(
                jax.ShapeDtypeStruct((count, width), BF),
                jax.ShapeDtypeStruct(queries.shape, BF),
            ),
            in_specs=[vmem] * 5,
            out_specs=(hbm, hbm),
            scratch_shapes=[
                pltpu.VMEM((count, width), BF),
                pltpu.VMEM(queries.shape, BF),
                pltpu.SemaphoreType.DMA((out_width // (2 * DHD) + 1,)),
            ],
            compiler_params=pltpu.CompilerParams(vmem_limit_bytes=24 * 2**20),
        )(wide, keys, values, held, bias)

    placed = (
        P(("dp", "frames"), "tok"),
        P(("dp", "frames"), None),
        P(("dp", "frames"), None),
        P(None, "tok", ("dp", "frames")),
        P("tok"),
        P(None, "tok"),
        P(None, "tok"),
        P(("dp", "frames"), "tok"),
        P(("dp", "frames")),
        P(("dp", "frames")),
    )
    return jax.shard_map(
        local,
        mesh=mesh,
        in_specs=placed,
        out_specs=(P(("dp", "frames"), "tok"), P(("dp", "frames"), "tok")),
        check_vma=False,
    )
```
